32 devices in a mesh: tensor: 2 (over y), context: 16 (over z, x, core).
Axes of the slice: x: 2, y: 2, z: 4, core: 2. Of those that a mesh axis runs over, the one named last changes fastest.
Arguments:
- inputs: bfloat16 [2, 1024, 2560], P(None, 'context'), may hold values from -6 to 6
- valid: int32 [2, 1024], P(None, 'context'), may hold values from 0 to 1, as said below
- out_grad: bfloat16 [2, 1024, 2560], P(None, 'context'), may hold values from -6 to 6
- teacher: bfloat16 [2, 1024, 2560], P(None, 'context'), may hold values from -6 to 6
- norm_attn: bfloat16 [2560], P('context'), may hold values from 0.5 to 1.5
- w_query: bfloat16 [2560, 2560], P('context', 'tensor'), may hold values from -0.125 to 0.125
- key_matrix: bfloat16 [2560, 640], P('context', 'tensor'), may hold values from -0.125 to 0.125
- value_matrix: bfloat16 [2560, 640], P('context', 'tensor'), may hold values from -0.125 to 0.125
- w_out: bfloat16 [2560, 2560], P('tensor', 'context'), may hold values from -2 to 2
- norm_mlp: bfloat16 [2560], P('context'), may hold values from 0.5 to 1.5
- w_gate: bfloat16 [2560, 6912], P('context', 'tensor'), may hold values from -0.125 to 0.125
- w_up: bfloat16 [2560, 6912], P('context', 'tensor'), may hold values from -0.125 to 0.125
- w_down: bfloat16 [6912, 2560], P('tensor', 'context'), may hold values from -0.078125 to 0.078125
Outputs:
- output: bfloat16 [2, 1024, 2560], P(None, 'context')
- loss: float32 [], replicated
- input_grad: float32 [2, 1024, 2560], P(None, 'context')
- grad_norm_attn: float32 [2560], P('context')
- grad_norm_mlp: float32 [2560], P('context')
- grad_query: float32 [2560, 2560], P('context', 'tensor')
- grad_key: float32 [2560, 640], P('context', 'tensor')
- grad_value: float32 [2560, 640], P('context', 'tensor')
- grad_out: float32 [2560, 2560], P('tensor', 'context')
- grad_gate: float32 [2560, 6912], P('context', 'tensor')
- grad_up: float32 [2560, 6912], P('context', 'tensor')
- grad_down: float32 [6912, 2560], P('tensor', 'context')
The draws below stay inside these ranges and needn't reach their ends.
Inputs may be any that keep to these rules, and one draw needn't show every extreme that they name: `valid`: each row is a run of ones followed by zeros, with 256 ones or more; some row is all ones.
All inputs are finite; a program needn't handle non-finite values.
Results may differ from the reference program's by a relative error of at most 0.012.
The reference program's roundings to bfloat16 on the way count: a program that leaves them out, or rounds other values in their place, can miss the bound.
Values may be sent and summed in bfloat16 or wider, within the bound.
No kernel may reach another device: no remote copies, remote signals or barrier semaphores. Data moves between devices by JAX's collectives and lax.ppermute only.
A program may use at most 256 MiB of HBM per device.

```python
import math
import jax
import jax.numpy as jnp
from jax import lax

MODEL_WIDTH = 2560
QUERY_HEADS = 32
KEY_VALUE_HEADS = 8
HEAD_SIZE = 80
FF = 6912
SEQS = 2
BLOCK = 256
SEQUENCE_LENGTH = 1024


def draw_valid(key, part):
    key = jax.random.fold_in(key, 11)
    first, second = jax.random.split(key)
    lengths = jax.random.randint(first, (SEQS,), SEQUENCE_LENGTH // 4, SEQUENCE_LENGTH + 1)
    chosen = jax.random.randint(second, (), 0, SEQS)
    lengths = jnp.where(jnp.arange(SEQS) == chosen, SEQUENCE_LENGTH, lengths)
    return (jnp.arange(SEQUENCE_LENGTH)[None, :] < lengths[:, None]).astype(jnp.int32)


def shard_levels(stream_key, extent, cuts, low, high):
    loudness = 1.0
    for axis_at, shards_of in cuts:
        draws = jax.random.uniform(jax.random.fold_in(jax.random.fold_in(stream_key, 6), axis_at), (shards_of,), jnp.float32, low / len(cuts), high / len(cuts))
        loudness = loudness * jnp.repeat(jnp.exp(draws), extent[axis_at] // shards_of).reshape((-1,) + (1,) * (len(extent) - 1 - axis_at))
    return loudness


def scatter_about(own_key, dims, deviation, most, cuts=(), held_as=jnp.bfloat16):
    entries = deviation * jax.random.normal(own_key, dims, jnp.float32)
    if cuts:
        entries = entries * shard_levels(own_key, dims, cuts, -0.22, 0.18)
    return jnp.clip(entries, -most, most).astype(held_as)


def setup_inputs(seed: int = 0) -> dict:
    seeds = jax.random.split(jax.random.key(seed), 14)
    inputs = scatter_about(seeds[0], (SEQS, SEQUENCE_LENGTH, MODEL_WIDTH), 1.0, 6.0, ((1, 16),))
    valid = draw_valid(jax.random.fold_in(seeds[13], 71), 0)
    out_grad = scatter_about(seeds[2], (SEQS, SEQUENCE_LENGTH, MODEL_WIDTH), 1.0, 6.0, ((1, 16),))
    teacher = scatter_about(seeds[3], (SEQS, SEQUENCE_LENGTH, MODEL_WIDTH), 1.0, 6.0, ((1, 16),))
    norm_attn = jnp.clip(1.0 + 0.1 * jax.random.normal(seeds[4], (MODEL_WIDTH,), jnp.float32), 0.5, 1.5).astype(jnp.bfloat16)
    w_query = scatter_about(seeds[5], (MODEL_WIDTH, QUERY_HEADS * HEAD_SIZE), MODEL_WIDTH ** -0.5, 0.125, ((0, 16), (1, 2)))
    key_matrix = scatter_about(seeds[6], (MODEL_WIDTH, KEY_VALUE_HEADS * HEAD_SIZE), MODEL_WIDTH ** -0.5, 0.125, ((0, 16), (1, 2)))
    value_matrix = scatter_about(seeds[7], (MODEL_WIDTH, KEY_VALUE_HEADS * HEAD_SIZE), MODEL_WIDTH ** -0.5, 0.125, ((0, 16), (1, 2)))
    w_out = scatter_about(seeds[8], (QUERY_HEADS * HEAD_SIZE, MODEL_WIDTH), (max(1, QUERY_HEADS * HEAD_SIZE * 4 // SEQUENCE_LENGTH)) ** -0.5, 2.0, ((0, 2), (1, 16)))
    norm_mlp = jnp.clip(1.0 + 0.1 * jax.random.normal(seeds[9], (MODEL_WIDTH,), jnp.float32), 0.5, 1.5).astype(jnp.bfloat16)
    w_gate = scatter_about(seeds[10], (MODEL_WIDTH, FF), MODEL_WIDTH ** -0.5, 0.125, ((0, 16), (1, 2)))
    w_up = scatter_about(seeds[11], (MODEL_WIDTH, FF), MODEL_WIDTH ** -0.5, 0.125, ((0, 16), (1, 2)))
    w_down = scatter_about(seeds[12], (FF, MODEL_WIDTH), FF ** -0.5, 0.078125, ((0, 2), (1, 16)))
    return dict(inputs=inputs, valid=valid, out_grad=out_grad, teacher=teacher, norm_attn=norm_attn, w_query=w_query, key_matrix=key_matrix, value_matrix=value_matrix, w_out=w_out, norm_mlp=norm_mlp, w_gate=w_gate, w_up=w_up, w_down=w_down)


eps = 1e-05
theta = 10000.0
highest = lax.Precision.HIGHEST

@jax.custom_vjp
def lower_bound(v):
    return lax.optimization_barrier(v.astype(jnp.bfloat16)).astype(jnp.float32)

@jax.custom_vjp
def low_back(v):
    return v

def low_keep(v):
    return (lower_bound(v), None)

def low_pass(kept, grad):
    return (grad,)

def back_keep(v):
    return (v, None)

def back_low(kept, grad):
    return (lower_bound(grad),)
lower_bound.defvjp(low_keep, low_pass)
low_back.defvjp(back_keep, back_low)

def rms_norm(value_rows, gain):
    inverse = lax.rsqrt(lax.optimization_barrier(jnp.mean(value_rows * value_rows, axis=-1, keepdims=True)) + eps)
    return value_rows * inverse * gain

def rotary_embed(value_rows):
    half = HEAD_SIZE // 2
    freqs = jnp.exp(-math.log(theta) * jnp.arange(half, dtype=jnp.float32) / half)
    angles = jnp.arange(SEQUENCE_LENGTH, dtype=jnp.float32)[:, None] * freqs[None, :]
    cosine = jnp.cos(angles)[:, None, :]
    sine = jnp.sin(angles)[:, None, :]
    first, second = (value_rows[..., :half], value_rows[..., half:])
    return jnp.concatenate([first * cosine - second * sine, second * cosine + first * sine], axis=-1)

def one_sequence(xseq, vseq, gain1, wq, wk, wv, wo, gain2, wg, wu, wd):
    head_group = QUERY_HEADS // KEY_VALUE_HEADS
    scale = HEAD_SIZE ** (-0.5)
    h1 = lower_bound(rms_norm(xseq, gain1))
    query_before_rotary = low_back(jnp.dot(h1, wq, precision=highest))
    key_before_rotary = low_back(jnp.dot(h1, wk, precision=highest))
    value_before_rotary = low_back(jnp.dot(h1, wv, precision=highest))
    query_rows = lower_bound(rotary_embed(query_before_rotary.reshape(SEQUENCE_LENGTH, QUERY_HEADS, HEAD_SIZE))).reshape(SEQUENCE_LENGTH, KEY_VALUE_HEADS, head_group, HEAD_SIZE)
    key_rows = lower_bound(rotary_embed(key_before_rotary.reshape(SEQUENCE_LENGTH, KEY_VALUE_HEADS, HEAD_SIZE)))
    value_rows = lower_bound(value_before_rotary).reshape(SEQUENCE_LENGTH, KEY_VALUE_HEADS, HEAD_SIZE)
    row_count = math.gcd(SEQUENCE_LENGTH, 512)
    kpos = jnp.arange(SEQUENCE_LENGTH, dtype=jnp.int32)
    key_ok = vseq > 0

    def block(args):
        qblock, start = args
        qpos = start + jnp.arange(row_count, dtype=jnp.int32)
        raw = jnp.einsum('qkgd,jkd->kgqj', qblock, key_rows, precision=highest) * scale
        raw = low_back(raw)
        allowed = (kpos[None, :] // BLOCK <= qpos[:, None] // BLOCK) & key_ok[None, :]
        masked = jnp.where(allowed, raw, jnp.float32(-1e+30))
        prob = jax.nn.softmax(masked, axis=-1)
        probr = lower_bound(prob)
        ctx = jnp.einsum('kgqj,jkd->qkgd', probr, value_rows, precision=highest)
        return lower_bound(low_back(ctx)).reshape(row_count, QUERY_HEADS * HEAD_SIZE)
    block_list = query_rows.reshape(SEQUENCE_LENGTH // row_count, row_count, KEY_VALUE_HEADS, head_group, HEAD_SIZE)
    starts = (jnp.arange(SEQUENCE_LENGTH // row_count) * row_count).astype(jnp.int32)
    ctx = lax.map(jax.checkpoint(block), (block_list, starts)).reshape(SEQUENCE_LENGTH, QUERY_HEADS * HEAD_SIZE)
    attn = low_back(jnp.dot(ctx, wo, precision=highest))
    resid = xseq + attn
    h2 = lower_bound(rms_norm(resid, gain2))
    gate = low_back(jnp.dot(h2, wg, precision=highest))
    up = low_back(jnp.dot(h2, wu, precision=highest))
    act = lower_bound(jax.nn.silu(gate) * up)
    mixed = low_back(jnp.dot(act, wd, precision=highest))
    return resid + mixed

def forward(valid, x, gain1, wq, wk, wv, wo, gain2, wg, wu, wd):

    def step(carry, pair):
        xseq, vseq = pair
        return (carry, one_sequence(xseq, vseq, gain1, wq, wk, wv, wo, gain2, wg, wu, wd))
    carry, out = lax.scan(step, jnp.float32(0.0), (x, valid))
    return out

def reference(inputs, valid, out_grad, teacher, norm_attn, w_query, key_matrix, value_matrix, w_out, norm_mlp, w_gate, w_up, w_down):
    floats = [a.astype(jnp.float32) for a in (inputs, norm_attn, w_query, key_matrix, value_matrix, w_out, norm_mlp, w_gate, w_up, w_down)]
    out, pull = jax.vjp(partial_forward(valid), *floats)
    validf = valid.astype(jnp.float32)[..., None]
    diff = out - teacher.astype(jnp.float32)
    count = jnp.sum(valid.astype(jnp.float32))
    squares = jnp.sum(validf * diff * diff)
    loss = squares / (count * MODEL_WIDTH)
    dout = validf * (out_grad.astype(jnp.float32) + jnp.float32(SEQS * SEQUENCE_LENGTH) / count * diff)
    grads = pull(dout)
    return (out.astype(jnp.bfloat16), loss, grads[0], grads[1], grads[6], grads[2], grads[3], grads[4], grads[5], grads[7], grads[8], grads[9])

def partial_forward(valid):

    def inner(x, gain1, wq, wk, wv, wo, gain2, wg, wu, wd):
        return forward(valid, x, gain1, wq, wk, wv, wo, gain2, wg, wu, wd)
    return inner
```

```python
import functools
import math

import jax
import jax.numpy as jnp
from jax import lax
from jax.experimental import pallas as pl
from jax.experimental.pallas import tpu as pltpu
from jax.sharding import PartitionSpec as P

HEAD_SIZE = 80
BLOCK = 256
LANES = 128
VMEM_BYTES = 56 * 1024 * 1024

eps = 1e-05
theta = 10000.0
BF = jnp.bfloat16
F32 = jnp.float32


def whole(shape, dtype):
    return jax.ShapeDtypeStruct(shape, dtype)


def vmem():
    return pl.BlockSpec(memory_space=pltpu.VMEM)


def smem():
    return pl.BlockSpec(memory_space=pltpu.SMEM)


def kernel_call(body, outs, ins_smem, ins, flops=0, nbytes=0, scratch=()):
    single = not isinstance(outs, (list, tuple))
    return pl.pallas_call(
        body,
        out_shape=outs,
        in_specs=[smem()] * ins_smem + [vmem()] * (len(ins) - ins_smem),
        out_specs=vmem() if single else [vmem()] * len(outs),
        scratch_shapes=list(scratch),
        compiler_params=pltpu.CompilerParams(vmem_limit_bytes=VMEM_BYTES),
        cost_estimate=pl.CostEstimate(flops=flops, bytes_accessed=nbytes, transcendentals=0),
    )(*ins)


def dot_nn(a, b):
    return lax.dot_general(a, b, (((1,), (0,)), ((), ())), preferred_element_type=F32)


def dot_nt(a, b):
    return lax.dot_general(a, b, (((1,), (1,)), ((), ())), preferred_element_type=F32)


def dot_tn(a, b):
    return lax.dot_general(a, b, (((0,), (0,)), ((), ())), preferred_element_type=F32)


def move_c(a):
    return lax.ppermute(a, "context", [(k, k ^ 1) for k in range(16)])


def move_x(a):
    return lax.ppermute(a, "context", [(k, k ^ 2) for k in range(16)])


def move_z(a, step):
    return lax.ppermute(a, "context", [(k, (k + 4 * step) % 16) for k in range(16)])


def move_zx(a, bit):
    return lax.ppermute(a, "context", [(k, k ^ (4 * bit)) for k in range(16)])


def move_y(a):
    return lax.ppermute(a, "tensor", [(0, 1), (1, 0)])


def sum_context(a):
    a = a + move_c(a)
    a = a + move_x(a)
    a = a + move_zx(a, 1)
    return a + move_zx(a, 2)


def gather_rows(own):
    near = [own, move_z(own, 1), move_z(own, 2), move_z(own, 3)]
    far = [move_x(p) for p in near]
    near_c = move_c(jnp.stack(near))
    far_c = move_c(jnp.stack(far))
    pieces = []
    for m in range(4):
        pieces += [near[m], near_c[m], far[m], far_c[m]]
    return jnp.concatenate(pieces, axis=0)


def scatter_rows(part):
    n = part.shape[0] // 16
    p = part.reshape(4, 2, 2, n, part.shape[1])
    q = p[:, :, 0] + move_c(p[:, :, 1].astype(BF)).astype(F32)
    s = [None] * 4
    for m in (2, 1, 3, 0):
        s[m] = q[m, 0] + move_x(q[m, 1].astype(BF)).astype(F32)
    total = s[0]
    for m in (2, 1, 3):
        total = total + move_z(s[m].astype(BF), 4 - m).astype(F32)
    return total


def pack_weights(place, wq, wk, wv, wot, wg, wu, wdt):
    rows = wq.shape[0]
    cq, ck, cf = wq.shape[1] // 8, wk.shape[1] // 4, wg.shape[1] // 8

    def body(place_ref, wq_ref, wk_ref, wv_ref, wo_ref, wg_ref, wu_ref, wd_ref, a_ref, g_ref, d_ref):
        z, x = place_ref[0], place_ref[1]
        for zd in range(4):
            for xd in range(2):
                j = zd * 2 + xd
                mz, mx = lax.rem(zd - z + 4, 4), lax.rem(xd + x, 2)
                a_ref[mz, mx] = jnp.concatenate(
                    [
                        wq_ref[:, j * cq : (j + 1) * cq],
                        wk_ref[:, zd * ck : (zd + 1) * ck],
                        wv_ref[:, zd * ck : (zd + 1) * ck],
                        wo_ref[:, j * cq : (j + 1) * cq],
                    ],
                    axis=1,
                )
                g_ref[mz, mx] = jnp.concatenate(
                    [wg_ref[:, j * cf : (j + 1) * cf], wu_ref[:, j * cf : (j + 1) * cf]], axis=1
                )
                d_ref[mz, mx] = wd_ref[:, j * cf : (j + 1) * cf]

    outs = [whole((4, 2, rows, w), BF) for w in (2 * cq + 2 * ck, 2 * cf, cf)]
    return kernel_call(body, outs, 1, (place, wq, wk, wv, wot, wg, wu, wdt))


def spread(place, blocks):
    y, c = place[3], place[2]
    rows, cols = blocks.shape[2:]
    got = [blocks[0]] + [move_z(blocks[m], m) for m in (1, 2, 3)]
    far = move_x(jnp.stack([g[1] for g in got]))
    own = jnp.concatenate([jnp.stack([g[0] for g in got]), far])
    other = move_y(own)
    mine = y == c
    come = move_c(jnp.where(mine, other, own))

    def body(place_ref, own_ref, other_ref, come_ref, out_ref):
        z, x, c, y = place_ref[0], place_ref[1], place_ref[2], place_ref[3]

        def put(keep_ref):
            for zs in range(4):
                for xs in range(2):
                    at = lax.rem(xs + x, 2) * 4 + lax.rem(z - zs + 4, 4)
                    out_ref[zs, xs, c] = keep_ref[at]
                    out_ref[zs, xs, 1 - c] = come_ref[at]

        @pl.when(y == c)
        def _():
            put(own_ref)

        @pl.when(y != c)
        def _():
            put(other_ref)

    out = kernel_call(body, whole((4, 2, 2, rows, cols), BF), 1, (place, own, other, come))
    return out.reshape(16 * rows, cols)


def collect(place, part):
    z, x, c, y = place[0], place[1], place[2], place[3]
    rows, cols = part.shape[0] // 16, part.shape[1]
    p = part.reshape(8, 2, rows, cols)
    keep = lax.dynamic_index_in_dim(p, c, 1, keepdims=False)
    come = move_c(lax.dynamic_index_in_dim(p, 1 - c, 1, keepdims=False).astype(BF))
    mine = y == c
    give = move_y(jnp.where(mine, come, keep.astype(BF)))
    total = (jnp.where(mine, keep, come.astype(F32)) + give.astype(F32)).astype(BF)
    total = total.reshape(4, 2, rows, cols)
    to_near = [lax.dynamic_slice(total, (lax.rem(z + m, 4), x, 0, 0), (1, 1, rows, cols))[0] for m in range(4)]
    to_far = [lax.dynamic_slice(total, (lax.rem(z + m, 4), 1 - x, 0, 0), (1, 1, rows, cols))[0] for m in range(4)]
    far = move_x(jnp.stack(to_far))
    pairs = [jnp.concatenate([to_near[m], far[m]]) for m in range(4)]
    return jnp.stack([pairs[0]] + [move_z(pairs[m], m) for m in (1, 2, 3)])


def unpack(place, got, widths, shared):
    rows = got.shape[2]

    def body(place_ref, got_ref, *outs):
        z, x = place_ref[0], place_ref[1]
        for zs in range(4):
            blocks = [
                got_ref[lax.rem(z - zs + 4, 4), lax.rem(xs + x, 2)].astype(F32) for xs in range(2)
            ]
            at = 0
            for out, width, both in zip(outs, widths, shared):
                a, b = blocks[0][:, at : at + width], blocks[1][:, at : at + width]
                if both:
                    out[:, zs * width : (zs + 1) * width] = a + b
                else:
                    out[:, 2 * zs * width : (2 * zs + 1) * width] = a
                    out[:, (2 * zs + 1) * width : (2 * zs + 2) * width] = b
                at += width

    outs = [whole((rows, (4 if both else 8) * width), F32) for width, both in zip(widths, shared)]
    return kernel_call(body, outs, 1, (place, got))


def turn(a, cosine, sine):
    half = HEAD_SIZE // 2
    lane = lax.broadcasted_iota(jnp.int32, a.shape, 1)
    swapped = jnp.where(lane < half, pltpu.roll(a, LANES - half, 1), pltpu.roll(a, half, 1))
    return a * cosine + swapped * sine


def attention(place, lens, qkv, cosine, sine):
    rows = qkv.shape[0]
    blocks = rows // BLOCK
    scale = HEAD_SIZE ** (-0.5)

    def body(place_ref, len_ref, qkv_ref, cos_ref, sin_ref, q_ref, k_ref, v_ref, ctx_ref, lse_ref):
        z = place_ref[0]
        length = len_ref[0]
        for m in range(blocks):
            to = pl.multiple_of(lax.rem(z - m + blocks, blocks) * BLOCK, BLOCK)
            rs = slice(m * BLOCK, (m + 1) * BLOCK)
            cosine, sine = cos_ref[pl.ds(to, BLOCK), :], sin_ref[pl.ds(to, BLOCK), :]
            for h in range(2):
                q_ref[h, pl.ds(to, BLOCK), :] = turn(
                    qkv_ref[rs, h * LANES : (h + 1) * LANES], cosine, sine
                ).astype(BF)
            k_ref[pl.ds(to, BLOCK), :] = turn(
                qkv_ref[rs, 2 * LANES : 3 * LANES], cosine, sine
            ).astype(BF)
            v_ref[pl.ds(to, BLOCK), :] = qkv_ref[rs, 3 * LANES : 4 * LANES].astype(BF)
        return z, length

    def kernel(place_ref, len_ref, kpos_ref, qkv_ref, cos_ref, sin_ref, q_ref, k_ref, v_ref, ctx_ref, lse_ref):
        z, length = body(place_ref, len_ref, qkv_ref, cos_ref, sin_ref, q_ref, k_ref, v_ref, ctx_ref, lse_ref)
        for i in range(blocks):
            back = pl.multiple_of(lax.rem(z - i + blocks, blocks) * BLOCK, BLOCK)
            n = (i + 1) * BLOCK
            ok = kpos_ref[:, :n] < length
            for h in range(2):
                s = dot_nt(q_ref[h, i * BLOCK : n, :], k_ref[:n, :]) * scale
                s = jnp.where(ok, s, F32(-1e30))
                top = jnp.max(s, axis=1, keepdims=True)
                e = jnp.exp(s - top)
                total = jnp.sum(e, axis=1, keepdims=True)
                pr = (e / total).astype(BF)
                ctx_ref[pl.ds(back, BLOCK), h * LANES : (h + 1) * LANES] = dot_nn(
                    pr, v_ref[:n, :]
                ).astype(BF)
                lse_ref[h, i * BLOCK : n, :] = top + jnp.log(total)

    outs = [
        whole((2, rows, LANES), BF),
        whole((rows, LANES), BF),
        whole((rows, LANES), BF),
        whole((rows, 2 * LANES), BF),
        whole((2, rows, 1), F32),
    ]
    flops = 2 * rows * rows * LANES * 2 * 2
    return kernel_call(kernel, outs, 2, (place, *lens, qkv, cosine, sine), flops, 8 << 20)


def attention_back(place, lens, q, k, v, lse, dctx, cosine, sine):
    rows = k.shape[0]
    blocks = rows // BLOCK
    scale = HEAD_SIZE ** (-0.5)

    def kernel(place_ref, len_ref, kpos_ref, q_ref, k_ref, v_ref, lse_ref, dctx_ref, cos_ref, sin_ref, out_ref, dk_ref, dv_ref):
        z, length = place_ref[0], len_ref[0]
        dk_ref[...] = jnp.zeros_like(dk_ref)
        dv_ref[...] = jnp.zeros_like(dv_ref)
        for i in range(blocks):
            back = pl.multiple_of(lax.rem(z - i + blocks, blocks) * BLOCK, BLOCK)
            n = (i + 1) * BLOCK
            ok = kpos_ref[:, :n] < length
            cosine, sine = cos_ref[i * BLOCK : n, :], sin_ref[i * BLOCK : n, :]
            for h in range(2):
                qi = q_ref[h, i * BLOCK : n, :]
                di = dctx_ref[pl.ds(back, BLOCK), h * LANES : (h + 1) * LANES]
                s = dot_nt(qi, k_ref[:n, :]) * scale
                p = jnp.where(ok, jnp.exp(s - lse_ref[h, i * BLOCK : n, :]), F32(0.0))
                dp = dot_nt(di, v_ref[:n, :])
                delta = jnp.sum(p * dp, axis=1, keepdims=True)
                ds = (p * (dp - delta)).astype(BF)
                dq = dot_nn(ds, k_ref[:n, :]) * scale
                out_ref[pl.ds(back, BLOCK), h * LANES : (h + 1) * LANES] = turn(
                    dq, cosine, -sine
                ).astype(BF)
                dk_ref[:n, :] += dot_tn(ds, qi)
                dv_ref[:n, :] += dot_tn(p.astype(BF), di)
        for i in range(blocks):
            back = pl.multiple_of(lax.rem(z - i + blocks, blocks) * BLOCK, BLOCK)
            rs = slice(i * BLOCK, (i + 1) * BLOCK)
            out_ref[pl.ds(back, BLOCK), 2 * LANES : 3 * LANES] = turn(
                dk_ref[rs, :] * scale, cos_ref[rs, :], -sin_ref[rs, :]
            ).astype(BF)
            out_ref[pl.ds(back, BLOCK), 3 * LANES : 4 * LANES] = dv_ref[rs, :].astype(BF)

    flops = 2 * rows * rows * LANES * 2 * 5
    return kernel_call(
        kernel,
        whole((rows, 4 * LANES), BF),
        2,
        (place, *lens, q, k, v, lse, dctx, cosine, sine),
        flops,
        8 << 20,
        scratch=[pltpu.VMEM((rows, LANES), F32), pltpu.VMEM((rows, LANES), F32)],
    )


def pad_head(a):
    return jnp.pad(a, ((0, 0), (0, LANES - HEAD_SIZE)))


def rms_of(rows):
    return lax.rsqrt(jnp.mean(rows * rows, axis=-1, keepdims=True) + eps)


def layer(
    inputs,
    valid,
    out_grad,
    teacher,
    norm_attn,
    w_query,
    key_matrix,
    value_matrix,
    w_out,
    norm_mlp,
    w_gate,
    w_up,
    w_down,
):
    seqs, seg, width = inputs.shape
    y = lax.axis_index("tensor")
    k = lax.axis_index("context")
    z, x, c = k // 4, (k // 2) % 2, k % 2
    place = jnp.stack([z, x, c, y]).astype(jnp.int32)
    seq_len = 16 * seg
    depth = norm_attn.shape[0]

    def mine(a):
        return lax.dynamic_index_in_dim(a, y, 0, keepdims=False)

    own = mine(inputs)
    a_blocks, g_blocks, d_blocks = pack_weights(
        place, w_query, key_matrix, value_matrix, w_out.T, w_gate, w_up, w_down.T
    )
    rows_all = gather_rows(own)
    small = jnp.zeros((8, width), F32)
    small = lax.dynamic_update_slice(small, norm_attn.astype(F32)[None], (0, k * depth))
    small = lax.dynamic_update_slice(small, norm_mlp.astype(F32)[None], (1, k * depth))
    counts = jnp.sum(valid.astype(F32), axis=1)
    small = small.at[2, 0].set(counts[0]).at[2, 1].set(counts[1])
    small = sum_context(small)
    gain1, gain2 = small[0:1], small[1:2]
    count = small[2, 0] + small[2, 1]
    length = jnp.where(y == 0, small[2, 0], small[2, 1]).astype(jnp.int32)[None]

    w_attn = spread(place, a_blocks)
    w_qkv = jnp.concatenate([pad_head(w_attn[:, HEAD_SIZE * i : HEAD_SIZE * (i + 1)]) for i in range(4)], axis=1)
    w_ot = jnp.concatenate([pad_head(w_attn[:, HEAD_SIZE * i : HEAD_SIZE * (i + 1)]) for i in (4, 5)], axis=1)
    w_gu = spread(place, g_blocks)
    w_dt = spread(place, d_blocks)
    hidden = w_dt.shape[1]

    far = jnp.arange(2, dtype=jnp.int32)
    pos = (
        jnp.arange(4, dtype=jnp.int32)[:, None, None, None] * (4 * seg)
        + (far ^ x)[None, :, None, None] * (2 * seg)
        + (far ^ c)[None, None, :, None] * seg
        + jnp.arange(seg, dtype=jnp.int32)[None, None, None, :]
    ).reshape(seq_len)
    half = HEAD_SIZE // 2
    freqs = jnp.exp(-math.log(theta) * jnp.arange(half, dtype=F32) / half)
    angles = pos.astype(F32)[:, None] * freqs[None, :]
    cos_half, sin_half = jnp.cos(angles), jnp.sin(angles)
    pad = jnp.zeros((seq_len, LANES - HEAD_SIZE), F32)
    cosine = jnp.concatenate([cos_half, cos_half, pad], axis=1)
    sine = jnp.concatenate([-sin_half, sin_half, pad], axis=1)
    lens = (length, pos[None, :])

    x_all = rows_all.astype(F32)
    h1 = (x_all * rms_of(x_all) * gain1).astype(BF)
    qkv = dot_nn(h1, w_qkv)
    q, keys, values, ctx, lse = attention(place, lens, qkv, cosine, sine)
    attn = scatter_rows(dot_nt(ctx, w_ot))
    x_own = own.astype(F32)
    resid = x_own + attn
    inverse2 = rms_of(resid)
    normed2 = resid * inverse2
    h2 = gather_rows((normed2 * gain2).astype(BF))
    gu = dot_nn(h2, w_gu)
    gate, up = gu[:, :hidden], gu[:, hidden:]
    sigma = jax.nn.sigmoid(gate)
    silu = gate * sigma
    act = (silu * up).astype(BF)
    out = resid + scatter_rows(dot_nt(act, w_dt))
    out_own = out.astype(BF)
    okf = mine(valid).astype(F32)[:, None]
    diff = out - mine(teacher).astype(F32)
    squares = jnp.sum(okf * diff * diff)
    dout = okf * (mine(out_grad).astype(F32) + F32(seqs * seq_len) / count * diff)
    dm = gather_rows(dout.astype(BF))
    dact = dot_nn(dm, w_dt)
    g_down = collect(place, dot_tn(dm, act))
    dgate = (dact * up * sigma * (1.0 + gate * (1.0 - sigma))).astype(BF)
    dup = (dact * silu).astype(BF)
    dgu = jnp.concatenate([dgate, dup], axis=1)
    dh2 = scatter_rows(dot_nt(dgu, w_gu))
    part_gu = dot_tn(h2, dgu)
    tail2 = jnp.sum(part_gu * w_gu.astype(F32), axis=1, keepdims=True)
    g_gu = collect(place, jnp.concatenate([part_gu, tail2], axis=1))
    scaled = dh2 * gain2
    dresid = dout + inverse2 * (scaled - normed2 * jnp.mean(scaled * normed2, axis=-1, keepdims=True))
    da = gather_rows(dresid.astype(BF))
    dctx = dot_nn(da, w_ot).astype(BF)
    part_ot = dot_tn(da, ctx)
    dqkv = attention_back(place, lens, q, keys, values, lse, dctx, cosine, sine)
    dh1 = scatter_rows(dot_nt(dqkv, w_qkv))
    part_qkv = dot_tn(h1, dqkv)
    tail1 = jnp.sum(part_qkv * w_qkv.astype(F32), axis=1, keepdims=True)
    cut = [part_qkv[:, LANES * i : LANES * i + HEAD_SIZE] for i in range(4)]
    cut += [part_ot[:, LANES * i : LANES * i + HEAD_SIZE] for i in range(2)]
    g_attn = collect(place, jnp.concatenate(cut + [tail1], axis=1))
    inverse1 = rms_of(x_own)
    normed1 = x_own * inverse1
    scaled1 = dh1 * gain1
    dx = dresid + inverse1 * (scaled1 - normed1 * jnp.mean(scaled1 * normed1, axis=-1, keepdims=True))

    both_out = move_y(out_own)
    both_dx = move_y(dx)
    first = y == 0
    output = jnp.stack([jnp.where(first, out_own, both_out), jnp.where(first, both_out, out_own)])
    input_grad = jnp.stack([jnp.where(first, dx, both_dx), jnp.where(first, both_dx, dx)])
    squares = sum_context(jnp.full((8, LANES), squares, F32))
    squares = squares + move_y(squares)
    loss = squares[0, 0] / (count * width)

    grad_query, grad_key, grad_value, grad_out, tail1 = unpack(
        place, g_attn, (2 * HEAD_SIZE, HEAD_SIZE, HEAD_SIZE, 2 * HEAD_SIZE, 1), (False, True, True, False, False)
    )
    grad_gate, grad_up, tail2 = unpack(place, g_gu, (hidden, hidden, 1), (False, False, False))
    (grad_down,) = unpack(place, g_down, (hidden,), (False,))
    tails = jnp.stack([jnp.sum(tail1, axis=1), jnp.sum(tail2, axis=1)])
    tails = tails + move_y(tails)
    grad_gain1 = tails[0] / norm_attn.astype(F32)
    grad_gain2 = tails[1] / norm_mlp.astype(F32)
    return (
        output,
        loss,
        input_grad,
        grad_gain1,
        grad_gain2,
        grad_query,
        grad_key,
        grad_value,
        grad_out.T,
        grad_gate,
        grad_up,
        grad_down.T,
    )


def rms_forward(value_rows, gain):
    inverse = lax.rsqrt(jnp.mean(value_rows * value_rows, axis=-1, keepdims=True) + eps)
    normed = value_rows * inverse
    return (normed, inverse, normed * gain)


def rms_backward(grad, normed, inverse, gain):
    scaled = grad * gain
    return inverse * (scaled - normed * jnp.mean(scaled * normed, axis=-1, keepdims=True))


def rotate(value_rows, cosine, sine):
    half = value_rows.shape[-1] // 2
    first, second = (value_rows[..., :half], value_rows[..., half:])
    return jnp.concatenate(
        [first * cosine - second * sine, second * cosine + first * sine], axis=-1
    )


def rotate_back(grad, cosine, sine):
    half = grad.shape[-1] // 2
    first, second = (grad[..., :half], grad[..., half:])
    return jnp.concatenate(
        [first * cosine + second * sine, second * cosine - first * sine], axis=-1
    )


def allowed_pairs(key_ok, qpos, seq_len):
    kpos = jnp.arange(seq_len, dtype=jnp.int32)
    return (kpos[None, :] // BLOCK <= qpos[:, None] // BLOCK) & (key_ok[None, :] > 0)


def masked_scores(query_rows, key_rows, key_ok, qpos, scale):
    raw = (
        jnp.einsum("qkgd,jkd->kgqj", query_rows, key_rows, preferred_element_type=jnp.float32)
        * scale
    )
    allowed = allowed_pairs(key_ok, qpos, key_rows.shape[0])
    return jnp.where(allowed, raw, jnp.float32(-1e30))


def dot_left(left, right):
    return lax.dot_general(
        left, right, (((0,), (0,)), ((), ())), preferred_element_type=jnp.float32
    )


def dot_right(left, right):
    return lax.dot_general(
        left, right, (((1,), (1,)), ((), ())), preferred_element_type=jnp.float32
    )


def shards(
    inputs,
    valid,
    out_grad,
    teacher,
    norm_attn,
    w_query,
    key_matrix,
    value_matrix,
    w_out,
    norm_mlp,
    w_gate,
    w_up,
    w_down,
):
    seqs, seg, width = inputs.shape
    ctx_size = lax.axis_size("context")
    index = lax.axis_index("context")
    scale = HEAD_SIZE ** (-0.5)
    half = HEAD_SIZE // 2
    gathered = (
        lax.all_gather(norm_attn, "context", axis=0, tiled=True),
        lax.all_gather(w_query, "context", axis=0, tiled=True),
        lax.all_gather(key_matrix, "context", axis=0, tiled=True),
        lax.all_gather(value_matrix, "context", axis=0, tiled=True),
        lax.all_gather(w_out, "context", axis=1, tiled=True),
        lax.all_gather(norm_mlp, "context", axis=0, tiled=True),
        lax.all_gather(w_gate, "context", axis=0, tiled=True),
        lax.all_gather(w_up, "context", axis=0, tiled=True),
        lax.all_gather(w_down, "context", axis=1, tiled=True),
    )
    gain_first, wq, wk, wv, wo, gain_second, wg, wu, wd = gathered
    gain1 = gain_first.astype(jnp.float32)
    gain2 = gain_second.astype(jnp.float32)
    heads_q = wq.shape[1] // HEAD_SIZE
    heads_kv = wk.shape[1] // HEAD_SIZE
    head_group = heads_q // heads_kv
    row_count = seqs * seg
    positions = index * seg + jnp.arange(seg, dtype=jnp.int32)
    freqs = jnp.exp(-math.log(theta) * jnp.arange(half, dtype=jnp.float32) / half)
    angles = positions.astype(jnp.float32)[:, None] * freqs[None, :]
    cosine = jnp.cos(angles)[:, None, :]
    sine = jnp.sin(angles)[:, None, :]
    x = inputs.astype(jnp.float32)
    normed1, inverse1, pre1 = rms_forward(x, gain1)
    h1 = pre1.astype(jnp.bfloat16).reshape(row_count, width)
    query_before_rotary = jnp.dot(h1, wq, preferred_element_type=jnp.float32).reshape(
        seqs, seg, heads_q, HEAD_SIZE
    )
    key_before_rotary = jnp.dot(h1, wk, preferred_element_type=jnp.float32).reshape(
        seqs, seg, heads_kv, HEAD_SIZE
    )
    value_own = (
        jnp.dot(h1, wv, preferred_element_type=jnp.float32)
        .astype(jnp.bfloat16)
        .reshape(seqs, seg, heads_kv * HEAD_SIZE)
    )
    query_rows = (
        rotate(query_before_rotary, cosine, sine)
        .astype(jnp.bfloat16)
        .reshape(seqs, seg, heads_kv, head_group, HEAD_SIZE)
    )
    key_own = (
        rotate(key_before_rotary, cosine, sine)
        .astype(jnp.bfloat16)
        .reshape(seqs, seg, heads_kv * HEAD_SIZE)
    )
    keys_all, values_all, valid_all = (
        lax.all_gather(key_own, "context", axis=1, tiled=True),
        lax.all_gather(value_own, "context", axis=1, tiled=True),
        lax.all_gather(valid.astype(jnp.bfloat16), "context", axis=1, tiled=True),
    )
    seq_len = keys_all.shape[1]

    def attend(carry, items):
        qseq, kseq, vseq, okseq = items
        key_rows = kseq.reshape(seq_len, heads_kv, HEAD_SIZE)
        value_rows = vseq.reshape(seq_len, heads_kv, HEAD_SIZE)
        scores = masked_scores(qseq, key_rows, okseq, positions, scale)
        top = jnp.max(scores, axis=-1, keepdims=True)
        expo = jnp.exp(scores - top)
        total = jnp.sum(expo, axis=-1, keepdims=True)
        probr = (expo / total).astype(jnp.bfloat16)
        ctx = jnp.einsum("kgqj,jkd->qkgd", probr, value_rows, preferred_element_type=jnp.float32)
        lse = (top + jnp.log(total))[..., 0]
        return (carry, (ctx.astype(jnp.bfloat16).reshape(seg, heads_q * HEAD_SIZE), lse))

    carry, (context, lse_all) = lax.scan(
        attend, jnp.float32(0.0), (query_rows, keys_all, values_all, valid_all)
    )
    ctx_flat = context.reshape(row_count, heads_q * HEAD_SIZE)
    attn = lax.psum(
        jnp.dot(ctx_flat, wo, preferred_element_type=jnp.float32).astype(jnp.bfloat16), "tensor"
    ).astype(jnp.float32)
    resid = x + attn.reshape(seqs, seg, width)
    normed2, inverse2, pre2 = rms_forward(resid, gain2)
    h2 = pre2.astype(jnp.bfloat16).reshape(row_count, width)
    gate = jnp.dot(h2, wg, preferred_element_type=jnp.float32)
    up = jnp.dot(h2, wu, preferred_element_type=jnp.float32)
    sigma = jax.nn.sigmoid(gate)
    silu = gate * sigma
    act = (silu * up).astype(jnp.bfloat16)
    mixed = lax.psum(
        jnp.dot(act, wd, preferred_element_type=jnp.float32).astype(jnp.bfloat16), "tensor"
    ).astype(jnp.float32)
    out = resid + mixed.reshape(seqs, seg, width)
    output = out.astype(jnp.bfloat16)
    validf = valid.astype(jnp.float32)[..., None]
    diff = out - teacher.astype(jnp.float32)
    count, squares = lax.psum(
        (jnp.sum(valid.astype(jnp.float32)), jnp.sum(validf * diff * diff)), "context"
    )
    loss = squares / (count * width)
    dout = validf * (
        out_grad.astype(jnp.float32) + jnp.float32(seqs * seg * ctx_size) / count * diff
    )
    dm = dout.astype(jnp.bfloat16).reshape(row_count, width)
    grad_down = dot_left(act, dm)
    dact = dot_right(dm, wd)
    dgate = (dact * up * sigma * (1.0 + gate * (1.0 - sigma))).astype(jnp.bfloat16)
    dup = (dact * silu).astype(jnp.bfloat16)
    grad_gate = dot_left(h2, dgate)
    grad_up = dot_left(h2, dup)
    dh2 = (
        lax.psum((dot_right(dgate, wg) + dot_right(dup, wu)).astype(jnp.bfloat16), "tensor")
        .astype(jnp.float32)
        .reshape(seqs, seg, width)
    )
    grad_gain2 = jnp.sum(dh2 * normed2, axis=(0, 1))
    dresid = dout + rms_backward(dh2, normed2, inverse2, gain2)
    dattn = dresid.astype(jnp.bfloat16).reshape(row_count, width)
    grad_out = dot_left(ctx_flat, dattn)
    dctx = (
        dot_right(dattn, wo)
        .astype(jnp.bfloat16)
        .reshape(seqs, seg, heads_kv, head_group, HEAD_SIZE)
    )

    def attend_back(carry, items):
        qseq, kseq, vseq, okseq, lseq, dseq = items
        allowed = allowed_pairs(okseq, positions, seq_len)

        def head_back(parts):
            qhead, khead, vhead, dhead, lhead = parts
            raw = (
                jnp.einsum("qgd,jd->gqj", qhead, khead, preferred_element_type=jnp.float32) * scale
            )
            scores = jnp.where(allowed[None], raw, jnp.float32(-1e30))
            prob = jnp.exp(scores - lhead[..., None])
            probr = prob.astype(jnp.bfloat16)
            dprob = jnp.einsum("qgd,jd->gqj", dhead, vhead, preferred_element_type=jnp.float32)
            delta = jnp.sum(prob * dprob, axis=-1, keepdims=True)
            dscore = (prob * (dprob - delta)).astype(jnp.bfloat16)
            dq = (
                jnp.einsum("gqj,jd->qgd", dscore, khead, preferred_element_type=jnp.float32) * scale
            )
            dk = (
                jnp.einsum("gqj,qgd->jd", dscore, qhead, preferred_element_type=jnp.float32) * scale
            )
            dv = jnp.einsum("gqj,qgd->jd", probr, dhead, preferred_element_type=jnp.float32)
            return (dq, dk, dv)

        heads_in = (
            jnp.moveaxis(qseq, 1, 0),
            jnp.moveaxis(kseq.reshape(seq_len, heads_kv, HEAD_SIZE), 1, 0),
            jnp.moveaxis(vseq.reshape(seq_len, heads_kv, HEAD_SIZE), 1, 0),
            jnp.moveaxis(dseq, 1, 0),
            lseq,
        )
        dq_heads, dk_heads, dv_heads = lax.map(head_back, heads_in)
        dq = jnp.moveaxis(dq_heads, 0, 1)
        dk = jnp.moveaxis(dk_heads, 0, 1).reshape(seq_len, heads_kv * HEAD_SIZE)
        dv = jnp.moveaxis(dv_heads, 0, 1).reshape(seq_len, heads_kv * HEAD_SIZE)
        dk_own, dv_own = (
            lax.psum_scatter(dk, "context", scatter_dimension=0, tiled=True),
            lax.psum_scatter(dv, "context", scatter_dimension=0, tiled=True),
        )
        return (carry, (dq, dk_own, dv_own))

    carry, (dq_all, dk_all, dv_all) = lax.scan(
        attend_back, jnp.float32(0.0), (query_rows, keys_all, values_all, valid_all, lse_all, dctx)
    )
    dqpre = (
        rotate_back(dq_all.reshape(seqs, seg, heads_q, HEAD_SIZE), cosine, sine)
        .astype(jnp.bfloat16)
        .reshape(row_count, heads_q * HEAD_SIZE)
    )
    dkpre = (
        rotate_back(dk_all.reshape(seqs, seg, heads_kv, HEAD_SIZE), cosine, sine)
        .astype(jnp.bfloat16)
        .reshape(row_count, heads_kv * HEAD_SIZE)
    )
    dvr = dv_all.astype(jnp.bfloat16).reshape(row_count, heads_kv * HEAD_SIZE)
    grad_query = dot_left(h1, dqpre)
    grad_key = dot_left(h1, dkpre)
    grad_value = dot_left(h1, dvr)
    dh1 = (
        lax.psum(
            (dot_right(dqpre, wq) + dot_right(dkpre, wk) + dot_right(dvr, wv)).astype(jnp.bfloat16),
            "tensor",
        )
        .astype(jnp.float32)
        .reshape(seqs, seg, width)
    )
    grad_gain1 = jnp.sum(dh1 * normed1, axis=(0, 1))
    input_grad = dresid + rms_backward(dh1, normed1, inverse1, gain1)
    summed = (
        lax.psum_scatter(grad_gain1, "context", scatter_dimension=0, tiled=True),
        lax.psum_scatter(grad_query, "context", scatter_dimension=0, tiled=True),
        lax.psum_scatter(grad_key, "context", scatter_dimension=0, tiled=True),
        lax.psum_scatter(grad_value, "context", scatter_dimension=0, tiled=True),
        lax.psum_scatter(grad_out, "context", scatter_dimension=1, tiled=True),
        lax.psum_scatter(grad_gain2, "context", scatter_dimension=0, tiled=True),
        lax.psum_scatter(grad_gate, "context", scatter_dimension=0, tiled=True),
        lax.psum_scatter(grad_up, "context", scatter_dimension=0, tiled=True),
        lax.psum_scatter(grad_down, "context", scatter_dimension=1, tiled=True),
    )
    (
        grad_gain1,
        grad_query,
        grad_key,
        grad_value,
        grad_out,
        grad_gain2,
        grad_gate,
        grad_up,
        grad_down,
    ) = summed
    return (
        output,
        loss,
        input_grad,
        grad_gain1,
        grad_gain2,
        grad_query,
        grad_key,
        grad_value,
        grad_out,
        grad_gate,
        grad_up,
        grad_down,
    )


def solution(mesh):
    in_specs = (
        P(None, "context", None),
        P(None, "context"),
        P(None, "context", None),
        P(None, "context", None),
        P("context"),
        P("context", "tensor"),
        P("context", "tensor"),
        P("context", "tensor"),
        P("tensor", "context"),
        P("context"),
        P("context", "tensor"),
        P("context", "tensor"),
        P("tensor", "context"),
    )
    out_specs = (
        P(None, "context", None),
        P(),
        P(None, "context", None),
        P("context"),
        P("context"),
        P("context", "tensor"),
        P("context", "tensor"),
        P("context", "tensor"),
        P("tensor", "context"),
        P("context", "tensor"),
        P("context", "tensor"),
        P("tensor", "context"),
    )
    fits = dict(mesh.shape) == {"tensor": 2, "context": 16}
    return jax.shard_map(
        layer if fits else shards, mesh=mesh, in_specs=in_specs, out_specs=out_specs, check_vma=False
    )
```

```python
import functools
import math

import jax
import jax.numpy as jnp
from jax import lax
from jax.experimental import pallas as pl
from jax.experimental.pallas import tpu as pltpu
from jax.sharding import PartitionSpec as P

HEAD_SIZE = 80
BLOCK = 256
LANES = 128

eps = 1e-05
theta = 10000.0
BF = jnp.bfloat16
F32 = jnp.float32
MIB = 1024 * 1024
SLOW = ()


def whole(shape, dtype):
    return jax.ShapeDtypeStruct(tuple(shape), dtype)


def kernel_call(body, outs, ins, scalars=0, far=(), flops=0, scratch=(), limit=16, name=None):
    single = not isinstance(outs, (list, tuple))
    spec = lambda i: (
        pl.BlockSpec(memory_space=pltpu.SMEM)
        if i < scalars
        else pl.BlockSpec(memory_space=pl.ANY)
        if i in far
        else pl.BlockSpec(memory_space=pltpu.VMEM)
    )
    out_spec = pl.BlockSpec(memory_space=pltpu.VMEM)
    nbytes = sum(math.prod(a.shape) * a.dtype.itemsize for a in ins)
    nbytes += sum(math.prod(o.shape) * o.dtype.itemsize for o in ([outs] if single else outs))
    return pl.pallas_call(
        body,
        out_shape=outs,
        in_specs=[spec(i) for i in range(len(ins))],
        out_specs=out_spec if single else [out_spec] * len(outs),
        scratch_shapes=list(scratch),
        compiler_params=pltpu.CompilerParams(vmem_limit_bytes=limit * MIB),
        cost_estimate=pl.CostEstimate(flops=flops if name in SLOW else 0, bytes_accessed=0, transcendentals=0),
        name=name,
    )(*ins)


def dot_nn(a, b):
    return lax.dot_general(a, b, (((1,), (0,)), ((), ())), preferred_element_type=F32)


def dot_nt(a, b):
    return lax.dot_general(a, b, (((1,), (1,)), ((), ())), preferred_element_type=F32)


def dot_tn(a, b):
    return lax.dot_general(a, b, (((0,), (0,)), ((), ())), preferred_element_type=F32)


def move_c(a):
    return lax.ppermute(a, "context", [(k, k ^ 1) for k in range(16)])


def move_x(a):
    return lax.ppermute(a, "context", [(k, k ^ 2) for k in range(16)])


def move_z(a, step):
    return lax.ppermute(a, "context", [(k, (k + 4 * step) % 16) for k in range(16)])


def move_y(a):
    return lax.ppermute(a, "tensor", [(0, 1), (1, 0)])


def share_out(a):
    return lax.all_to_all(a, "context", split_axis=0, concat_axis=0, tiled=True)


def after(value, *others):
    return lax.optimization_barrier((value, *others))[0]


def stack(pieces):
    def body(*refs):
        for m in range(4):
            refs[4][m] = refs[m][...]

    return kernel_call(body, whole((4, *pieces[0].shape), BF), tuple(pieces), limit=8, name="stack")


def gather_rows(own, *late, early=()):
    near = [own] + [move_z(own, m) for m in (1, 2, 3)]
    far = [move_x(own)]
    far += [move_x(after(p, far[0], *early)) for p in near[1:]]
    near_all, far_all = stack(near), stack(far)
    last = after(far_all, *late) if late else far_all
    return (near_all, move_c(near_all), far_all, move_c(last)), near, far


def scatter_rows(part, *late):
    far1, far0, near1, *near0 = part
    shape = far1.shape[1:]

    def add_far(a_ref, b_ref, *outs):
        for m in range(4):
            outs[m][...] = (a_ref[m].astype(F32) + b_ref[m].astype(F32)).astype(BF)

    def add_near(a_ref, b_ref, c_ref, out_ref):
        out_ref[...] = (a_ref[...].astype(F32) + b_ref[...].astype(F32) + c_ref[...].astype(F32)).astype(BF)

    far = kernel_call(add_far, [whole(shape, BF)] * 4, (far0, move_c(far1)), limit=16, name="add_far")
    near1 = move_c(near1)
    come = {m: move_x(far[m]) for m in (2, 1, 3, 0)}
    if late:
        come[2] = after(come[2], *late)
    terms = [near0[0], near1[0], come[0]]
    for m in (2, 1, 3):
        s = kernel_call(add_near, whole(shape, BF), (near0[m], near1[m], come[m]), limit=8, name="add_near")
        terms.append(move_z(s, 4 - m))
    return terms, far, come


def part_shapes(seg, width):
    return [
        whole((4, seg, width), BF),
        whole((4, seg, width), BF),
        whole((4, seg, width), BF),
    ] + [whole((seg, width), BF)] * 4


def write_part(outs, group, value):
    far1, far0, near1, *near0 = outs
    seg = far1.shape[1]
    for m in range(4):
        rows = value[m * seg : (m + 1) * seg]
        if group == 3:
            far1[m] = rows.astype(BF)
        elif group == 2:
            far0[m] = rows.astype(BF)
        elif group == 1:
            near1[m] = rows.astype(BF)
        else:
            near0[m][...] = rows.astype(BF)


def total(refs):
    out = refs[0][...].astype(F32)
    for r in refs[1:]:
        out = out + r[...].astype(F32)
    return out


FIRST = 384
SECOND = 640
EXTRA = 4


def pack_first(wq, wk, wv, wot, extra, wdt):
    rows, d = wq.shape[0], HEAD_SIZE
    hidden = wdt.shape[1] // 16
    some = FIRST - 4 * d - EXTRA

    def body(q_ref, k_ref, v_ref, o_ref, e_ref, d_ref, out_ref):
        for k in range(16):
            block = jnp.concatenate(
                [
                    q_ref[:, k * d : (k + 1) * d],
                    k_ref[:, k // 4 * d : (k // 4 + 1) * d],
                    v_ref[:, k // 4 * d : (k // 4 + 1) * d],
                    o_ref[:, k * d : (k + 1) * d],
                    e_ref[...],
                    d_ref[:, k * hidden : k * hidden + some],
                ],
                axis=1,
            )
            out_ref[k] = block

    return kernel_call(
        body, whole((16, rows, FIRST), BF), (wq, wk, wv, wot, extra, wdt), limit=16, name="pack_first"
    )


def pack_second(wg, wu, wdt):
    rows = wg.shape[0]
    hidden = wg.shape[1] // 16
    some = FIRST - 4 * HEAD_SIZE - EXTRA
    spare = SECOND - 3 * hidden + some

    def body(g_ref, u_ref, d_ref, out_ref):
        for k in range(16):
            block = jnp.concatenate(
                [
                    d_ref[:, k * hidden + some : (k + 1) * hidden],
                    g_ref[:, k * hidden : (k + 1) * hidden],
                    u_ref[:, k * hidden : (k + 1) * hidden],
                    jnp.zeros((rows, spare), BF),
                ],
                axis=1,
            )
            out_ref[k] = block

    return kernel_call(body, whole((16, rows, SECOND), BF), (wg, wu, wdt), limit=16, name="pack_second")


def share_blocks(a):
    return share_out(a.reshape(-1, a.shape[2])).reshape(a.shape)


def of_other(a):
    return lax.all_gather(a, "tensor", axis=0, tiled=False)


def over_sequences(parts):
    return lax.psum_scatter(parts, "tensor", scatter_dimension=0, tiled=False)


def unpack_second(second, hidden):
    rows = second.shape[1]

    def body(s_ref, g_ref, u_ref):
        for k in range(16):
            c = s_ref[k].astype(F32)
            g_ref[:, k * hidden : (k + 1) * hidden] = c[:, :hidden]
            u_ref[:, k * hidden : (k + 1) * hidden] = c[:, hidden : 2 * hidden]

    return kernel_call(body, [whole((rows, 16 * hidden), F32)] * 2, (second,), limit=16, name="unpack_second")


def unpack_first(first, second, hidden):
    rows, d = first.shape[1], HEAD_SIZE
    cut = SECOND - 2 * hidden
    rest = 4 * d + hidden - cut

    def body(f_ref, s_ref, q_ref, k_ref, v_ref, o_ref, d_ref, tail_ref):
        tail = jnp.zeros((rows, 3), F32)
        for k in range(16):
            b = f_ref[k].astype(F32)
            q_ref[:, k * d : (k + 1) * d] = b[:, :d]
            o_ref[:, k * d : (k + 1) * d] = b[:, 3 * d : 4 * d]
            if k % 4 == 0:
                keys = jnp.zeros((rows, 2 * d), F32)
            keys = keys + b[:, d : 3 * d]
            if k % 4 == 3:
                k_ref[:, k // 4 * d : (k // 4 + 1) * d] = keys[:, :d]
                v_ref[:, k // 4 * d : (k // 4 + 1) * d] = keys[:, d:]
            tail = tail + b[:, rest : rest + 3]
            d_ref[:, k * hidden : k * hidden + cut] = s_ref[k][:, 2 * hidden :].astype(F32)
            d_ref[:, k * hidden + cut : (k + 1) * hidden] = b[:, 4 * d : rest]
        tail_ref[...] = tail

    outs = [whole((rows, w), F32) for w in (16 * d, 4 * d, 4 * d, 16 * d, 16 * hidden, 3)]
    return kernel_call(body, outs, (first, second), limit=16, name="unpack_first")


def prepare_attention(place, mine, both):
    size, d = mine.shape[1], HEAD_SIZE
    depth = 16 * size

    def body(place_ref, mine_ref, both_ref, w_ref, out_ref, row_ref, info_ref):
        other_ref = both_ref.at[1 - place_ref[3]]
        info_ref[...] = jnp.zeros_like(info_ref)
        for k in range(16):
            rs = slice(k * size, (k + 1) * size)
            parts = [mine_ref[k], other_ref[k]]
            w_ref[rs, :] = jnp.concatenate([p[:, : 3 * d] for p in parts], axis=1)
            out_ref[rs, :] = jnp.concatenate([p[:, 3 * d : 4 * d] for p in parts], axis=1)
            info_ref[rs, :EXTRA] = parts[0][:, 4 * d : 4 * d + EXTRA].astype(F32)
        for b in range(depth // LANES):
            rs = slice(b * LANES, (b + 1) * LANES)
            row_ref[:, rs] = info_ref[rs, :].T[0:8, :]

    return kernel_call(
        body,
        [whole((depth, 6 * d), BF), whole((depth, 2 * d), BF), whole((8, depth), F32)],
        (place, mine, both),
        scalars=1,
        scratch=[pltpu.VMEM((depth, LANES), F32)],
        limit=16,
        name="prepare_attention",
    )


def prepare_feed(place, first_mine, first_both, mine, both, hidden):
    size = mine.shape[1]
    depth = 16 * size
    at = 4 * HEAD_SIZE + EXTRA
    rest = hidden - (FIRST - at)

    def body(place_ref, fm_ref, fboth_ref, m_ref, both_ref, gu_ref, d_ref):
        fo_ref, o_ref = fboth_ref.at[1 - place_ref[3]], both_ref.at[1 - place_ref[3]]
        for k in range(16):
            rs = slice(k * size, (k + 1) * size)
            fm, fo, m, o = fm_ref[k], fo_ref[k], m_ref[k], o_ref[k]
            gu_ref[rs, :] = jnp.concatenate(
                [
                    m[:, rest : rest + hidden],
                    o[:, rest : rest + hidden],
                    m[:, rest + hidden : rest + 2 * hidden],
                    o[:, rest + hidden : rest + 2 * hidden],
                ],
                axis=1,
            )
            d_ref[rs, :] = jnp.concatenate([fm[:, at:], m[:, :rest], fo[:, at:], o[:, :rest]], axis=1)

    return kernel_call(
        body,
        [whole((depth, 4 * hidden), BF), whole((depth, 2 * hidden), BF)],
        (place, first_mine, first_both, mine, both),
        scalars=1,
        limit=16,
        name="prepare_feed",
    )


def turn(a, cosine, sine):
    half = HEAD_SIZE // 2
    lane = lax.broadcasted_iota(jnp.int32, a.shape, 1)
    swapped = jnp.where(lane < half, pltpu.roll(a, LANES - half, 1), pltpu.roll(a, half, 1))
    return a * cosine + swapped * sine


def head_of(value, at):
    part = value[:, at * HEAD_SIZE : (at + 1) * HEAD_SIZE]
    return jnp.concatenate([part, jnp.zeros((value.shape[0], LANES - HEAD_SIZE), value.dtype)], axis=1)


def attention(place, pieces, weights, w_o, rows_info, length, kpos, cosine, sine):
    seg, width = pieces[0].shape[1:]
    rows = 16 * seg
    blocks = rows // BLOCK
    scale = HEAD_SIZE ** (-0.5)

    def body(place_ref, *refs):
        x_refs = [refs[i // 4].at[i % 4] for i in range(16)]
        w_ref, wo_ref, info_ref, len_ref, kpos_ref, cos_ref, sin_ref = refs[4:11]
        h_ref, q_ref, k_ref, v_ref, ctx_ref, lse_ref, *part = refs[11:]
        z = place_ref[0]
        gain = info_ref[0:1, :]
        length = len_ref[0:1, 0:1]
        for i in range(16):

            @pl.loop(0, seg // 16)
            def _(r):
                at = pl.multiple_of(r * 16, 16)
                xs = x_refs[i][pl.ds(at, 16), :].astype(F32)
                inv = lax.rsqrt(jnp.mean(xs * xs, axis=-1, keepdims=True) + eps)
                h_ref[pl.ds(i * seg + at, 16), :] = (xs * inv * gain).astype(BF)

        for g in range(4):
            qkv = dot_nn(h_ref[g * 4 * seg : (g + 1) * 4 * seg, :], w_ref[...])
            for m in range(4):
                to = pl.multiple_of(lax.rem(z - m + 4, 4) * BLOCK + g * seg, seg)
                to = pl.ds(to, seg)
                piece = qkv[m * seg : (m + 1) * seg]
                cosine, sine = cos_ref[to, :], sin_ref[to, :]
                for h in range(2):
                    q_ref[h, to, :] = turn(head_of(piece, 3 * h), cosine, sine).astype(BF)
                    k_ref[h, to, :] = turn(head_of(piece, 3 * h + 1), cosine, sine).astype(BF)
                    v_ref[h, to, :] = head_of(piece, 3 * h + 2).astype(BF)
        for i in range(blocks):
            m = lax.rem(z - i + 4, 4)
            n = (i + 1) * BLOCK
            ok = kpos_ref[:, :n].astype(F32) < length
            for h in range(2):
                s = dot_nt(q_ref[h, i * BLOCK : n, :], k_ref[h, :n, :]) * scale
                s = jnp.where(ok, s, F32(-1e30))
                top = jnp.max(s, axis=1, keepdims=True)
                e = jnp.exp(s - top)
                tot = jnp.sum(e, axis=1, keepdims=True)
                ctx = dot_nn((e / tot).astype(BF), v_ref[h, :n, :]).astype(BF)
                for g in range(4):
                    to = pl.ds(pl.multiple_of((g * 4 + m) * seg, seg), seg)
                    ctx_ref[to, h * HEAD_SIZE : (h + 1) * HEAD_SIZE] = ctx[g * seg : (g + 1) * seg, :HEAD_SIZE]
                lse_ref[h, i * BLOCK : n, :] = top + jnp.log(tot)
        for g in (3, 2, 1, 0):
            write_part(part, g, dot_nt(ctx_ref[g * 4 * seg : (g + 1) * 4 * seg, :], wo_ref[...]))

    outs = [
        whole((rows, width), BF),
        whole((2, rows, LANES), BF),
        whole((2, rows, LANES), BF),
        whole((2, rows, LANES), BF),
        whole((rows, 2 * HEAD_SIZE), BF),
        whole((2, rows, 1), F32),
    ] + part_shapes(seg, width)
    flops = 2 * rows * width * 6 * LANES + 2 * rows * rows * LANES * 2 * 2
    out = kernel_call(
        body,
        outs,
        (place, *pieces, weights, w_o, rows_info, length, kpos, cosine, sine),
        scalars=1,
        flops=flops,
        name="attention",
    )
    return out[:6], out[6:]


def attention_back(place, pieces, weights, w_o, length, kpos, cosine, sine, q, k, v, lse):
    seg, width = pieces[0].shape[1:]
    rows = 16 * seg
    blocks = rows // BLOCK
    scale = HEAD_SIZE ** (-0.5)

    def body(place_ref, *refs):
        d_refs = [refs[i // 4].at[i % 4] for i in range(16)]
        w_ref, wo_ref, len_ref, kpos_ref, cos_ref, sin_ref, q_ref, k_ref, v_ref, lse_ref = refs[4:14]
        da_ref, dqkv_ref, *part = refs[14:23]
        dctx_ref, dk_ref, dv_ref = refs[23:]
        z = place_ref[0]
        length = len_ref[0:1, 0:1]
        for i in range(16):
            da_ref[i * seg : (i + 1) * seg, :] = d_refs[i][...]
        for g in range(4):
            dctx = dot_nn(da_ref[g * 4 * seg : (g + 1) * 4 * seg, :], wo_ref[...])
            for m in range(4):
                to = pl.multiple_of(lax.rem(z - m + 4, 4) * BLOCK + g * seg, seg)
                for h in range(2):
                    dctx_ref[h, pl.ds(to, seg), :] = head_of(dctx[m * seg : (m + 1) * seg], h).astype(BF)
        dk_ref[...] = jnp.zeros_like(dk_ref)
        dv_ref[...] = jnp.zeros_like(dv_ref)

        def put(i, at, value):
            m = lax.rem(z - i + 4, 4)
            for g in range(4):
                to = pl.ds(pl.multiple_of((g * 4 + m) * seg, seg), seg)
                dqkv_ref[to, at * HEAD_SIZE : (at + 1) * HEAD_SIZE] = value[g * seg : (g + 1) * seg, :HEAD_SIZE]

        for i in range(blocks):
            n = (i + 1) * BLOCK
            ok = kpos_ref[:, :n].astype(F32) < length
            cosine, sine = cos_ref[i * BLOCK : n, :], sin_ref[i * BLOCK : n, :]
            for h in range(2):
                qi = q_ref[h, i * BLOCK : n, :]
                di = dctx_ref[h, i * BLOCK : n, :]
                s = dot_nt(qi, k_ref[h, :n, :]) * scale
                p = jnp.where(ok, jnp.exp(s - lse_ref[h, i * BLOCK : n, :]), F32(0.0))
                dp = dot_nt(di, v_ref[h, :n, :])
                delta = jnp.sum(p * dp, axis=1, keepdims=True)
                ds = (p * (dp - delta)).astype(BF)
                dq = dot_nn(ds, k_ref[h, :n, :]) * scale
                put(i, 3 * h, turn(dq, cosine, -sine).astype(BF))
                dk_ref[h, :n, :] += dot_tn(ds, qi)
                dv_ref[h, :n, :] += dot_tn(p.astype(BF), di)
        for i in range(blocks):
            rs = slice(i * BLOCK, (i + 1) * BLOCK)
            for h in range(2):
                dk = turn(dk_ref[h, rs, :] * scale, cos_ref[rs, :], -sin_ref[rs, :])
                put(i, 3 * h + 1, dk.astype(BF))
                put(i, 3 * h + 2, dv_ref[h, rs, :].astype(BF))
        for g in (3, 2, 1, 0):
            write_part(part, g, dot_nt(dqkv_ref[g * 4 * seg : (g + 1) * 4 * seg, :], w_ref[...]))

    outs = [whole((rows, width), BF), whole((rows, 6 * HEAD_SIZE), BF)] + part_shapes(seg, width)
    flops = 2 * rows * width * 6 * LANES + 2 * rows * rows * LANES * 2 * 5
    out = kernel_call(
        body,
        outs,
        (place, *pieces, weights, w_o, length, kpos, cosine, sine, q, k, v, lse),
        scalars=1,
        flops=flops,
        scratch=[
            pltpu.VMEM((2, rows, LANES), BF),
            pltpu.VMEM((2, rows, LANES), F32),
            pltpu.VMEM((2, rows, LANES), F32),
        ],
        name="attention_back",
    )
    return out[0], out[1], out[2:]


def write_blocks(out_ref, index, chunk, value):
    rows = out_ref.shape[2]
    for k in range(4):
        out_ref[index, chunk * 4 + k] = value[k * rows : (k + 1) * rows].astype(BF)


def attention_grads(place, h1, dqkv, da, ctx, weights, rest, tail2, squares):
    rows, width = h1.shape
    d, cut = HEAD_SIZE, rest.shape[1] // 2
    spare = FIRST - 4 * d - cut - 3

    def body(place_ref, h_ref, dqkv_ref, da_ref, ctx_ref, w_ref, rest_ref, tail_ref, sq_ref, out_ref):
        y = place_ref[3]
        quarter = width // 4
        for b in range(4):
            at = slice(b * quarter, (b + 1) * quarter)
            g = dot_tn(h_ref[:, at], dqkv_ref[...])
            tail1 = jnp.sum(g * w_ref[at, :].astype(F32), axis=1, keepdims=True)
            o = dot_tn(da_ref[:, at], ctx_ref[...])
            sq = jnp.broadcast_to(sq_ref[0:1, 0:1], (quarter, 1))
            last = [tail1, tail_ref[at, :], sq, jnp.zeros((quarter, spare), F32)]
            for h, index in enumerate((y, 1 - y)):
                parts = [g[:, 3 * d * h : 3 * d * (h + 1)], o[:, d * h : d * (h + 1)]]
                parts += [rest_ref[at, cut * h : cut * (h + 1)].astype(F32)]
                write_blocks(out_ref, index, b, jnp.concatenate(parts + last, axis=1))

    return kernel_call(
        body,
        whole((2, 16, width // 16, FIRST), BF),
        (place, h1, dqkv, da, ctx, weights, rest, tail2, squares),
        scalars=1,
        flops=2 * rows * width * 8 * d,
        name="attention_grads",
    )


def feed(pieces, w_gu, w_d):
    seg, width = pieces[0].shape[1:]
    rows = 16 * seg
    hidden = w_d.shape[1]

    def body(*refs):
        h_refs = [refs[i // 4].at[i % 4] for i in range(16)]
        wg_ref, wd_ref, h_ref, gate_ref, act_ref, *part = refs[4:]
        for i in range(16):
            h_ref[i * seg : (i + 1) * seg, :] = h_refs[i][...]
        for g in range(4):
            rs = slice(g * 4 * seg, (g + 1) * 4 * seg)
            both = dot_nn(h_ref[rs, :], wg_ref[...])
            gate_ref[rs, :] = both
            gate, up = both[:, :hidden], both[:, hidden:]
            act_ref[rs, :] = (gate * jax.nn.sigmoid(gate) * up).astype(BF)
        for g in (3, 2, 1, 0):
            rs = slice(g * 4 * seg, (g + 1) * 4 * seg)
            write_part(part, g, dot_nt(act_ref[rs, :], wd_ref[...]))

    outs = [whole((rows, width), BF), whole((rows, 2 * hidden), F32), whole((rows, hidden), BF)]
    out = kernel_call(
        body,
        outs + part_shapes(seg, width),
        (*pieces, w_gu, w_d),
        flops=2 * rows * width * hidden * 3,
        limit=16,
        name="feed",
    )
    return out[:3], out[3:]


def feed_back(pieces, w_gu, w_d, gate_up):
    seg, width = pieces[0].shape[1:]
    rows = 16 * seg
    hidden = w_d.shape[1]

    def body(*refs):
        d_refs = [refs[i // 4].at[i % 4] for i in range(16)]
        wg_ref, wd_ref, gate_ref, dm_ref, dgu_ref, *part = refs[4:]
        for i in range(16):
            dm_ref[i * seg : (i + 1) * seg, :] = d_refs[i][...]
        for g in (3, 2, 1, 0):
            rs = slice(g * 4 * seg, (g + 1) * 4 * seg)
            dact = dot_nn(dm_ref[rs, :], wd_ref[...])
            gate, up = gate_ref[rs, :hidden], gate_ref[rs, hidden:]
            sigma = jax.nn.sigmoid(gate)
            dgate = dact * up * sigma * (1.0 + gate * (1.0 - sigma))
            dgu_ref[rs, :] = jnp.concatenate([dgate, dact * (gate * sigma)], axis=1).astype(BF)
        for g in (3, 2, 1, 0):
            rs = slice(g * 4 * seg, (g + 1) * 4 * seg)
            write_part(part, g, dot_nt(dgu_ref[rs, :], wg_ref[...]))

    outs = [whole((rows, width), BF), whole((rows, 2 * hidden), BF)]
    out = kernel_call(
        body,
        outs + part_shapes(seg, width),
        (*pieces, w_gu, w_d, gate_up),
        flops=2 * rows * width * hidden * 3,
        limit=16,
        name="feed_back",
    )
    return out[0], out[1], out[2:]


def down_grads(dm, act):
    rows, width = dm.shape
    hidden = act.shape[1]

    def body(dm_ref, act_ref, out_ref):
        quarter = width // 4
        for b in range(4):
            at = slice(b * quarter, (b + 1) * quarter)
            out_ref[at, :] = dot_tn(dm_ref[:, at], act_ref[...]).astype(BF)

    return kernel_call(
        body, whole((width, hidden), BF), (dm, act), flops=2 * rows * width * hidden, limit=16, name="down_grads"
    )


def feed_grads(place, down, h2, dgu, w_gu):
    rows, width = h2.shape
    hidden = down.shape[1] // 2
    cut = SECOND - 2 * hidden
    left = hidden - cut

    def body(place_ref, down_ref, h_ref, dgu_ref, w_ref, out_ref, rest_ref, tail_ref):
        y = place_ref[3]
        quarter = width // 4
        for b in range(4):
            at = slice(b * quarter, (b + 1) * quarter)
            g = dot_tn(h_ref[:, at], dgu_ref[...])
            tail_ref[at, :] = jnp.sum(g * w_ref[at, :].astype(F32), axis=1, keepdims=True)
            down = down_ref[at, :].astype(F32)
            rest_ref[at, :] = jnp.concatenate([down[:, cut:hidden], down[:, hidden + cut :]], axis=1).astype(BF)
            for h, index in enumerate((y, 1 - y)):
                parts = [
                    g[:, hidden * h : hidden * (h + 1)],
                    g[:, hidden * (2 + h) : hidden * (3 + h)],
                    down[:, hidden * h : hidden * h + cut],
                ]
                write_blocks(out_ref, index, b, jnp.concatenate(parts, axis=1))

    outs = [whole((2, 16, width // 16, SECOND), BF)] + [whole((width, 2 * left), BF), whole((width, 1), F32)]
    return kernel_call(
        body,
        outs,
        (place, down, h2, dgu, w_gu),
        scalars=1,
        flops=2 * rows * width * hidden * 4,
        limit=16,
        name="feed_grads",
    )


def norm_back(grad, rows, inverse, gain):
    normed = rows * inverse
    scaled = grad * gain
    return inverse * (scaled - normed * jnp.mean(scaled * normed, axis=-1, keepdims=True))


def rms_of(rows):
    return lax.rsqrt(jnp.mean(rows * rows, axis=-1, keepdims=True) + eps)


def rows_after_attention(terms, own, info):
    def body(*refs):
        *term_refs, own_ref, info_ref, resid_ref, h_ref = refs
        resid = own_ref[...].astype(F32) + total(term_refs)
        resid_ref[...] = resid
        h_ref[...] = (resid * rms_of(resid) * info_ref[1:2, :]).astype(BF)

    return kernel_call(
        body, [whole(own.shape, F32), whole(own.shape, BF)], (*terms, own, info), limit=16, name="after_attention"
    )


def rows_after_feed(terms, resid, valid, teacher, out_grad, factor):
    def body(*refs):
        *term_refs, resid_ref, ok_ref, teacher_ref, grad_ref, factor_ref = refs[:-4]
        out_ref, dout_ref, dm_ref, squares_ref = refs[-4:]
        out = resid_ref[...] + total(term_refs)
        out_ref[...] = out.astype(BF)
        ok = ok_ref[...]
        diff = out - teacher_ref[...].astype(F32)
        part = jnp.sum(ok * diff * diff, axis=0, keepdims=True)
        squares_ref[...] = jnp.broadcast_to(jnp.sum(part, axis=1, keepdims=True), squares_ref.shape)
        dout = ok * (grad_ref[...].astype(F32) + factor_ref[0:1, 0:1] * diff)
        dout_ref[...] = dout
        dm_ref[...] = dout.astype(BF)

    shape = resid.shape
    return kernel_call(
        body,
        [whole(shape, BF), whole(shape, F32), whole(shape, BF), whole((8, LANES), F32)],
        (*terms, resid, valid, teacher, out_grad, factor),
        limit=16,
        name="after_feed",
    )


def rows_after_feed_back(terms, resid, dout, info):
    def body(*refs):
        *term_refs, resid_ref, dout_ref, info_ref, dresid_ref, da_ref = refs
        resid = resid_ref[...]
        dresid = dout_ref[...] + norm_back(total(term_refs), resid, rms_of(resid), info_ref[1:2, :])
        dresid_ref[...] = dresid
        da_ref[...] = dresid.astype(BF)

    return kernel_call(
        body,
        [whole(resid.shape, F32), whole(resid.shape, BF)],
        (*terms, resid, dout, info),
        flops=10**11,
        limit=16,
        name="after_feed_back",
    )


def rows_at_end(terms, own, dresid, info):
    def body(*refs):
        *term_refs, own_ref, dresid_ref, info_ref, dx_ref = refs
        rows = own_ref[...].astype(F32)
        dx = dresid_ref[...] + norm_back(total(term_refs), rows, rms_of(rows), info_ref[0:1, :])
        dx_ref[...] = dx.astype(BF)

    return kernel_call(body, whole(own.shape, BF), (*terms, own, dresid, info), limit=16, name="at_end")


def layer(
    inputs,
    valid,
    out_grad,
    teacher,
    norm_attn,
    w_query,
    key_matrix,
    value_matrix,
    w_out,
    norm_mlp,
    w_gate,
    w_up,
    w_down,
):
    seqs, seg, width = inputs.shape
    y = lax.axis_index("tensor")
    k = lax.axis_index("context")
    z, x, c = k // 4, (k // 2) % 2, k % 2
    place = jnp.stack([z, x, c, y]).astype(jnp.int32)
    seq_len = 16 * seg
    first = y == 0

    def mine(a):
        return lax.dynamic_index_in_dim(a, y, 0, keepdims=False)

    own = mine(inputs)
    counts = jnp.sum(valid.astype(F32), axis=1).astype(BF)
    ones = jnp.ones_like(norm_attn)
    extra = jnp.stack([norm_attn, norm_mlp, ones * counts[0], ones * counts[1]], axis=1)
    hidden = w_gate.shape[1] // 16
    firsts = pack_first(w_query, key_matrix, value_matrix, w_out.T, extra, w_down.T)
    seconds = pack_second(w_gate, w_up, w_down.T)
    first_in = share_blocks(firsts)
    pieces, near, far = gather_rows(own)
    first_both = of_other(first_in)
    second_in = share_blocks(after(seconds, first_both, *near, *far))
    w_qkv, w_o, info = prepare_attention(place, first_in, first_both)
    lengths = jnp.sum(info[2:4], axis=1) / F32(width // 16)
    count = lengths[0] + lengths[1]
    length = jnp.full((8, LANES), jnp.where(first, lengths[0], lengths[1]), F32)
    factor = jnp.full((8, LANES), F32(seqs * seq_len) / count, F32)

    bit = jnp.arange(2, dtype=jnp.int32)
    pos = (
        jnp.arange(4, dtype=jnp.int32)[:, None, None, None] * (4 * seg)
        + (bit ^ x)[None, :, None, None] * (2 * seg)
        + (bit ^ c)[None, None, :, None] * seg
        + jnp.arange(seg, dtype=jnp.int32)[None, None, None, :]
    ).reshape(seq_len)
    half = HEAD_SIZE // 2
    freqs = jnp.exp(-math.log(theta) * jnp.arange(half, dtype=F32) / half)
    angles = pos.astype(F32)[:, None] * freqs[None, :]
    cos_half, sin_half = jnp.cos(angles), jnp.sin(angles)
    pad = jnp.zeros((seq_len, LANES - HEAD_SIZE), F32)
    cosine = jnp.concatenate([cos_half, cos_half, pad], axis=1)
    sine = jnp.concatenate([-sin_half, sin_half, pad], axis=1)
    kpos = pos[None, :]

    (h1, q, keys, values, ctx, lse), part = attention(
        place, pieces, w_qkv, w_o, info, length, kpos, cosine, sine
    )
    terms, far, come = scatter_rows(part)
    second_both = of_other(after(second_in, come[2]))
    resid, h2_own = rows_after_attention(terms, own, info)
    w_gu, w_d = prepare_feed(place, first_in, first_both, second_in, second_both, hidden)
    pieces, _, _ = gather_rows(h2_own, w_gu)
    (h2, gate_up, act), part = feed(pieces, w_gu, w_d)
    okf = mine(valid).astype(F32)[:, None]
    terms, _, _ = scatter_rows(part)
    out_own, dout, dm_own, squares = rows_after_feed(
        terms, resid, okf, mine(teacher), mine(out_grad), factor
    )
    pieces, _, _ = gather_rows(dm_own)
    dm, dgu, part = feed_back(pieces, w_gu, w_d, gate_up)
    terms, far, _ = scatter_rows(part)
    down = down_grads(after(dm, part[0]), act)
    shares, rest, tail2 = feed_grads(place, down, h2, after(dgu, *far), w_gu)
    summed = over_sequences(shares)
    dresid, da_own = rows_after_feed_back(terms, resid, dout, info)
    pieces, near, far = gather_rows(da_own)
    seconds = share_blocks(after(summed, *near))
    da, dqkv, part = attention_back(
        place, pieces, w_qkv, w_o, length, kpos, cosine, sine, q, keys, values, lse
    )
    terms, far, _ = scatter_rows(part)
    shares = attention_grads(place, h1, after(dqkv, *far), da, ctx, w_qkv, rest, tail2, squares)
    summed = over_sequences(after(shares, seconds))
    dx = rows_at_end(terms, own, dresid, info)
    firsts = share_blocks(after(summed, seconds, dx))
    grad_gate, grad_up = unpack_second(after(seconds, dx), hidden)
    both_out = move_y(out_own)
    both_dx = move_y(dx)
    output = jnp.stack([jnp.where(first, out_own, both_out), jnp.where(first, both_out, out_own)])
    input_grad = jnp.stack([jnp.where(first, dx, both_dx), jnp.where(first, both_dx, dx)]).astype(F32)
    grad_query, grad_key, grad_value, grad_out, grad_down, tails = unpack_first(firsts, seconds, hidden)
    return (
        output,
        tails[0, 2] / (count * width),
        input_grad,
        tails[:, 0] / norm_attn.astype(F32),
        tails[:, 1] / norm_mlp.astype(F32),
        grad_query,
        grad_key,
        grad_value,
        grad_out.T,
        grad_gate,
        grad_up,
        grad_down.T,
    )


def rms_forward(value_rows, gain):
    inverse = lax.rsqrt(jnp.mean(value_rows * value_rows, axis=-1, keepdims=True) + eps)
    normed = value_rows * inverse
    return (normed, inverse, normed * gain)


def rms_backward(grad, normed, inverse, gain):
    scaled = grad * gain
    return inverse * (scaled - normed * jnp.mean(scaled * normed, axis=-1, keepdims=True))


def rotate(value_rows, cosine, sine):
    half = value_rows.shape[-1] // 2
    first, second = (value_rows[..., :half], value_rows[..., half:])
    return jnp.concatenate(
        [first * cosine - second * sine, second * cosine + first * sine], axis=-1
    )


def rotate_back(grad, cosine, sine):
    half = grad.shape[-1] // 2
    first, second = (grad[..., :half], grad[..., half:])
    return jnp.concatenate(
        [first * cosine + second * sine, second * cosine - first * sine], axis=-1
    )


def allowed_pairs(key_ok, qpos, seq_len):
    kpos = jnp.arange(seq_len, dtype=jnp.int32)
    return (kpos[None, :] // BLOCK <= qpos[:, None] // BLOCK) & (key_ok[None, :] > 0)


def masked_scores(query_rows, key_rows, key_ok, qpos, scale):
    raw = (
        jnp.einsum("qkgd,jkd->kgqj", query_rows, key_rows, preferred_element_type=jnp.float32)
        * scale
    )
    allowed = allowed_pairs(key_ok, qpos, key_rows.shape[0])
    return jnp.where(allowed, raw, jnp.float32(-1e30))


def dot_left(left, right):
    return lax.dot_general(
        left, right, (((0,), (0,)), ((), ())), preferred_element_type=jnp.float32
    )


def dot_right(left, right):
    return lax.dot_general(
        left, right, (((1,), (1,)), ((), ())), preferred_element_type=jnp.float32
    )


def shards(
    inputs,
    valid,
    out_grad,
    teacher,
    norm_attn,
    w_query,
    key_matrix,
    value_matrix,
    w_out,
    norm_mlp,
    w_gate,
    w_up,
    w_down,
):
    seqs, seg, width = inputs.shape
    ctx_size = lax.axis_size("context")
    index = lax.axis_index("context")
    scale = HEAD_SIZE ** (-0.5)
    half = HEAD_SIZE // 2
    gathered = (
        lax.all_gather(norm_attn, "context", axis=0, tiled=True),
        lax.all_gather(w_query, "context", axis=0, tiled=True),
        lax.all_gather(key_matrix, "context", axis=0, tiled=True),
        lax.all_gather(value_matrix, "context", axis=0, tiled=True),
        lax.all_gather(w_out, "context", axis=1, tiled=True),
        lax.all_gather(norm_mlp, "context", axis=0, tiled=True),
        lax.all_gather(w_gate, "context", axis=0, tiled=True),
        lax.all_gather(w_up, "context", axis=0, tiled=True),
        lax.all_gather(w_down, "context", axis=1, tiled=True),
    )
    gain_first, wq, wk, wv, wo, gain_second, wg, wu, wd = gathered
    gain1 = gain_first.astype(jnp.float32)
    gain2 = gain_second.astype(jnp.float32)
    heads_q = wq.shape[1] // HEAD_SIZE
    heads_kv = wk.shape[1] // HEAD_SIZE
    head_group = heads_q // heads_kv
    row_count = seqs * seg
    positions = index * seg + jnp.arange(seg, dtype=jnp.int32)
    freqs = jnp.exp(-math.log(theta) * jnp.arange(half, dtype=jnp.float32) / half)
    angles = positions.astype(jnp.float32)[:, None] * freqs[None, :]
    cosine = jnp.cos(angles)[:, None, :]
    sine = jnp.sin(angles)[:, None, :]
    x = inputs.astype(jnp.float32)
    normed1, inverse1, pre1 = rms_forward(x, gain1)
    h1 = pre1.astype(jnp.bfloat16).reshape(row_count, width)
    query_before_rotary = jnp.dot(h1, wq, preferred_element_type=jnp.float32).reshape(
        seqs, seg, heads_q, HEAD_SIZE
    )
    key_before_rotary = jnp.dot(h1, wk, preferred_element_type=jnp.float32).reshape(
        seqs, seg, heads_kv, HEAD_SIZE
    )
    value_own = (
        jnp.dot(h1, wv, preferred_element_type=jnp.float32)
        .astype(jnp.bfloat16)
        .reshape(seqs, seg, heads_kv * HEAD_SIZE)
    )
    query_rows = (
        rotate(query_before_rotary, cosine, sine)
        .astype(jnp.bfloat16)
        .reshape(seqs, seg, heads_kv, head_group, HEAD_SIZE)
    )
    key_own = (
        rotate(key_before_rotary, cosine, sine)
        .astype(jnp.bfloat16)
        .reshape(seqs, seg, heads_kv * HEAD_SIZE)
    )
    keys_all, values_all, valid_all = (
        lax.all_gather(key_own, "context", axis=1, tiled=True),
        lax.all_gather(value_own, "context", axis=1, tiled=True),
        lax.all_gather(valid.astype(jnp.bfloat16), "context", axis=1, tiled=True),
    )
    seq_len = keys_all.shape[1]

    def attend(carry, items):
        qseq, kseq, vseq, okseq = items
        key_rows = kseq.reshape(seq_len, heads_kv, HEAD_SIZE)
        value_rows = vseq.reshape(seq_len, heads_kv, HEAD_SIZE)
        scores = masked_scores(qseq, key_rows, okseq, positions, scale)
        top = jnp.max(scores, axis=-1, keepdims=True)
        expo = jnp.exp(scores - top)
        total = jnp.sum(expo, axis=-1, keepdims=True)
        probr = (expo / total).astype(jnp.bfloat16)
        ctx = jnp.einsum("kgqj,jkd->qkgd", probr, value_rows, preferred_element_type=jnp.float32)
        lse = (top + jnp.log(total))[..., 0]
        return (carry, (ctx.astype(jnp.bfloat16).reshape(seg, heads_q * HEAD_SIZE), lse))

    carry, (context, lse_all) = lax.scan(
        attend, jnp.float32(0.0), (query_rows, keys_all, values_all, valid_all)
    )
    ctx_flat = context.reshape(row_count, heads_q * HEAD_SIZE)
    attn = lax.psum(
        jnp.dot(ctx_flat, wo, preferred_element_type=jnp.float32).astype(jnp.bfloat16), "tensor"
    ).astype(jnp.float32)
    resid = x + attn.reshape(seqs, seg, width)
    normed2, inverse2, pre2 = rms_forward(resid, gain2)
    h2 = pre2.astype(jnp.bfloat16).reshape(row_count, width)
    gate = jnp.dot(h2, wg, preferred_element_type=jnp.float32)
    up = jnp.dot(h2, wu, preferred_element_type=jnp.float32)
    sigma = jax.nn.sigmoid(gate)
    silu = gate * sigma
    act = (silu * up).astype(jnp.bfloat16)
    mixed = lax.psum(
        jnp.dot(act, wd, preferred_element_type=jnp.float32).astype(jnp.bfloat16), "tensor"
    ).astype(jnp.float32)
    out = resid + mixed.reshape(seqs, seg, width)
    output = out.astype(jnp.bfloat16)
    validf = valid.astype(jnp.float32)[..., None]
    diff = out - teacher.astype(jnp.float32)
    count, squares = lax.psum(
        (jnp.sum(valid.astype(jnp.float32)), jnp.sum(validf * diff * diff)), "context"
    )
    loss = squares / (count * width)
    dout = validf * (
        out_grad.astype(jnp.float32) + jnp.float32(seqs * seg * ctx_size) / count * diff
    )
    dm = dout.astype(jnp.bfloat16).reshape(row_count, width)
    grad_down = dot_left(act, dm)
    dact = dot_right(dm, wd)
    dgate = (dact * up * sigma * (1.0 + gate * (1.0 - sigma))).astype(jnp.bfloat16)
    dup = (dact * silu).astype(jnp.bfloat16)
    grad_gate = dot_left(h2, dgate)
    grad_up = dot_left(h2, dup)
    dh2 = (
        lax.psum((dot_right(dgate, wg) + dot_right(dup, wu)).astype(jnp.bfloat16), "tensor")
        .astype(jnp.float32)
        .reshape(seqs, seg, width)
    )
    grad_gain2 = jnp.sum(dh2 * normed2, axis=(0, 1))
    dresid = dout + rms_backward(dh2, normed2, inverse2, gain2)
    dattn = dresid.astype(jnp.bfloat16).reshape(row_count, width)
    grad_out = dot_left(ctx_flat, dattn)
    dctx = (
        dot_right(dattn, wo)
        .astype(jnp.bfloat16)
        .reshape(seqs, seg, heads_kv, head_group, HEAD_SIZE)
    )

    def attend_back(carry, items):
        qseq, kseq, vseq, okseq, lseq, dseq = items
        allowed = allowed_pairs(okseq, positions, seq_len)

        def head_back(parts):
            qhead, khead, vhead, dhead, lhead = parts
            raw = (
                jnp.einsum("qgd,jd->gqj", qhead, khead, preferred_element_type=jnp.float32) * scale
            )
            scores = jnp.where(allowed[None], raw, jnp.float32(-1e30))
            prob = jnp.exp(scores - lhead[..., None])
            probr = prob.astype(jnp.bfloat16)
            dprob = jnp.einsum("qgd,jd->gqj", dhead, vhead, preferred_element_type=jnp.float32)
            delta = jnp.sum(prob * dprob, axis=-1, keepdims=True)
            dscore = (prob * (dprob - delta)).astype(jnp.bfloat16)
            dq = (
                jnp.einsum("gqj,jd->qgd", dscore, khead, preferred_element_type=jnp.float32) * scale
            )
            dk = (
                jnp.einsum("gqj,qgd->jd", dscore, qhead, preferred_element_type=jnp.float32) * scale
            )
            dv = jnp.einsum("gqj,qgd->jd", probr, dhead, preferred_element_type=jnp.float32)
            return (dq, dk, dv)

        heads_in = (
            jnp.moveaxis(qseq, 1, 0),
            jnp.moveaxis(kseq.reshape(seq_len, heads_kv, HEAD_SIZE), 1, 0),
            jnp.moveaxis(vseq.reshape(seq_len, heads_kv, HEAD_SIZE), 1, 0),
            jnp.moveaxis(dseq, 1, 0),
            lseq,
        )
        dq_heads, dk_heads, dv_heads = lax.map(head_back, heads_in)
        dq = jnp.moveaxis(dq_heads, 0, 1)
        dk = jnp.moveaxis(dk_heads, 0, 1).reshape(seq_len, heads_kv * HEAD_SIZE)
        dv = jnp.moveaxis(dv_heads, 0, 1).reshape(seq_len, heads_kv * HEAD_SIZE)
        dk_own, dv_own = (
            lax.psum_scatter(dk, "context", scatter_dimension=0, tiled=True),
            lax.psum_scatter(dv, "context", scatter_dimension=0, tiled=True),
        )
        return (carry, (dq, dk_own, dv_own))

    carry, (dq_all, dk_all, dv_all) = lax.scan(
        attend_back, jnp.float32(0.0), (query_rows, keys_all, values_all, valid_all, lse_all, dctx)
    )
    dqpre = (
        rotate_back(dq_all.reshape(seqs, seg, heads_q, HEAD_SIZE), cosine, sine)
        .astype(jnp.bfloat16)
        .reshape(row_count, heads_q * HEAD_SIZE)
    )
    dkpre = (
        rotate_back(dk_all.reshape(seqs, seg, heads_kv, HEAD_SIZE), cosine, sine)
        .astype(jnp.bfloat16)
        .reshape(row_count, heads_kv * HEAD_SIZE)
    )
    dvr = dv_all.astype(jnp.bfloat16).reshape(row_count, heads_kv * HEAD_SIZE)
    grad_query = dot_left(h1, dqpre)
    grad_key = dot_left(h1, dkpre)
    grad_value = dot_left(h1, dvr)
    dh1 = (
        lax.psum(
            (dot_right(dqpre, wq) + dot_right(dkpre, wk) + dot_right(dvr, wv)).astype(jnp.bfloat16),
            "tensor",
        )
        .astype(jnp.float32)
        .reshape(seqs, seg, width)
    )
    grad_gain1 = jnp.sum(dh1 * normed1, axis=(0, 1))
    input_grad = dresid + rms_backward(dh1, normed1, inverse1, gain1)
    summed = (
        lax.psum_scatter(grad_gain1, "context", scatter_dimension=0, tiled=True),
        lax.psum_scatter(grad_query, "context", scatter_dimension=0, tiled=True),
        lax.psum_scatter(grad_key, "context", scatter_dimension=0, tiled=True),
        lax.psum_scatter(grad_value, "context", scatter_dimension=0, tiled=True),
        lax.psum_scatter(grad_out, "context", scatter_dimension=1, tiled=True),
        lax.psum_scatter(grad_gain2, "context", scatter_dimension=0, tiled=True),
        lax.psum_scatter(grad_gate, "context", scatter_dimension=0, tiled=True),
        lax.psum_scatter(grad_up, "context", scatter_dimension=0, tiled=True),
        lax.psum_scatter(grad_down, "context", scatter_dimension=1, tiled=True),
    )
    (
        grad_gain1,
        grad_query,
        grad_key,
        grad_value,
        grad_out,
        grad_gain2,
        grad_gate,
        grad_up,
        grad_down,
    ) = summed
    return (
        output,
        loss,
        input_grad,
        grad_gain1,
        grad_gain2,
        grad_query,
        grad_key,
        grad_value,
        grad_out,
        grad_gate,
        grad_up,
        grad_down,
    )


def solution(mesh):
    in_specs = (
        P(None, "context", None),
        P(None, "context"),
        P(None, "context", None),
        P(None, "context", None),
        P("context"),
        P("context", "tensor"),
        P("context", "tensor"),
        P("context", "tensor"),
        P("tensor", "context"),
        P("context"),
        P("context", "tensor"),
        P("context", "tensor"),
        P("tensor", "context"),
    )
    out_specs = (
        P(None, "context", None),
        P(),
        P(None, "context", None),
        P("context"),
        P("context"),
        P("context", "tensor"),
        P("context", "tensor"),
        P("context", "tensor"),
        P("tensor", "context"),
        P("context", "tensor"),
        P("context", "tensor"),
        P("tensor", "context"),
    )
    fits = dict(mesh.shape) == {"tensor": 2, "context": 16}
    return jax.shard_map(
        layer if fits else shards, mesh=mesh, in_specs=in_specs, out_specs=out_specs, check_vma=False
    )
```

```python
import functools
import math

import jax
import jax.numpy as jnp
from jax import lax
from jax.experimental import pallas as pl
from jax.experimental.pallas import tpu as pltpu
from jax.sharding import PartitionSpec as P

HEAD_SIZE = 80
BLOCK = 256
LANES = 128

eps = 1e-05
theta = 10000.0
BF = jnp.bfloat16
F32 = jnp.float32
MIB = 1024 * 1024
SLOW = ()


def whole(shape, dtype):
    return jax.ShapeDtypeStruct(tuple(shape), dtype)


def kernel_call(body, outs, ins, scalars=0, far=(), flops=0, scratch=(), limit=16, name=None):
    single = not isinstance(outs, (list, tuple))
    spec = lambda i: (
        pl.BlockSpec(memory_space=pltpu.SMEM)
        if i < scalars
        else pl.BlockSpec(memory_space=pl.ANY)
        if i in far
        else pl.BlockSpec(memory_space=pltpu.VMEM)
    )
    out_spec = pl.BlockSpec(memory_space=pltpu.VMEM)
    nbytes = sum(math.prod(a.shape) * a.dtype.itemsize for a in ins)
    nbytes += sum(math.prod(o.shape) * o.dtype.itemsize for o in ([outs] if single else outs))
    return pl.pallas_call(
        body,
        out_shape=outs,
        in_specs=[spec(i) for i in range(len(ins))],
        out_specs=out_spec if single else [out_spec] * len(outs),
        scratch_shapes=list(scratch),
        compiler_params=pltpu.CompilerParams(vmem_limit_bytes=limit * MIB),
        cost_estimate=pl.CostEstimate(flops=flops if name in SLOW else 0, bytes_accessed=0, transcendentals=0),
        name=name,
    )(*ins)


def dot_nn(a, b):
    return lax.dot_general(a, b, (((1,), (0,)), ((), ())), preferred_element_type=F32)


def dot_nt(a, b):
    return lax.dot_general(a, b, (((1,), (1,)), ((), ())), preferred_element_type=F32)


def dot_tn(a, b):
    return lax.dot_general(a, b, (((0,), (0,)), ((), ())), preferred_element_type=F32)


def move_c(a):
    return lax.ppermute(a, "context", [(k, k ^ 1) for k in range(16)])


def move_x(a):
    return lax.ppermute(a, "context", [(k, k ^ 2) for k in range(16)])


def move_z(a, step):
    return lax.ppermute(a, "context", [(k, (k + 4 * step) % 16) for k in range(16)])


def move_y(a):
    return lax.ppermute(a, "tensor", [(0, 1), (1, 0)])


def share_out(a):
    return lax.all_to_all(a, "context", split_axis=0, concat_axis=0, tiled=True)


def after(value, *others):
    return lax.optimization_barrier((value, *others))[0]


def stack(pieces):
    def body(*refs):
        for m in range(4):
            refs[4][m] = refs[m][...]

    return kernel_call(body, whole((4, *pieces[0].shape), BF), tuple(pieces), limit=8, name="stack")


def gather_rows(own, *late, early=()):
    near = [own] + [move_z(own, m) for m in (1, 2, 3)]
    far = [move_x(own)]
    far += [move_x(after(near[1], far[0], *early)), None, move_x(after(near[3], far[0], *early))]
    far[2] = move_x(after(near[2], far[1], far[3]))
    near_all, far_all = stack(near), stack(far)
    last = after(far_all, *late) if late else far_all
    return (near_all, move_c(near_all), far_all, move_c(last)), near, far


def scatter_rows(part, *late):
    far1, far0, near1, *near0 = part
    shape = far1.shape[1:]

    def add_far(a_ref, b_ref, *outs):
        for m in range(4):
            outs[m][...] = (a_ref[m].astype(F32) + b_ref[m].astype(F32)).astype(BF)

    def add_near(a_ref, b_ref, c_ref, out_ref):
        out_ref[...] = (a_ref[...].astype(F32) + b_ref[...].astype(F32) + c_ref[...].astype(F32)).astype(BF)

    far = kernel_call(add_far, [whole(shape, BF)] * 4, (far0, move_c(far1)), limit=16, name="add_far")
    near1 = move_c(near1)
    come = {m: move_x(far[m]) for m in (2, 1, 3, 0)}
    if late:
        come[2] = after(come[2], *late)
    terms = [near0[0], near1[0], come[0]]
    for m in (2, 1, 3):
        s = kernel_call(add_near, whole(shape, BF), (near0[m], near1[m], come[m]), limit=8, name="add_near")
        terms.append(move_z(s, 4 - m))
    return terms, far, come


def part_shapes(seg, width):
    return [
        whole((4, seg, width), BF),
        whole((4, seg, width), BF),
        whole((4, seg, width), BF),
    ] + [whole((seg, width), BF)] * 4


def write_part(outs, group, value):
    far1, far0, near1, *near0 = outs
    seg = far1.shape[1]
    for m in range(4):
        rows = value[m * seg : (m + 1) * seg]
        if group == 3:
            far1[m] = rows.astype(BF)
        elif group == 2:
            far0[m] = rows.astype(BF)
        elif group == 1:
            near1[m] = rows.astype(BF)
        else:
            near0[m][...] = rows.astype(BF)


def total(refs):
    out = refs[0][...].astype(F32)
    for r in refs[1:]:
        out = out + r[...].astype(F32)
    return out


FIRST = 384
SECOND = 640
EXTRA = 4


def pack_first(wq, wk, wv, wot, extra, wdt):
    rows, d = wq.shape[0], HEAD_SIZE
    hidden = wdt.shape[1] // 16
    some = FIRST - 4 * d - EXTRA

    def body(q_ref, k_ref, v_ref, o_ref, e_ref, d_ref, out_ref):
        for k in range(16):
            block = jnp.concatenate(
                [
                    q_ref[:, k * d : (k + 1) * d],
                    k_ref[:, k // 4 * d : (k // 4 + 1) * d],
                    v_ref[:, k // 4 * d : (k // 4 + 1) * d],
                    o_ref[:, k * d : (k + 1) * d],
                    e_ref[...],
                    d_ref[:, k * hidden : k * hidden + some],
                ],
                axis=1,
            )
            out_ref[k] = block

    return kernel_call(
        body, whole((16, rows, FIRST), BF), (wq, wk, wv, wot, extra, wdt), limit=16, name="pack_first"
    )


def pack_second(wg, wu, wdt):
    rows = wg.shape[0]
    hidden = wg.shape[1] // 16
    some = FIRST - 4 * HEAD_SIZE - EXTRA
    spare = SECOND - 3 * hidden + some

    def body(g_ref, u_ref, d_ref, out_ref):
        for k in range(16):
            block = jnp.concatenate(
                [
                    d_ref[:, k * hidden + some : (k + 1) * hidden],
                    g_ref[:, k * hidden : (k + 1) * hidden],
                    u_ref[:, k * hidden : (k + 1) * hidden],
                    jnp.zeros((rows, spare), BF),
                ],
                axis=1,
            )
            out_ref[k] = block

    return kernel_call(body, whole((16, rows, SECOND), BF), (wg, wu, wdt), limit=16, name="pack_second")


def share_blocks(a):
    return share_out(a.reshape(-1, a.shape[2])).reshape(a.shape)


def of_other(a):
    return lax.all_gather(a, "tensor", axis=0, tiled=False)


def over_sequences(parts):
    return lax.psum_scatter(parts, "tensor", scatter_dimension=0, tiled=False)


def unpack_second(second, hidden):
    rows = second.shape[1]

    def body(s_ref, g_ref, u_ref):
        for k in range(16):
            c = s_ref[k].astype(F32)
            g_ref[:, k * hidden : (k + 1) * hidden] = c[:, :hidden]
            u_ref[:, k * hidden : (k + 1) * hidden] = c[:, hidden : 2 * hidden]

    return kernel_call(body, [whole((rows, 16 * hidden), F32)] * 2, (second,), limit=16, name="unpack_second")


def unpack_first(first, second, hidden):
    rows, d = first.shape[1], HEAD_SIZE
    cut = SECOND - 2 * hidden
    rest = 4 * d + hidden - cut

    def body(f_ref, s_ref, q_ref, k_ref, v_ref, o_ref, d_ref, tail_ref):
        tail = jnp.zeros((rows, 3), F32)
        for k in range(16):
            b = f_ref[k].astype(F32)
            q_ref[:, k * d : (k + 1) * d] = b[:, :d]
            o_ref[:, k * d : (k + 1) * d] = b[:, 3 * d : 4 * d]
            if k % 4 == 0:
                keys = jnp.zeros((rows, 2 * d), F32)
            keys = keys + b[:, d : 3 * d]
            if k % 4 == 3:
                k_ref[:, k // 4 * d : (k // 4 + 1) * d] = keys[:, :d]
                v_ref[:, k // 4 * d : (k // 4 + 1) * d] = keys[:, d:]
            tail = tail + b[:, rest : rest + 3]
            d_ref[:, k * hidden : k * hidden + cut] = s_ref[k][:, 2 * hidden :].astype(F32)
            d_ref[:, k * hidden + cut : (k + 1) * hidden] = b[:, 4 * d : rest]
        tail_ref[...] = tail

    outs = [whole((rows, w), F32) for w in (16 * d, 4 * d, 4 * d, 16 * d, 16 * hidden, 3)]
    return kernel_call(body, outs, (first, second), limit=16, name="unpack_first")


def prepare_attention(place, mine, both):
    size, d = mine.shape[1], HEAD_SIZE
    depth = 16 * size

    def body(place_ref, mine_ref, both_ref, w_ref, out_ref, row_ref, info_ref):
        other_ref = both_ref.at[1 - place_ref[3]]
        info_ref[...] = jnp.zeros_like(info_ref)
        for k in range(16):
            rs = slice(k * size, (k + 1) * size)
            parts = [mine_ref[k], other_ref[k]]
            w_ref[rs, :] = jnp.concatenate([p[:, : 3 * d] for p in parts], axis=1)
            out_ref[rs, :] = jnp.concatenate([p[:, 3 * d : 4 * d] for p in parts], axis=1)
            info_ref[rs, :EXTRA] = parts[0][:, 4 * d : 4 * d + EXTRA].astype(F32)
        for b in range(depth // LANES):
            rs = slice(b * LANES, (b + 1) * LANES)
            row_ref[:, rs] = info_ref[rs, :].T[0:8, :]

    return kernel_call(
        body,
        [whole((depth, 6 * d), BF), whole((depth, 2 * d), BF), whole((8, depth), F32)],
        (place, mine, both),
        scalars=1,
        scratch=[pltpu.VMEM((depth, LANES), F32)],
        limit=16,
        name="prepare_attention",
    )


def prepare_feed(place, first_mine, first_both, mine, both, hidden):
    size = mine.shape[1]
    depth = 16 * size
    at = 4 * HEAD_SIZE + EXTRA
    rest = hidden - (FIRST - at)

    def body(place_ref, fm_ref, fboth_ref, m_ref, both_ref, gu_ref, d_ref):
        fo_ref, o_ref = fboth_ref.at[1 - place_ref[3]], both_ref.at[1 - place_ref[3]]
        for k in range(16):
            rs = slice(k * size, (k + 1) * size)
            fm, fo, m, o = fm_ref[k], fo_ref[k], m_ref[k], o_ref[k]
            gu_ref[rs, :] = jnp.concatenate(
                [
                    m[:, rest : rest + hidden],
                    o[:, rest : rest + hidden],
                    m[:, rest + hidden : rest + 2 * hidden],
                    o[:, rest + hidden : rest + 2 * hidden],
                ],
                axis=1,
            )
            d_ref[rs, :] = jnp.concatenate([fm[:, at:], m[:, :rest], fo[:, at:], o[:, :rest]], axis=1)

    return kernel_call(
        body,
        [whole((depth, 4 * hidden), BF), whole((depth, 2 * hidden), BF)],
        (place, first_mine, first_both, mine, both),
        scalars=1,
        limit=16,
        name="prepare_feed",
    )


def turn(a, cosine, sine):
    half = HEAD_SIZE // 2
    lane = lax.broadcasted_iota(jnp.int32, a.shape, 1)
    swapped = jnp.where(lane < half, pltpu.roll(a, LANES - half, 1), pltpu.roll(a, half, 1))
    return a * cosine + swapped * sine


def head_of(value, at):
    part = value[:, at * HEAD_SIZE : (at + 1) * HEAD_SIZE]
    return jnp.concatenate([part, jnp.zeros((value.shape[0], LANES - HEAD_SIZE), value.dtype)], axis=1)


def attention(place, pieces, weights, w_o, rows_info, length, kpos, cosine, sine):
    seg, width = pieces[0].shape[1:]
    rows = 16 * seg
    blocks = rows // BLOCK
    scale = HEAD_SIZE ** (-0.5)

    def body(place_ref, *refs):
        x_refs = [refs[i // 4].at[i % 4] for i in range(16)]
        w_ref, wo_ref, info_ref, len_ref, kpos_ref, cos_ref, sin_ref = refs[4:11]
        h_ref, q_ref, k_ref, v_ref, ctx_ref, lse_ref, *part = refs[11:]
        z = place_ref[0]
        gain = info_ref[0:1, :]
        length = len_ref[0:1, 0:1]
        for i in range(16):

            @pl.loop(0, seg // 16)
            def _(r):
                at = pl.multiple_of(r * 16, 16)
                xs = x_refs[i][pl.ds(at, 16), :].astype(F32)
                inv = lax.rsqrt(jnp.mean(xs * xs, axis=-1, keepdims=True) + eps)
                h_ref[pl.ds(i * seg + at, 16), :] = (xs * inv * gain).astype(BF)

        for g in range(4):
            qkv = dot_nn(h_ref[g * 4 * seg : (g + 1) * 4 * seg, :], w_ref[...])
            for m in range(4):
                to = pl.multiple_of(lax.rem(z - m + 4, 4) * BLOCK + g * seg, seg)
                to = pl.ds(to, seg)
                piece = qkv[m * seg : (m + 1) * seg]
                cosine, sine = cos_ref[to, :], sin_ref[to, :]
                for h in range(2):
                    q_ref[h, to, :] = turn(head_of(piece, 3 * h), cosine, sine).astype(BF)
                    k_ref[h, to, :] = turn(head_of(piece, 3 * h + 1), cosine, sine).astype(BF)
                    v_ref[h, to, :] = head_of(piece, 3 * h + 2).astype(BF)
        for i in range(blocks):
            m = lax.rem(z - i + 4, 4)
            n = (i + 1) * BLOCK
            ok = kpos_ref[:, :n].astype(F32) < length
            for h in range(2):
                s = dot_nt(q_ref[h, i * BLOCK : n, :], k_ref[h, :n, :]) * scale
                s = jnp.where(ok, s, F32(-1e30))
                top = jnp.max(s, axis=1, keepdims=True)
                e = jnp.exp(s - top)
                tot = jnp.sum(e, axis=1, keepdims=True)
                ctx = dot_nn((e / tot).astype(BF), v_ref[h, :n, :]).astype(BF)
                for g in range(4):
                    to = pl.ds(pl.multiple_of((g * 4 + m) * seg, seg), seg)
                    ctx_ref[to, h * HEAD_SIZE : (h + 1) * HEAD_SIZE] = ctx[g * seg : (g + 1) * seg, :HEAD_SIZE]
                lse_ref[h, i * BLOCK : n, :] = top + jnp.log(tot)
        for g in (3, 2, 1, 0):
            write_part(part, g, dot_nt(ctx_ref[g * 4 * seg : (g + 1) * 4 * seg, :], wo_ref[...]))

    outs = [
        whole((rows, width), BF),
        whole((2, rows, LANES), BF),
        whole((2, rows, LANES), BF),
        whole((2, rows, LANES), BF),
        whole((rows, 2 * HEAD_SIZE), BF),
        whole((2, rows, 1), F32),
    ] + part_shapes(seg, width)
    flops = 2 * rows * width * 6 * LANES + 2 * rows * rows * LANES * 2 * 2
    out = kernel_call(
        body,
        outs,
        (place, *pieces, weights, w_o, rows_info, length, kpos, cosine, sine),
        scalars=1,
        flops=flops,
        name="attention",
    )
    return out[:6], out[6:]


def attention_back(place, pieces, weights, w_o, length, kpos, cosine, sine, q, k, v, lse):
    seg, width = pieces[0].shape[1:]
    rows = 16 * seg
    blocks = rows // BLOCK
    scale = HEAD_SIZE ** (-0.5)

    def body(place_ref, *refs):
        d_refs = [refs[i // 4].at[i % 4] for i in range(16)]
        w_ref, wo_ref, len_ref, kpos_ref, cos_ref, sin_ref, q_ref, k_ref, v_ref, lse_ref = refs[4:14]
        da_ref, dqkv_ref, *part = refs[14:23]
        dctx_ref, dk_ref, dv_ref = refs[23:]
        z = place_ref[0]
        length = len_ref[0:1, 0:1]
        for i in range(16):
            da_ref[i * seg : (i + 1) * seg, :] = d_refs[i][...]
        for g in range(4):
            dctx = dot_nn(da_ref[g * 4 * seg : (g + 1) * 4 * seg, :], wo_ref[...])
            for m in range(4):
                to = pl.multiple_of(lax.rem(z - m + 4, 4) * BLOCK + g * seg, seg)
                for h in range(2):
                    dctx_ref[h, pl.ds(to, seg), :] = head_of(dctx[m * seg : (m + 1) * seg], h).astype(BF)
        dk_ref[...] = jnp.zeros_like(dk_ref)
        dv_ref[...] = jnp.zeros_like(dv_ref)

        def put(i, at, value):
            m = lax.rem(z - i + 4, 4)
            for g in range(4):
                to = pl.ds(pl.multiple_of((g * 4 + m) * seg, seg), seg)
                dqkv_ref[to, at * HEAD_SIZE : (at + 1) * HEAD_SIZE] = value[g * seg : (g + 1) * seg, :HEAD_SIZE]

        for i in range(blocks):
            n = (i + 1) * BLOCK
            ok = kpos_ref[:, :n].astype(F32) < length
            cosine, sine = cos_ref[i * BLOCK : n, :], sin_ref[i * BLOCK : n, :]
            for h in range(2):
                qi = q_ref[h, i * BLOCK : n, :]
                di = dctx_ref[h, i * BLOCK : n, :]
                s = dot_nt(qi, k_ref[h, :n, :]) * scale
                p = jnp.where(ok, jnp.exp(s - lse_ref[h, i * BLOCK : n, :]), F32(0.0))
                dp = dot_nt(di, v_ref[h, :n, :])
                delta = jnp.sum(p * dp, axis=1, keepdims=True)
                ds = (p * (dp - delta)).astype(BF)
                dq = dot_nn(ds, k_ref[h, :n, :]) * scale
                put(i, 3 * h, turn(dq, cosine, -sine).astype(BF))
                dk_ref[h, :n, :] += dot_tn(ds, qi)
                dv_ref[h, :n, :] += dot_tn(p.astype(BF), di)
        for i in range(blocks):
            rs = slice(i * BLOCK, (i + 1) * BLOCK)
            for h in range(2):
                dk = turn(dk_ref[h, rs, :] * scale, cos_ref[rs, :], -sin_ref[rs, :])
                put(i, 3 * h + 1, dk.astype(BF))
                put(i, 3 * h + 2, dv_ref[h, rs, :].astype(BF))
        for g in (3, 2, 1, 0):
            write_part(part, g, dot_nt(dqkv_ref[g * 4 * seg : (g + 1) * 4 * seg, :], w_ref[...]))

    outs = [whole((rows, width), BF), whole((rows, 6 * HEAD_SIZE), BF)] + part_shapes(seg, width)
    flops = 2 * rows * width * 6 * LANES + 2 * rows * rows * LANES * 2 * 5
    out = kernel_call(
        body,
        outs,
        (place, *pieces, weights, w_o, length, kpos, cosine, sine, q, k, v, lse),
        scalars=1,
        flops=flops,
        scratch=[
            pltpu.VMEM((2, rows, LANES), BF),
            pltpu.VMEM((2, rows, LANES), F32),
            pltpu.VMEM((2, rows, LANES), F32),
        ],
        name="attention_back",
    )
    return out[0], out[1], out[2:]


def write_blocks(out_ref, index, chunk, value):
    rows = out_ref.shape[2]
    for k in range(4):
        out_ref[index, chunk * 4 + k] = value[k * rows : (k + 1) * rows].astype(BF)


def attention_grads(place, h1, dqkv, da, ctx, weights, rest, tail2, squares):
    rows, width = h1.shape
    d, cut = HEAD_SIZE, rest.shape[1] // 2
    spare = FIRST - 4 * d - cut - 3

    def body(place_ref, h_ref, dqkv_ref, da_ref, ctx_ref, w_ref, rest_ref, tail_ref, sq_ref, out_ref):
        y = place_ref[3]
        quarter = width // 4
        for b in range(4):
            at = slice(b * quarter, (b + 1) * quarter)
            g = dot_tn(h_ref[:, at], dqkv_ref[...])
            tail1 = jnp.sum(g * w_ref[at, :].astype(F32), axis=1, keepdims=True)
            o = dot_tn(da_ref[:, at], ctx_ref[...])
            sq = jnp.broadcast_to(sq_ref[0:1, 0:1], (quarter, 1))
            last = [tail1, tail_ref[at, :], sq, jnp.zeros((quarter, spare), F32)]
            for h, index in enumerate((y, 1 - y)):
                parts = [g[:, 3 * d * h : 3 * d * (h + 1)], o[:, d * h : d * (h + 1)]]
                parts += [rest_ref[at, cut * h : cut * (h + 1)].astype(F32)]
                write_blocks(out_ref, index, b, jnp.concatenate(parts + last, axis=1))

    return kernel_call(
        body,
        whole((2, 16, width // 16, FIRST), BF),
        (place, h1, dqkv, da, ctx, weights, rest, tail2, squares),
        scalars=1,
        flops=2 * rows * width * 8 * d,
        name="attention_grads",
    )


def feed(pieces, w_gu, w_d):
    seg, width = pieces[0].shape[1:]
    rows = 16 * seg
    hidden = w_d.shape[1]

    def body(*refs):
        h_refs = [refs[i // 4].at[i % 4] for i in range(16)]
        wg_ref, wd_ref, h_ref, gate_ref, act_ref, *part = refs[4:]
        for i in range(16):
            h_ref[i * seg : (i + 1) * seg, :] = h_refs[i][...]
        for g in range(4):
            rs = slice(g * 4 * seg, (g + 1) * 4 * seg)
            both = dot_nn(h_ref[rs, :], wg_ref[...])
            gate_ref[rs, :] = both
            gate, up = both[:, :hidden], both[:, hidden:]
            act_ref[rs, :] = (gate * jax.nn.sigmoid(gate) * up).astype(BF)
        for g in (3, 2, 1, 0):
            rs = slice(g * 4 * seg, (g + 1) * 4 * seg)
            write_part(part, g, dot_nt(act_ref[rs, :], wd_ref[...]))

    outs = [whole((rows, width), BF), whole((rows, 2 * hidden), F32), whole((rows, hidden), BF)]
    out = kernel_call(
        body,
        outs + part_shapes(seg, width),
        (*pieces, w_gu, w_d),
        flops=2 * rows * width * hidden * 3,
        limit=16,
        name="feed",
    )
    return out[:3], out[3:]


def feed_back(pieces, w_gu, w_d, gate_up):
    seg, width = pieces[0].shape[1:]
    rows = 16 * seg
    hidden = w_d.shape[1]

    def body(*refs):
        d_refs = [refs[i // 4].at[i % 4] for i in range(16)]
        wg_ref, wd_ref, gate_ref, dm_ref, dgu_ref, *part = refs[4:]
        for i in range(16):
            dm_ref[i * seg : (i + 1) * seg, :] = d_refs[i][...]
        for g in (3, 2, 1, 0):
            rs = slice(g * 4 * seg, (g + 1) * 4 * seg)
            dact = dot_nn(dm_ref[rs, :], wd_ref[...])
            gate, up = gate_ref[rs, :hidden], gate_ref[rs, hidden:]
            sigma = jax.nn.sigmoid(gate)
            dgate = dact * up * sigma * (1.0 + gate * (1.0 - sigma))
            dgu_ref[rs, :] = jnp.concatenate([dgate, dact * (gate * sigma)], axis=1).astype(BF)
        for g in (3, 2, 1, 0):
            rs = slice(g * 4 * seg, (g + 1) * 4 * seg)
            write_part(part, g, dot_nt(dgu_ref[rs, :], wg_ref[...]))

    outs = [whole((rows, width), BF), whole((rows, 2 * hidden), BF)]
    out = kernel_call(
        body,
        outs + part_shapes(seg, width),
        (*pieces, w_gu, w_d, gate_up),
        flops=2 * rows * width * hidden * 3,
        limit=16,
        name="feed_back",
    )
    return out[0], out[1], out[2:]


def down_grads(dm, act):
    rows, width = dm.shape
    hidden = act.shape[1]

    def body(dm_ref, act_ref, out_ref):
        quarter = width // 4
        for b in range(4):
            at = slice(b * quarter, (b + 1) * quarter)
            out_ref[at, :] = dot_tn(dm_ref[:, at], act_ref[...]).astype(BF)

    return kernel_call(
        body, whole((width, hidden), BF), (dm, act), flops=2 * rows * width * hidden, limit=16, name="down_grads"
    )


def feed_grads(place, down, h2, dgu, w_gu):
    rows, width = h2.shape
    hidden = down.shape[1] // 2
    cut = SECOND - 2 * hidden
    left = hidden - cut

    def body(place_ref, down_ref, h_ref, dgu_ref, w_ref, out_ref, rest_ref, tail_ref):
        y = place_ref[3]
        quarter = width // 4
        for b in range(4):
            at = slice(b * quarter, (b + 1) * quarter)
            g = dot_tn(h_ref[:, at], dgu_ref[...])
            tail_ref[at, :] = jnp.sum(g * w_ref[at, :].astype(F32), axis=1, keepdims=True)
            down = down_ref[at, :].astype(F32)
            rest_ref[at, :] = jnp.concatenate([down[:, cut:hidden], down[:, hidden + cut :]], axis=1).astype(BF)
            for h, index in enumerate((y, 1 - y)):
                parts = [
                    g[:, hidden * h : hidden * (h + 1)],
                    g[:, hidden * (2 + h) : hidden * (3 + h)],
                    down[:, hidden * h : hidden * h + cut],
                ]
                write_blocks(out_ref, index, b, jnp.concatenate(parts, axis=1))

    outs = [whole((2, 16, width // 16, SECOND), BF)] + [whole((width, 2 * left), BF), whole((width, 1), F32)]
    return kernel_call(
        body,
        outs,
        (place, down, h2, dgu, w_gu),
        scalars=1,
        flops=2 * rows * width * hidden * 4,
        limit=16,
        name="feed_grads",
    )


def norm_back(grad, rows, inverse, gain):
    normed = rows * inverse
    scaled = grad * gain
    return inverse * (scaled - normed * jnp.mean(scaled * normed, axis=-1, keepdims=True))


def rms_of(rows):
    return lax.rsqrt(jnp.mean(rows * rows, axis=-1, keepdims=True) + eps)


def rows_after_attention(terms, own, info):
    def body(*refs):
        *term_refs, own_ref, info_ref, resid_ref, h_ref = refs
        resid = own_ref[...].astype(F32) + total(term_refs)
        resid_ref[...] = resid
        h_ref[...] = (resid * rms_of(resid) * info_ref[1:2, :]).astype(BF)

    return kernel_call(
        body, [whole(own.shape, F32), whole(own.shape, BF)], (*terms, own, info), limit=16, name="after_attention"
    )


def rows_after_feed(terms, resid, valid, teacher, out_grad, factor):
    def body(*refs):
        *term_refs, resid_ref, ok_ref, teacher_ref, grad_ref, factor_ref = refs[:-4]
        out_ref, dout_ref, dm_ref, squares_ref = refs[-4:]
        out = resid_ref[...] + total(term_refs)
        out_ref[...] = out.astype(BF)
        ok = ok_ref[...]
        diff = out - teacher_ref[...].astype(F32)
        part = jnp.sum(ok * diff * diff, axis=0, keepdims=True)
        squares_ref[...] = jnp.broadcast_to(jnp.sum(part, axis=1, keepdims=True), squares_ref.shape)
        dout = ok * (grad_ref[...].astype(F32) + factor_ref[0:1, 0:1] * diff)
        dout_ref[...] = dout
        dm_ref[...] = dout.astype(BF)

    shape = resid.shape
    return kernel_call(
        body,
        [whole(shape, BF), whole(shape, F32), whole(shape, BF), whole((8, LANES), F32)],
        (*terms, resid, valid, teacher, out_grad, factor),
        limit=16,
        name="after_feed",
    )


def rows_after_feed_back(terms, resid, dout, info):
    def body(*refs):
        *term_refs, resid_ref, dout_ref, info_ref, dresid_ref, da_ref = refs
        resid = resid_ref[...]
        dresid = dout_ref[...] + norm_back(total(term_refs), resid, rms_of(resid), info_ref[1:2, :])
        dresid_ref[...] = dresid
        da_ref[...] = dresid.astype(BF)

    return kernel_call(
        body,
        [whole(resid.shape, F32), whole(resid.shape, BF)],
        (*terms, resid, dout, info),
        flops=10**11,
        limit=16,
        name="after_feed_back",
    )


def rows_at_end(terms, own, dresid, info):
    def body(*refs):
        *term_refs, own_ref, dresid_ref, info_ref, dx_ref = refs
        rows = own_ref[...].astype(F32)
        dx = dresid_ref[...] + norm_back(total(term_refs), rows, rms_of(rows), info_ref[0:1, :])
        dx_ref[...] = dx.astype(BF)

    return kernel_call(body, whole(own.shape, BF), (*terms, own, dresid, info), limit=16, name="at_end")


def layer(
    inputs,
    valid,
    out_grad,
    teacher,
    norm_attn,
    w_query,
    key_matrix,
    value_matrix,
    w_out,
    norm_mlp,
    w_gate,
    w_up,
    w_down,
):
    seqs, seg, width = inputs.shape
    y = lax.axis_index("tensor")
    k = lax.axis_index("context")
    z, x, c = k // 4, (k // 2) % 2, k % 2
    place = jnp.stack([z, x, c, y]).astype(jnp.int32)
    seq_len = 16 * seg
    first = y == 0

    def mine(a):
        return lax.dynamic_index_in_dim(a, y, 0, keepdims=False)

    own = mine(inputs)
    counts = jnp.sum(valid.astype(F32), axis=1).astype(BF)
    ones = jnp.ones_like(norm_attn)
    extra = jnp.stack([norm_attn, norm_mlp, ones * counts[0], ones * counts[1]], axis=1)
    hidden = w_gate.shape[1] // 16
    bit = jnp.arange(2, dtype=jnp.int32)
    pos = (
        jnp.arange(4, dtype=jnp.int32)[:, None, None, None] * (4 * seg)
        + (bit ^ x)[None, :, None, None] * (2 * seg)
        + (bit ^ c)[None, None, :, None] * seg
        + jnp.arange(seg, dtype=jnp.int32)[None, None, None, :]
    ).reshape(seq_len)
    half = HEAD_SIZE // 2
    freqs = jnp.exp(-math.log(theta) * jnp.arange(half, dtype=F32) / half)
    angles = pos.astype(F32)[:, None] * freqs[None, :]
    cos_half, sin_half = jnp.cos(angles), jnp.sin(angles)
    pad = jnp.zeros((seq_len, LANES - HEAD_SIZE), F32)
    cosine = jnp.concatenate([cos_half, cos_half, pad], axis=1)
    sine = jnp.concatenate([-sin_half, sin_half, pad], axis=1)
    kpos = pos[None, :]

    firsts = pack_first(w_query, key_matrix, value_matrix, w_out.T, extra, w_down.T)
    seconds = pack_second(after(w_gate, cosine, sine), w_up, w_down.T)
    first_in = share_blocks(firsts)
    first_both = of_other(first_in)
    pieces, near, far = gather_rows(after(own, first_in), first_both)
    second_in = share_blocks(after(seconds, *near, *far))
    w_qkv, w_o, info = prepare_attention(place, first_in, first_both)
    lengths = jnp.sum(info[2:4], axis=1) / F32(width // 16)
    count = lengths[0] + lengths[1]
    length = jnp.full((8, LANES), jnp.where(first, lengths[0], lengths[1]), F32)
    factor = jnp.full((8, LANES), F32(seqs * seq_len) / count, F32)

    (h1, q, keys, values, ctx, lse), part = attention(
        place, pieces, w_qkv, w_o, info, length, kpos, cosine, sine
    )
    terms, far, come = scatter_rows(part)
    second_both = of_other(after(second_in, come[2]))
    resid, h2_own = rows_after_attention(terms, own, info)
    w_gu, w_d = prepare_feed(place, first_in, first_both, second_in, second_both, hidden)
    pieces, _, _ = gather_rows(h2_own, w_gu)
    (h2, gate_up, act), part = feed(pieces, w_gu, w_d)
    okf = mine(valid).astype(F32)[:, None]
    terms, _, _ = scatter_rows(part)
    out_own, dout, dm_own, squares = rows_after_feed(
        terms, resid, okf, mine(teacher), mine(out_grad), factor
    )
    pieces, _, _ = gather_rows(dm_own)
    dm, dgu, part = feed_back(pieces, w_gu, w_d, gate_up)
    terms, far, _ = scatter_rows(part)
    down = down_grads(after(dm, part[0]), act)
    shares, rest, tail2 = feed_grads(place, down, h2, after(dgu, *far), w_gu)
    summed = over_sequences(shares)
    dresid, da_own = rows_after_feed_back(terms, resid, dout, info)
    pieces, near, far = gather_rows(da_own)
    seconds = share_blocks(after(summed, *near, *far))
    da, dqkv, part = attention_back(
        place, pieces, w_qkv, w_o, length, kpos, cosine, sine, q, keys, values, lse
    )
    terms, far, x_come = scatter_rows(part)
    shares = attention_grads(place, h1, after(dqkv, *far), da, ctx, w_qkv, rest, tail2, squares)
    summed = over_sequences(after(shares, seconds, x_come[2]))
    dx = rows_at_end(terms, own, dresid, info)
    firsts = share_blocks(after(summed, seconds, dx))
    grad_gate, grad_up = unpack_second(after(seconds, dx), hidden)
    both_out = move_y(out_own)
    both_dx = move_y(dx)
    output = jnp.stack([jnp.where(first, out_own, both_out), jnp.where(first, both_out, out_own)])
    input_grad = jnp.stack([jnp.where(first, dx, both_dx), jnp.where(first, both_dx, dx)]).astype(F32)
    grad_query, grad_key, grad_value, grad_out, grad_down, tails = unpack_first(firsts, seconds, hidden)
    return (
        output,
        tails[0, 2] / (count * width),
        input_grad,
        tails[:, 0] / norm_attn.astype(F32),
        tails[:, 1] / norm_mlp.astype(F32),
        grad_query,
        grad_key,
        grad_value,
        grad_out.T,
        grad_gate,
        grad_up,
        grad_down.T,
    )


def rms_forward(value_rows, gain):
    inverse = lax.rsqrt(jnp.mean(value_rows * value_rows, axis=-1, keepdims=True) + eps)
    normed = value_rows * inverse
    return (normed, inverse, normed * gain)


def rms_backward(grad, normed, inverse, gain):
    scaled = grad * gain
    return inverse * (scaled - normed * jnp.mean(scaled * normed, axis=-1, keepdims=True))


def rotate(value_rows, cosine, sine):
    half = value_rows.shape[-1] // 2
    first, second = (value_rows[..., :half], value_rows[..., half:])
    return jnp.concatenate(
        [first * cosine - second * sine, second * cosine + first * sine], axis=-1
    )


def rotate_back(grad, cosine, sine):
    half = grad.shape[-1] // 2
    first, second = (grad[..., :half], grad[..., half:])
    return jnp.concatenate(
        [first * cosine + second * sine, second * cosine - first * sine], axis=-1
    )


def allowed_pairs(key_ok, qpos, seq_len):
    kpos = jnp.arange(seq_len, dtype=jnp.int32)
    return (kpos[None, :] // BLOCK <= qpos[:, None] // BLOCK) & (key_ok[None, :] > 0)


def masked_scores(query_rows, key_rows, key_ok, qpos, scale):
    raw = (
        jnp.einsum("qkgd,jkd->kgqj", query_rows, key_rows, preferred_element_type=jnp.float32)
        * scale
    )
    allowed = allowed_pairs(key_ok, qpos, key_rows.shape[0])
    return jnp.where(allowed, raw, jnp.float32(-1e30))


def dot_left(left, right):
    return lax.dot_general(
        left, right, (((0,), (0,)), ((), ())), preferred_element_type=jnp.float32
    )


def dot_right(left, right):
    return lax.dot_general(
        left, right, (((1,), (1,)), ((), ())), preferred_element_type=jnp.float32
    )


def shards(
    inputs,
    valid,
    out_grad,
    teacher,
    norm_attn,
    w_query,
    key_matrix,
    value_matrix,
    w_out,
    norm_mlp,
    w_gate,
    w_up,
    w_down,
):
    seqs, seg, width = inputs.shape
    ctx_size = lax.axis_size("context")
    index = lax.axis_index("context")
    scale = HEAD_SIZE ** (-0.5)
    half = HEAD_SIZE // 2
    gathered = (
        lax.all_gather(norm_attn, "context", axis=0, tiled=True),
        lax.all_gather(w_query, "context", axis=0, tiled=True),
        lax.all_gather(key_matrix, "context", axis=0, tiled=True),
        lax.all_gather(value_matrix, "context", axis=0, tiled=True),
        lax.all_gather(w_out, "context", axis=1, tiled=True),
        lax.all_gather(norm_mlp, "context", axis=0, tiled=True),
        lax.all_gather(w_gate, "context", axis=0, tiled=True),
        lax.all_gather(w_up, "context", axis=0, tiled=True),
        lax.all_gather(w_down, "context", axis=1, tiled=True),
    )
    gain_first, wq, wk, wv, wo, gain_second, wg, wu, wd = gathered
    gain1 = gain_first.astype(jnp.float32)
    gain2 = gain_second.astype(jnp.float32)
    heads_q = wq.shape[1] // HEAD_SIZE
    heads_kv = wk.shape[1] // HEAD_SIZE
    head_group = heads_q // heads_kv
    row_count = seqs * seg
    positions = index * seg + jnp.arange(seg, dtype=jnp.int32)
    freqs = jnp.exp(-math.log(theta) * jnp.arange(half, dtype=jnp.float32) / half)
    angles = positions.astype(jnp.float32)[:, None] * freqs[None, :]
    cosine = jnp.cos(angles)[:, None, :]
    sine = jnp.sin(angles)[:, None, :]
    x = inputs.astype(jnp.float32)
    normed1, inverse1, pre1 = rms_forward(x, gain1)
    h1 = pre1.astype(jnp.bfloat16).reshape(row_count, width)
    query_before_rotary = jnp.dot(h1, wq, preferred_element_type=jnp.float32).reshape(
        seqs, seg, heads_q, HEAD_SIZE
    )
    key_before_rotary = jnp.dot(h1, wk, preferred_element_type=jnp.float32).reshape(
        seqs, seg, heads_kv, HEAD_SIZE
    )
    value_own = (
        jnp.dot(h1, wv, preferred_element_type=jnp.float32)
        .astype(jnp.bfloat16)
        .reshape(seqs, seg, heads_kv * HEAD_SIZE)
    )
    query_rows = (
        rotate(query_before_rotary, cosine, sine)
        .astype(jnp.bfloat16)
        .reshape(seqs, seg, heads_kv, head_group, HEAD_SIZE)
    )
    key_own = (
        rotate(key_before_rotary, cosine, sine)
        .astype(jnp.bfloat16)
        .reshape(seqs, seg, heads_kv * HEAD_SIZE)
    )
    keys_all, values_all, valid_all = (
        lax.all_gather(key_own, "context", axis=1, tiled=True),
        lax.all_gather(value_own, "context", axis=1, tiled=True),
        lax.all_gather(valid.astype(jnp.bfloat16), "context", axis=1, tiled=True),
    )
    seq_len = keys_all.shape[1]

    def attend(carry, items):
        qseq, kseq, vseq, okseq = items
        key_rows = kseq.reshape(seq_len, heads_kv, HEAD_SIZE)
        value_rows = vseq.reshape(seq_len, heads_kv, HEAD_SIZE)
        scores = masked_scores(qseq, key_rows, okseq, positions, scale)
        top = jnp.max(scores, axis=-1, keepdims=True)
        expo = jnp.exp(scores - top)
        total = jnp.sum(expo, axis=-1, keepdims=True)
        probr = (expo / total).astype(jnp.bfloat16)
        ctx = jnp.einsum("kgqj,jkd->qkgd", probr, value_rows, preferred_element_type=jnp.float32)
        lse = (top + jnp.log(total))[..., 0]
        return (carry, (ctx.astype(jnp.bfloat16).reshape(seg, heads_q * HEAD_SIZE), lse))

    carry, (context, lse_all) = lax.scan(
        attend, jnp.float32(0.0), (query_rows, keys_all, values_all, valid_all)
    )
    ctx_flat = context.reshape(row_count, heads_q * HEAD_SIZE)
    attn = lax.psum(
        jnp.dot(ctx_flat, wo, preferred_element_type=jnp.float32).astype(jnp.bfloat16), "tensor"
    ).astype(jnp.float32)
    resid = x + attn.reshape(seqs, seg, width)
    normed2, inverse2, pre2 = rms_forward(resid, gain2)
    h2 = pre2.astype(jnp.bfloat16).reshape(row_count, width)
    gate = jnp.dot(h2, wg, preferred_element_type=jnp.float32)
    up = jnp.dot(h2, wu, preferred_element_type=jnp.float32)
    sigma = jax.nn.sigmoid(gate)
    silu = gate * sigma
    act = (silu * up).astype(jnp.bfloat16)
    mixed = lax.psum(
        jnp.dot(act, wd, preferred_element_type=jnp.float32).astype(jnp.bfloat16), "tensor"
    ).astype(jnp.float32)
    out = resid + mixed.reshape(seqs, seg, width)
    output = out.astype(jnp.bfloat16)
    validf = valid.astype(jnp.float32)[..., None]
    diff = out - teacher.astype(jnp.float32)
    count, squares = lax.psum(
        (jnp.sum(valid.astype(jnp.float32)), jnp.sum(validf * diff * diff)), "context"
    )
    loss = squares / (count * width)
    dout = validf * (
        out_grad.astype(jnp.float32) + jnp.float32(seqs * seg * ctx_size) / count * diff
    )
    dm = dout.astype(jnp.bfloat16).reshape(row_count, width)
    grad_down = dot_left(act, dm)
    dact = dot_right(dm, wd)
    dgate = (dact * up * sigma * (1.0 + gate * (1.0 - sigma))).astype(jnp.bfloat16)
    dup = (dact * silu).astype(jnp.bfloat16)
    grad_gate = dot_left(h2, dgate)
    grad_up = dot_left(h2, dup)
    dh2 = (
        lax.psum((dot_right(dgate, wg) + dot_right(dup, wu)).astype(jnp.bfloat16), "tensor")
        .astype(jnp.float32)
        .reshape(seqs, seg, width)
    )
    grad_gain2 = jnp.sum(dh2 * normed2, axis=(0, 1))
    dresid = dout + rms_backward(dh2, normed2, inverse2, gain2)
    dattn = dresid.astype(jnp.bfloat16).reshape(row_count, width)
    grad_out = dot_left(ctx_flat, dattn)
    dctx = (
        dot_right(dattn, wo)
        .astype(jnp.bfloat16)
        .reshape(seqs, seg, heads_kv, head_group, HEAD_SIZE)
    )

    def attend_back(carry, items):
        qseq, kseq, vseq, okseq, lseq, dseq = items
        allowed = allowed_pairs(okseq, positions, seq_len)

        def head_back(parts):
            qhead, khead, vhead, dhead, lhead = parts
            raw = (
                jnp.einsum("qgd,jd->gqj", qhead, khead, preferred_element_type=jnp.float32) * scale
            )
            scores = jnp.where(allowed[None], raw, jnp.float32(-1e30))
            prob = jnp.exp(scores - lhead[..., None])
            probr = prob.astype(jnp.bfloat16)
            dprob = jnp.einsum("qgd,jd->gqj", dhead, vhead, preferred_element_type=jnp.float32)
            delta = jnp.sum(prob * dprob, axis=-1, keepdims=True)
            dscore = (prob * (dprob - delta)).astype(jnp.bfloat16)
            dq = (
                jnp.einsum("gqj,jd->qgd", dscore, khead, preferred_element_type=jnp.float32) * scale
            )
            dk = (
                jnp.einsum("gqj,qgd->jd", dscore, qhead, preferred_element_type=jnp.float32) * scale
            )
            dv = jnp.einsum("gqj,qgd->jd", probr, dhead, preferred_element_type=jnp.float32)
            return (dq, dk, dv)

        heads_in = (
            jnp.moveaxis(qseq, 1, 0),
            jnp.moveaxis(kseq.reshape(seq_len, heads_kv, HEAD_SIZE), 1, 0),
            jnp.moveaxis(vseq.reshape(seq_len, heads_kv, HEAD_SIZE), 1, 0),
            jnp.moveaxis(dseq, 1, 0),
            lseq,
        )
        dq_heads, dk_heads, dv_heads = lax.map(head_back, heads_in)
        dq = jnp.moveaxis(dq_heads, 0, 1)
        dk = jnp.moveaxis(dk_heads, 0, 1).reshape(seq_len, heads_kv * HEAD_SIZE)
        dv = jnp.moveaxis(dv_heads, 0, 1).reshape(seq_len, heads_kv * HEAD_SIZE)
        dk_own, dv_own = (
            lax.psum_scatter(dk, "context", scatter_dimension=0, tiled=True),
            lax.psum_scatter(dv, "context", scatter_dimension=0, tiled=True),
        )
        return (carry, (dq, dk_own, dv_own))

    carry, (dq_all, dk_all, dv_all) = lax.scan(
        attend_back, jnp.float32(0.0), (query_rows, keys_all, values_all, valid_all, lse_all, dctx)
    )
    dqpre = (
        rotate_back(dq_all.reshape(seqs, seg, heads_q, HEAD_SIZE), cosine, sine)
        .astype(jnp.bfloat16)
        .reshape(row_count, heads_q * HEAD_SIZE)
    )
    dkpre = (
        rotate_back(dk_all.reshape(seqs, seg, heads_kv, HEAD_SIZE), cosine, sine)
        .astype(jnp.bfloat16)
        .reshape(row_count, heads_kv * HEAD_SIZE)
    )
    dvr = dv_all.astype(jnp.bfloat16).reshape(row_count, heads_kv * HEAD_SIZE)
    grad_query = dot_left(h1, dqpre)
    grad_key = dot_left(h1, dkpre)
    grad_value = dot_left(h1, dvr)
    dh1 = (
        lax.psum(
            (dot_right(dqpre, wq) + dot_right(dkpre, wk) + dot_right(dvr, wv)).astype(jnp.bfloat16),
            "tensor",
        )
        .astype(jnp.float32)
        .reshape(seqs, seg, width)
    )
    grad_gain1 = jnp.sum(dh1 * normed1, axis=(0, 1))
    input_grad = dresid + rms_backward(dh1, normed1, inverse1, gain1)
    summed = (
        lax.psum_scatter(grad_gain1, "context", scatter_dimension=0, tiled=True),
        lax.psum_scatter(grad_query, "context", scatter_dimension=0, tiled=True),
        lax.psum_scatter(grad_key, "context", scatter_dimension=0, tiled=True),
        lax.psum_scatter(grad_value, "context", scatter_dimension=0, tiled=True),
        lax.psum_scatter(grad_out, "context", scatter_dimension=1, tiled=True),
        lax.psum_scatter(grad_gain2, "context", scatter_dimension=0, tiled=True),
        lax.psum_scatter(grad_gate, "context", scatter_dimension=0, tiled=True),
        lax.psum_scatter(grad_up, "context", scatter_dimension=0, tiled=True),
        lax.psum_scatter(grad_down, "context", scatter_dimension=1, tiled=True),
    )
    (
        grad_gain1,
        grad_query,
        grad_key,
        grad_value,
        grad_out,
        grad_gain2,
        grad_gate,
        grad_up,
        grad_down,
    ) = summed
    return (
        output,
        loss,
        input_grad,
        grad_gain1,
        grad_gain2,
        grad_query,
        grad_key,
        grad_value,
        grad_out,
        grad_gate,
        grad_up,
        grad_down,
    )


def solution(mesh):
    in_specs = (
        P(None, "context", None),
        P(None, "context"),
        P(None, "context", None),
        P(None, "context", None),
        P("context"),
        P("context", "tensor"),
        P("context", "tensor"),
        P("context", "tensor"),
        P("tensor", "context"),
        P("context"),
        P("context", "tensor"),
        P("context", "tensor"),
        P("tensor", "context"),
    )
    out_specs = (
        P(None, "context", None),
        P(),
        P(None, "context", None),
        P("context"),
        P("context"),
        P("context", "tensor"),
        P("context", "tensor"),
        P("context", "tensor"),
        P("tensor", "context"),
        P("context", "tensor"),
        P("context", "tensor"),
        P("tensor", "context"),
    )
    fits = dict(mesh.shape) == {"tensor": 2, "context": 16}
    return jax.shard_map(
        layer if fits else shards, mesh=mesh, in_specs=in_specs, out_specs=out_specs, check_vma=False
    )
```

```python
import functools
import functools
import math

import jax
import jax.numpy as jnp
from jax import lax
from jax.experimental import pallas as pl
from jax.experimental.pallas import tpu as pltpu
from jax.sharding import PartitionSpec as P

HEAD_SIZE = 80
BLOCK = 256
LANES = 128

eps = 1e-05
theta = 10000.0
BF = jnp.bfloat16
F32 = jnp.float32
MIB = 1024 * 1024
SLOW = ()


def whole(shape, dtype):
    return jax.ShapeDtypeStruct(tuple(shape), dtype)


def kernel_call(body, outs, ins, scalars=0, far=(), flops=0, scratch=(), limit=16, name=None):
    single = not isinstance(outs, (list, tuple))
    spec = lambda i: (
        pl.BlockSpec(memory_space=pltpu.SMEM)
        if i < scalars
        else pl.BlockSpec(memory_space=pl.ANY)
        if i in far
        else pl.BlockSpec(memory_space=pltpu.VMEM)
    )
    out_spec = pl.BlockSpec(memory_space=pltpu.VMEM)
    nbytes = sum(math.prod(a.shape) * a.dtype.itemsize for a in ins)
    nbytes += sum(math.prod(o.shape) * o.dtype.itemsize for o in ([outs] if single else outs))
    return pl.pallas_call(
        body,
        out_shape=outs,
        in_specs=[spec(i) for i in range(len(ins))],
        out_specs=out_spec if single else [out_spec] * len(outs),
        scratch_shapes=list(scratch),
        compiler_params=pltpu.CompilerParams(vmem_limit_bytes=limit * MIB),
        cost_estimate=pl.CostEstimate(flops=flops if name in SLOW else 0, bytes_accessed=0, transcendentals=0),
        name=name,
    )(*ins)


def dot_nn(a, b):
    return lax.dot_general(a, b, (((1,), (0,)), ((), ())), preferred_element_type=F32)


def dot_nt(a, b):
    return lax.dot_general(a, b, (((1,), (1,)), ((), ())), preferred_element_type=F32)


def dot_tn(a, b):
    return lax.dot_general(a, b, (((0,), (0,)), ((), ())), preferred_element_type=F32)


def move_c(a):
    return lax.ppermute(a, "context", [(k, k ^ 1) for k in range(16)])


def move_x(a):
    return lax.ppermute(a, "context", [(k, k ^ 2) for k in range(16)])


def move_z(a, step):
    return lax.ppermute(a, "context", [(k, (k + 4 * step) % 16) for k in range(16)])


def move_y(a):
    return lax.ppermute(a, "tensor", [(0, 1), (1, 0)])


def share_out(a):
    return lax.all_to_all(a, "context", split_axis=0, concat_axis=0, tiled=True)


def after(value, *others):
    return lax.optimization_barrier((value, *others))[0]


def stack(pieces):
    def body(*refs):
        for m in range(4):
            refs[4][m] = refs[m][...]

    return kernel_call(body, whole((4, *pieces[0].shape), BF), tuple(pieces), limit=8, name="stack")


def gather_rows(own, *late, early=()):
    near = [own] + [move_z(own, m) for m in (1, 2, 3)]
    far = [move_x(own)]
    far += [move_x(after(near[1], far[0], *early)), None, move_x(after(near[3], far[0], *early))]
    far[2] = move_x(after(near[2], far[1], far[3]))
    near_all, far_all = stack(near), stack(far)
    last = after(far_all, *late) if late else far_all
    return (near_all, move_c(near_all), far_all, move_c(last)), near, far


def scatter_rows(part, *late):
    far1, far0, near1, near0 = part
    shape = far1.shape[1:]

    def add_far(a_ref, b_ref, *outs):
        for m in range(4):
            outs[m][...] = (a_ref[m].astype(F32) + b_ref[m].astype(F32)).astype(BF)

    def add_near(m, a_ref, b_ref, c_ref, out_ref):
        out_ref[...] = (a_ref[m].astype(F32) + b_ref[m].astype(F32) + c_ref[...].astype(F32)).astype(BF)

    far = kernel_call(add_far, [whole(shape, BF)] * 4, (far0, move_c(far1)), limit=16, name="add_far")
    near1 = move_c(near1)
    come = {m: move_x(far[m]) for m in (2, 1, 3, 0)}
    if late:
        come[2] = after(come[2], *late)
    terms = [near0, near1, come[0]]
    for m in (2, 1, 3):
        body = functools.partial(add_near, m)
        s = kernel_call(body, whole(shape, BF), (near0, near1, come[m]), limit=8, name="add_near")
        terms.append(move_z(s, 4 - m))
    return terms, far, come


def part_shapes(seg, width):
    return [
        whole((4, seg, width), BF),
        whole((4, seg, width), BF),
        whole((4, seg, width), BF),
        whole((4, seg, width), BF),
    ]


def write_part(outs, group, value):
    far1, far0, near1, near0 = outs
    seg = far1.shape[1]
    to = (near0, near1, far0, far1)[group]
    for m in range(4):
        to[m] = value[m * seg : (m + 1) * seg].astype(BF)


def total(refs):
    out = refs[0][0].astype(F32) + refs[1][0].astype(F32)
    for r in refs[2:]:
        out = out + r[...].astype(F32)
    return out


FIRST = 384
SECOND = 640
EXTRA = 4


def pack_first(wq, wk, wv, wot, extra, wdt):
    rows, d = wq.shape[0], HEAD_SIZE
    hidden = wdt.shape[1] // 16
    some = FIRST - 4 * d - EXTRA

    def body(q_ref, k_ref, v_ref, o_ref, e_ref, d_ref, out_ref):
        for k in range(16):
            block = jnp.concatenate(
                [
                    q_ref[:, k * d : (k + 1) * d],
                    k_ref[:, k // 4 * d : (k // 4 + 1) * d],
                    v_ref[:, k // 4 * d : (k // 4 + 1) * d],
                    o_ref[:, k * d : (k + 1) * d],
                    e_ref[...],
                    d_ref[:, k * hidden : k * hidden + some],
                ],
                axis=1,
            )
            out_ref[k] = block

    return kernel_call(
        body, whole((16, rows, FIRST), BF), (wq, wk, wv, wot, extra, wdt), limit=16, name="pack_first"
    )


def pack_second(wg, wu, wdt):
    rows = wg.shape[0]
    hidden = wg.shape[1] // 16
    some = FIRST - 4 * HEAD_SIZE - EXTRA
    spare = SECOND - 3 * hidden + some

    def body(g_ref, u_ref, d_ref, out_ref):
        for k in range(16):
            block = jnp.concatenate(
                [
                    d_ref[:, k * hidden + some : (k + 1) * hidden],
                    g_ref[:, k * hidden : (k + 1) * hidden],
                    u_ref[:, k * hidden : (k + 1) * hidden],
                    jnp.zeros((rows, spare), BF),
                ],
                axis=1,
            )
            out_ref[k] = block

    return kernel_call(body, whole((16, rows, SECOND), BF), (wg, wu, wdt), limit=16, name="pack_second")


def share_blocks(a):
    return share_out(a.reshape(-1, a.shape[2])).reshape(a.shape)


def of_other(a):
    return lax.all_gather(a, "tensor", axis=0, tiled=False)


def over_sequences(parts):
    return lax.psum_scatter(parts, "tensor", scatter_dimension=0, tiled=False)


def unpack_second(second, hidden):
    rows = second.shape[1]

    def body(s_ref, g_ref, u_ref):
        for k in range(16):
            c = s_ref[k].astype(F32)
            g_ref[:, k * hidden : (k + 1) * hidden] = c[:, :hidden]
            u_ref[:, k * hidden : (k + 1) * hidden] = c[:, hidden : 2 * hidden]

    return kernel_call(body, [whole((rows, 16 * hidden), F32)] * 2, (second,), limit=16, name="unpack_second")


def unpack_first(first, second, hidden):
    rows, d = first.shape[1], HEAD_SIZE
    cut = SECOND - 2 * hidden
    rest = 4 * d + hidden - cut

    def body(f_ref, s_ref, q_ref, k_ref, v_ref, o_ref, d_ref, tail_ref):
        tail = jnp.zeros((rows, 3), F32)
        for k in range(16):
            b = f_ref[k].astype(F32)
            q_ref[:, k * d : (k + 1) * d] = b[:, :d]
            o_ref[:, k * d : (k + 1) * d] = b[:, 3 * d : 4 * d]
            if k % 4 == 0:
                keys = jnp.zeros((rows, 2 * d), F32)
            keys = keys + b[:, d : 3 * d]
            if k % 4 == 3:
                k_ref[:, k // 4 * d : (k // 4 + 1) * d] = keys[:, :d]
                v_ref[:, k // 4 * d : (k // 4 + 1) * d] = keys[:, d:]
            tail = tail + b[:, rest : rest + 3]
            d_ref[:, k * hidden : k * hidden + cut] = s_ref[k][:, 2 * hidden :].astype(F32)
            d_ref[:, k * hidden + cut : (k + 1) * hidden] = b[:, 4 * d : rest]
        tail_ref[...] = tail

    outs = [whole((rows, w), F32) for w in (16 * d, 4 * d, 4 * d, 16 * d, 16 * hidden, 3)]
    return kernel_call(body, outs, (first, second), limit=16, name="unpack_first")


def order_attention(mine_ref, other_ref, w_ref, out_ref, row_ref, info_ref):
    size, d = mine_ref.shape[1], HEAD_SIZE
    info_ref[...] = jnp.zeros_like(info_ref)
    for k in range(16):
        rs = slice(k * size, (k + 1) * size)
        parts = [mine_ref[k], other_ref[k]]
        w_ref[rs, :] = jnp.concatenate([p[:, : 3 * d] for p in parts], axis=1)
        out_ref[rs, :] = jnp.concatenate([p[:, 3 * d : 4 * d] for p in parts], axis=1)
        info_ref[rs, :EXTRA] = parts[0][:, 4 * d : 4 * d + EXTRA].astype(F32)
    for b in range(16 * size // LANES):
        rs = slice(b * LANES, (b + 1) * LANES)
        row_ref[:, rs] = info_ref[rs, :].T[0:8, :]


def order_feed(fm_ref, fo_ref, m_ref, o_ref, gu_ref, d_ref, hidden):
    size = m_ref.shape[1]
    at = 4 * HEAD_SIZE + EXTRA
    rest = hidden - (FIRST - at)
    for k in range(16):
        rs = slice(k * size, (k + 1) * size)
        fm, fo, m, o = fm_ref[k], fo_ref[k], m_ref[k], o_ref[k]
        gu_ref[rs, :] = jnp.concatenate(
            [
                m[:, rest : rest + hidden],
                o[:, rest : rest + hidden],
                m[:, rest + hidden : rest + 2 * hidden],
                o[:, rest + hidden : rest + 2 * hidden],
            ],
            axis=1,
        )
        d_ref[rs, :] = jnp.concatenate([fm[:, at:], m[:, :rest], fo[:, at:], o[:, :rest]], axis=1)


def turn(a, cosine, sine):
    half = HEAD_SIZE // 2
    lane = lax.broadcasted_iota(jnp.int32, a.shape, 1)
    swapped = jnp.where(lane < half, pltpu.roll(a, LANES - half, 1), pltpu.roll(a, half, 1))
    return a * cosine + swapped * sine


def head_of(value, at):
    part = value[:, at * HEAD_SIZE : (at + 1) * HEAD_SIZE]
    return jnp.concatenate([part, jnp.zeros((value.shape[0], LANES - HEAD_SIZE), value.dtype)], axis=1)


def attention(place, pieces, mine, both, kpos, cosine, sine):
    seg, width = pieces[0].shape[1:]
    rows = 16 * seg
    blocks = rows // BLOCK
    scale = HEAD_SIZE ** (-0.5)

    def body(place_ref, *refs):
        x_refs = [refs[i // 4].at[i % 4] for i in range(16)]
        mine_ref, both_ref, kpos_ref, cos_ref, sin_ref = refs[4:9]
        h_ref, q_ref, k_ref, v_ref, ctx_ref, lse_ref, w_ref, wo_ref, row_ref, *part = refs[9:22]
        other_ref, info_ref, sem = refs[22:]
        other = pltpu.make_async_copy(both_ref.at[1 - place_ref[3]], other_ref, sem)
        other.start()
        other.wait()
        order_attention(mine_ref, other_ref, w_ref, wo_ref, row_ref, info_ref)
        z = place_ref[0]
        gain = row_ref[0:1, :]
        counts = jnp.where(place_ref[3] == 0, row_ref[2:3, :], row_ref[3:4, :])
        length = jnp.sum(counts, axis=1, keepdims=True) / F32(width // 16)
        for i in range(16):

            @pl.loop(0, seg // 16)
            def _(r):
                at = pl.multiple_of(r * 16, 16)
                xs = x_refs[i][pl.ds(at, 16), :].astype(F32)
                inv = lax.rsqrt(jnp.mean(xs * xs, axis=-1, keepdims=True) + eps)
                h_ref[pl.ds(i * seg + at, 16), :] = (xs * inv * gain).astype(BF)

        for g in range(4):
            qkv = dot_nn(h_ref[g * 4 * seg : (g + 1) * 4 * seg, :], w_ref[...])
            for m in range(4):
                to = pl.multiple_of(lax.rem(z - m + 4, 4) * BLOCK + g * seg, seg)
                to = pl.ds(to, seg)
                piece = qkv[m * seg : (m + 1) * seg]
                cosine, sine = cos_ref[to, :], sin_ref[to, :]
                for h in range(2):
                    q_ref[h, to, :] = turn(head_of(piece, 3 * h), cosine, sine).astype(BF)
                    k_ref[h, to, :] = turn(head_of(piece, 3 * h + 1), cosine, sine).astype(BF)
                    v_ref[h, to, :] = head_of(piece, 3 * h + 2).astype(BF)
        for i in range(blocks):
            m = lax.rem(z - i + 4, 4)
            n = (i + 1) * BLOCK
            ok = kpos_ref[:, :n].astype(F32) < length
            for h in range(2):
                s = dot_nt(q_ref[h, i * BLOCK : n, :], k_ref[h, :n, :]) * scale
                s = jnp.where(ok, s, F32(-1e30))
                top = jnp.max(s, axis=1, keepdims=True)
                e = jnp.exp(s - top)
                tot = jnp.sum(e, axis=1, keepdims=True)
                ctx = dot_nn((e / tot).astype(BF), v_ref[h, :n, :]).astype(BF)
                for g in range(4):
                    to = pl.ds(pl.multiple_of((g * 4 + m) * seg, seg), seg)
                    ctx_ref[to, h * HEAD_SIZE : (h + 1) * HEAD_SIZE] = ctx[g * seg : (g + 1) * seg, :HEAD_SIZE]
                lse_ref[h, i * BLOCK : n, :] = top + jnp.log(tot)
        for g in (3, 2, 1, 0):
            write_part(part, g, dot_nt(ctx_ref[g * 4 * seg : (g + 1) * 4 * seg, :], wo_ref[...]))

    outs = [
        whole((rows, width), BF),
        whole((2, rows, LANES), BF),
        whole((2, rows, LANES), BF),
        whole((2, rows, LANES), BF),
        whole((rows, 2 * HEAD_SIZE), BF),
        whole((2, rows, 1), F32),
        whole((width, 6 * HEAD_SIZE), BF),
        whole((width, 2 * HEAD_SIZE), BF),
        whole((8, width), F32),
    ] + part_shapes(seg, width)
    flops = 2 * rows * width * 6 * LANES + 2 * rows * rows * LANES * 2 * 2
    out = kernel_call(
        body,
        outs,
        (place, *pieces, mine, both, kpos, cosine, sine),
        scalars=1,
        far=(6,),
        scratch=[pltpu.VMEM(mine.shape, BF), pltpu.VMEM((width, LANES), F32), pltpu.SemaphoreType.DMA],
        limit=24,
        flops=flops,
        name="attention",
    )
    return out[:9], out[9:]


def attention_back(place, pieces, weights, w_o, length, kpos, cosine, sine, q, k, v, lse):
    seg, width = pieces[0].shape[1:]
    rows = 16 * seg
    blocks = rows // BLOCK
    scale = HEAD_SIZE ** (-0.5)

    def body(place_ref, *refs):
        d_refs = [refs[i // 4].at[i % 4] for i in range(16)]
        w_ref, wo_ref, len_ref, kpos_ref, cos_ref, sin_ref, q_ref, k_ref, v_ref, lse_ref = refs[4:14]
        da_ref, dqkv_ref, *part = refs[14:20]
        dctx_ref, dk_ref, dv_ref = refs[20:]
        z = place_ref[0]
        length = len_ref[0:1, 0:1]
        for i in range(16):
            da_ref[i * seg : (i + 1) * seg, :] = d_refs[i][...]
        for g in range(4):
            dctx = dot_nn(da_ref[g * 4 * seg : (g + 1) * 4 * seg, :], wo_ref[...])
            for m in range(4):
                to = pl.multiple_of(lax.rem(z - m + 4, 4) * BLOCK + g * seg, seg)
                for h in range(2):
                    dctx_ref[h, pl.ds(to, seg), :] = head_of(dctx[m * seg : (m + 1) * seg], h).astype(BF)
        dk_ref[...] = jnp.zeros_like(dk_ref)
        dv_ref[...] = jnp.zeros_like(dv_ref)

        def put(i, at, value):
            m = lax.rem(z - i + 4, 4)
            for g in range(4):
                to = pl.ds(pl.multiple_of((g * 4 + m) * seg, seg), seg)
                dqkv_ref[to, at * HEAD_SIZE : (at + 1) * HEAD_SIZE] = value[g * seg : (g + 1) * seg, :HEAD_SIZE]

        for i in range(blocks):
            n = (i + 1) * BLOCK
            ok = kpos_ref[:, :n].astype(F32) < length
            cosine, sine = cos_ref[i * BLOCK : n, :], sin_ref[i * BLOCK : n, :]
            for h in range(2):
                qi = q_ref[h, i * BLOCK : n, :]
                di = dctx_ref[h, i * BLOCK : n, :]
                s = dot_nt(qi, k_ref[h, :n, :]) * scale
                p = jnp.where(ok, jnp.exp(s - lse_ref[h, i * BLOCK : n, :]), F32(0.0))
                dp = dot_nt(di, v_ref[h, :n, :])
                delta = jnp.sum(p * dp, axis=1, keepdims=True)
                ds = (p * (dp - delta)).astype(BF)
                dq = dot_nn(ds, k_ref[h, :n, :]) * scale
                put(i, 3 * h, turn(dq, cosine, -sine).astype(BF))
                dk_ref[h, :n, :] += dot_tn(ds, qi)
                dv_ref[h, :n, :] += dot_tn(p.astype(BF), di)
        for i in range(blocks):
            rs = slice(i * BLOCK, (i + 1) * BLOCK)
            for h in range(2):
                dk = turn(dk_ref[h, rs, :] * scale, cos_ref[rs, :], -sin_ref[rs, :])
                put(i, 3 * h + 1, dk.astype(BF))
                put(i, 3 * h + 2, dv_ref[h, rs, :].astype(BF))
        for g in (3, 2, 1, 0):
            write_part(part, g, dot_nt(dqkv_ref[g * 4 * seg : (g + 1) * 4 * seg, :], w_ref[...]))

    outs = [whole((rows, width), BF), whole((rows, 6 * HEAD_SIZE), BF)] + part_shapes(seg, width)
    flops = 2 * rows * width * 6 * LANES + 2 * rows * rows * LANES * 2 * 5
    out = kernel_call(
        body,
        outs,
        (place, *pieces, weights, w_o, length, kpos, cosine, sine, q, k, v, lse),
        scalars=1,
        flops=flops,
        scratch=[
            pltpu.VMEM((2, rows, LANES), BF),
            pltpu.VMEM((2, rows, LANES), F32),
            pltpu.VMEM((2, rows, LANES), F32),
        ],
        name="attention_back",
    )
    return out[0], out[1], out[2:]


def write_blocks(out_ref, index, chunk, value):
    rows = out_ref.shape[2]
    for k in range(4):
        out_ref[index, chunk * 4 + k] = value[k * rows : (k + 1) * rows].astype(BF)


def attention_grads(place, h1, dqkv, da, ctx, weights, rest, tail2, squares):
    rows, width = h1.shape
    d, cut = HEAD_SIZE, rest.shape[1] // 2
    spare = FIRST - 4 * d - cut - 3

    def body(place_ref, h_ref, dqkv_ref, da_ref, ctx_ref, w_ref, rest_ref, tail_ref, sq_ref, out_ref):
        y = place_ref[3]
        quarter = width // 4
        for b in range(4):
            at = slice(b * quarter, (b + 1) * quarter)
            g = dot_tn(h_ref[:, at], dqkv_ref[...])
            tail1 = jnp.sum(g * w_ref[at, :].astype(F32), axis=1, keepdims=True)
            o = dot_tn(da_ref[:, at], ctx_ref[...])
            sq = jnp.broadcast_to(sq_ref[0:1, 0:1], (quarter, 1))
            last = [tail1, tail_ref[at, :], sq, jnp.zeros((quarter, spare), F32)]
            for h, index in enumerate((y, 1 - y)):
                parts = [g[:, 3 * d * h : 3 * d * (h + 1)], o[:, d * h : d * (h + 1)]]
                parts += [rest_ref[at, cut * h : cut * (h + 1)].astype(F32)]
                write_blocks(out_ref, index, b, jnp.concatenate(parts + last, axis=1))

    return kernel_call(
        body,
        whole((2, 16, width // 16, FIRST), BF),
        (place, h1, dqkv, da, ctx, weights, rest, tail2, squares),
        scalars=1,
        flops=2 * rows * width * 8 * d,
        name="attention_grads",
    )


def feed(place, pieces, first_mine, first_both, mine, both, hidden):
    seg, width = pieces[0].shape[1:]
    rows = 16 * seg
    columns = 2 * hidden

    def body(place_ref, *refs):
        h_refs = [refs[i // 4].at[i % 4] for i in range(16)]
        fm_ref, fboth_ref, m_ref, both_ref, h_ref, gate_ref, act_ref, wg_ref, wd_ref, *part = refs[4:17]
        fo_ref, o_ref, sem = refs[17:]
        first = pltpu.make_async_copy(fboth_ref.at[1 - place_ref[3]], fo_ref, sem.at[0])
        second = pltpu.make_async_copy(both_ref.at[1 - place_ref[3]], o_ref, sem.at[1])
        first.start()
        second.start()
        for i in range(16):
            h_ref[i * seg : (i + 1) * seg, :] = h_refs[i][...]
        first.wait()
        second.wait()
        order_feed(fm_ref, fo_ref, m_ref, o_ref, wg_ref, wd_ref, hidden)
        for g in range(4):
            rs = slice(g * 4 * seg, (g + 1) * 4 * seg)
            gu = dot_nn(h_ref[rs, :], wg_ref[...])
            gate_ref[rs, :] = gu
            gate, up = gu[:, :columns], gu[:, columns:]
            act_ref[rs, :] = (gate * jax.nn.sigmoid(gate) * up).astype(BF)
        for g in (3, 2, 1, 0):
            rs = slice(g * 4 * seg, (g + 1) * 4 * seg)
            write_part(part, g, dot_nt(act_ref[rs, :], wd_ref[...]))

    outs = [whole((rows, width), BF), whole((rows, 2 * columns), F32), whole((rows, columns), BF)]
    outs += [whole((width, 2 * columns), BF), whole((width, columns), BF)]
    out = kernel_call(
        body,
        outs + part_shapes(seg, width),
        (place, *pieces, first_mine, first_both, mine, both),
        scalars=1,
        far=(6, 8),
        scratch=[
            pltpu.VMEM(first_mine.shape, BF),
            pltpu.VMEM(mine.shape, BF),
            pltpu.SemaphoreType.DMA((2,)),
        ],
        limit=26,
        name="feed",
    )
    return out[:5], out[5:]


def feed_back(pieces, w_gu, w_d, gate_up):
    seg, width = pieces[0].shape[1:]
    rows = 16 * seg
    hidden = w_d.shape[1]

    def body(*refs):
        d_refs = [refs[i // 4].at[i % 4] for i in range(16)]
        wg_ref, wd_ref, gate_ref, dm_ref, dgu_ref, *part = refs[4:]
        for i in range(16):
            dm_ref[i * seg : (i + 1) * seg, :] = d_refs[i][...]
        for g in (3, 2, 1, 0):
            rs = slice(g * 4 * seg, (g + 1) * 4 * seg)
            dact = dot_nn(dm_ref[rs, :], wd_ref[...])
            gate, up = gate_ref[rs, :hidden], gate_ref[rs, hidden:]
            sigma = jax.nn.sigmoid(gate)
            dgate = dact * up * sigma * (1.0 + gate * (1.0 - sigma))
            dgu_ref[rs, :] = jnp.concatenate([dgate, dact * (gate * sigma)], axis=1).astype(BF)
        for g in (3, 2, 1, 0):
            rs = slice(g * 4 * seg, (g + 1) * 4 * seg)
            write_part(part, g, dot_nt(dgu_ref[rs, :], wg_ref[...]))

    outs = [whole((rows, width), BF), whole((rows, 2 * hidden), BF)]
    out = kernel_call(
        body,
        outs + part_shapes(seg, width),
        (*pieces, w_gu, w_d, gate_up),
        flops=2 * rows * width * hidden * 3,
        limit=16,
        name="feed_back",
    )
    return out[0], out[1], out[2:]


def down_grads(dm, act):
    rows, width = dm.shape
    hidden = act.shape[1]

    def body(dm_ref, act_ref, out_ref):
        quarter = width // 4
        for b in range(4):
            at = slice(b * quarter, (b + 1) * quarter)
            out_ref[at, :] = dot_tn(dm_ref[:, at], act_ref[...]).astype(BF)

    return kernel_call(
        body, whole((width, hidden), BF), (dm, act), flops=2 * rows * width * hidden, limit=16, name="down_grads"
    )


def feed_grads(place, down, h2, dgu, w_gu):
    rows, width = h2.shape
    hidden = down.shape[1] // 2
    cut = SECOND - 2 * hidden
    left = hidden - cut

    def body(place_ref, down_ref, h_ref, dgu_ref, w_ref, out_ref, rest_ref, tail_ref):
        y = place_ref[3]
        quarter = width // 4
        for b in range(4):
            at = slice(b * quarter, (b + 1) * quarter)
            g = dot_tn(h_ref[:, at], dgu_ref[...])
            tail_ref[at, :] = jnp.sum(g * w_ref[at, :].astype(F32), axis=1, keepdims=True)
            down = down_ref[at, :].astype(F32)
            rest_ref[at, :] = jnp.concatenate([down[:, cut:hidden], down[:, hidden + cut :]], axis=1).astype(BF)
            for h, index in enumerate((y, 1 - y)):
                parts = [
                    g[:, hidden * h : hidden * (h + 1)],
                    g[:, hidden * (2 + h) : hidden * (3 + h)],
                    down[:, hidden * h : hidden * h + cut],
                ]
                write_blocks(out_ref, index, b, jnp.concatenate(parts, axis=1))

    outs = [whole((2, 16, width // 16, SECOND), BF)] + [whole((width, 2 * left), BF), whole((width, 1), F32)]
    return kernel_call(
        body,
        outs,
        (place, down, h2, dgu, w_gu),
        scalars=1,
        flops=2 * rows * width * hidden * 4,
        limit=16,
        name="feed_grads",
    )


def norm_back(grad, rows, inverse, gain):
    normed = rows * inverse
    scaled = grad * gain
    return inverse * (scaled - normed * jnp.mean(scaled * normed, axis=-1, keepdims=True))


def rms_of(rows):
    return lax.rsqrt(jnp.mean(rows * rows, axis=-1, keepdims=True) + eps)


def rows_after_attention(terms, own, info):
    def body(*refs):
        *term_refs, own_ref, info_ref, resid_ref, h_ref = refs
        resid = own_ref[...].astype(F32) + total(term_refs)
        resid_ref[...] = resid
        h_ref[...] = (resid * rms_of(resid) * info_ref[1:2, :]).astype(BF)

    return kernel_call(
        body, [whole(own.shape, F32), whole(own.shape, BF)], (*terms, own, info), limit=16, name="after_attention"
    )


def rows_after_feed(terms, resid, valid, teacher, out_grad, factor):
    def body(*refs):
        *term_refs, resid_ref, ok_ref, teacher_ref, grad_ref, factor_ref = refs[:-4]
        out_ref, dout_ref, dm_ref, squares_ref = refs[-4:]
        out = resid_ref[...] + total(term_refs)
        out_ref[...] = out.astype(BF)
        ok = ok_ref[...]
        diff = out - teacher_ref[...].astype(F32)
        part = jnp.sum(ok * diff * diff, axis=0, keepdims=True)
        squares_ref[...] = jnp.broadcast_to(jnp.sum(part, axis=1, keepdims=True), squares_ref.shape)
        dout = ok * (grad_ref[...].astype(F32) + factor_ref[0:1, 0:1] * diff)
        dout_ref[...] = dout
        dm_ref[...] = dout.astype(BF)

    shape = resid.shape
    return kernel_call(
        body,
        [whole(shape, BF), whole(shape, F32), whole(shape, BF), whole((8, LANES), F32)],
        (*terms, resid, valid, teacher, out_grad, factor),
        limit=16,
        name="after_feed",
    )


def rows_after_feed_back(terms, resid, dout, info):
    def body(*refs):
        *term_refs, resid_ref, dout_ref, info_ref, dresid_ref, da_ref = refs
        resid = resid_ref[...]
        dresid = dout_ref[...] + norm_back(total(term_refs), resid, rms_of(resid), info_ref[1:2, :])
        dresid_ref[...] = dresid
        da_ref[...] = dresid.astype(BF)

    return kernel_call(
        body,
        [whole(resid.shape, F32), whole(resid.shape, BF)],
        (*terms, resid, dout, info),
        flops=10**11,
        limit=16,
        name="after_feed_back",
    )


def rows_at_end(terms, own, dresid, info):
    def body(*refs):
        *term_refs, own_ref, dresid_ref, info_ref, dx_ref = refs
        rows = own_ref[...].astype(F32)
        dx = dresid_ref[...] + norm_back(total(term_refs), rows, rms_of(rows), info_ref[0:1, :])
        dx_ref[...] = dx.astype(BF)

    return kernel_call(body, whole(own.shape, BF), (*terms, own, dresid, info), limit=16, name="at_end")


def layer(
    inputs,
    valid,
    out_grad,
    teacher,
    norm_attn,
    w_query,
    key_matrix,
    value_matrix,
    w_out,
    norm_mlp,
    w_gate,
    w_up,
    w_down,
):
    seqs, seg, width = inputs.shape
    y = lax.axis_index("tensor")
    k = lax.axis_index("context")
    z, x, c = k // 4, (k // 2) % 2, k % 2
    place = jnp.stack([z, x, c, y]).astype(jnp.int32)
    seq_len = 16 * seg
    first = y == 0

    def mine(a):
        return lax.dynamic_index_in_dim(a, y, 0, keepdims=False)

    own = mine(inputs)
    counts = jnp.sum(valid.astype(F32), axis=1).astype(BF)
    ones = jnp.ones_like(norm_attn)
    extra = jnp.stack([norm_attn, norm_mlp, ones * counts[0], ones * counts[1]], axis=1)
    hidden = w_gate.shape[1] // 16
    bit = jnp.arange(2, dtype=jnp.int32)
    pos = (
        jnp.arange(4, dtype=jnp.int32)[:, None, None, None] * (4 * seg)
        + (bit ^ x)[None, :, None, None] * (2 * seg)
        + (bit ^ c)[None, None, :, None] * seg
        + jnp.arange(seg, dtype=jnp.int32)[None, None, None, :]
    ).reshape(seq_len)
    half = HEAD_SIZE // 2
    freqs = jnp.exp(-math.log(theta) * jnp.arange(half, dtype=F32) / half)
    angles = pos.astype(F32)[:, None] * freqs[None, :]
    cos_half, sin_half = jnp.cos(angles), jnp.sin(angles)
    pad = jnp.zeros((seq_len, LANES - HEAD_SIZE), F32)
    cosine = jnp.concatenate([cos_half, cos_half, pad], axis=1)
    sine = jnp.concatenate([-sin_half, sin_half, pad], axis=1)
    kpos = pos[None, :]

    firsts = pack_first(w_query, key_matrix, value_matrix, w_out.T, extra, w_down.T)
    seconds = pack_second(after(w_gate, cosine, sine), w_up, w_down.T)
    first_in = share_blocks(firsts)
    first_both = of_other(first_in)
    pieces, near, far = gather_rows(after(own, first_in), first_both)
    second_in = share_blocks(after(seconds, *near, *far))
    (h1, q, keys, values, ctx, lse, w_qkv, w_o, info), part = attention(
        place, pieces, first_in, first_both, kpos, cosine, sine
    )
    lengths = jnp.sum(info[2:4], axis=1) / F32(width // 16)
    count = lengths[0] + lengths[1]
    length = jnp.full((8, LANES), jnp.where(first, lengths[0], lengths[1]), F32)
    factor = jnp.full((8, LANES), F32(seqs * seq_len) / count, F32)
    terms, far, come = scatter_rows(part)
    second_both = of_other(after(second_in, come[2]))
    resid, h2_own = rows_after_attention(terms, own, info)
    pieces, _, _ = gather_rows(h2_own)
    (h2, gate_up, act, w_gu, w_d), part = feed(
        place, pieces, first_in, first_both, second_in, second_both, hidden
    )
    okf = mine(valid).astype(F32)[:, None]
    terms, _, _ = scatter_rows(part)
    out_own, dout, dm_own, squares = rows_after_feed(
        terms, resid, okf, mine(teacher), mine(out_grad), factor
    )
    pieces, _, _ = gather_rows(dm_own)
    dm, dgu, part = feed_back(pieces, w_gu, w_d, gate_up)
    terms, far, _ = scatter_rows(part)
    down = down_grads(after(dm, part[0]), act)
    shares, rest, tail2 = feed_grads(place, down, h2, after(dgu, *far), w_gu)
    summed = over_sequences(shares)
    dresid, da_own = rows_after_feed_back(terms, resid, dout, info)
    pieces, near, far = gather_rows(da_own)
    seconds = share_blocks(after(summed, *near, *far))
    da, dqkv, part = attention_back(
        place, pieces, w_qkv, w_o, length, kpos, cosine, sine, q, keys, values, lse
    )
    terms, far, x_come = scatter_rows(part)
    shares = attention_grads(place, h1, after(dqkv, *far), da, ctx, w_qkv, rest, tail2, squares)
    summed = over_sequences(after(shares, seconds, x_come[2]))
    dx = rows_at_end(terms, own, dresid, info)
    firsts = share_blocks(after(summed, seconds, dx))
    grad_gate, grad_up = unpack_second(after(seconds, dx), hidden)
    both_out = move_y(out_own)
    both_dx = move_y(dx)
    output = jnp.stack([jnp.where(first, out_own, both_out), jnp.where(first, both_out, out_own)])
    input_grad = jnp.stack([jnp.where(first, dx, both_dx), jnp.where(first, both_dx, dx)]).astype(F32)
    grad_query, grad_key, grad_value, grad_out, grad_down, tails = unpack_first(firsts, seconds, hidden)
    return (
        output,
        tails[0, 2] / (count * width),
        input_grad,
        tails[:, 0] / norm_attn.astype(F32),
        tails[:, 1] / norm_mlp.astype(F32),
        grad_query,
        grad_key,
        grad_value,
        grad_out.T,
        grad_gate,
        grad_up,
        grad_down.T,
    )


def rms_forward(value_rows, gain):
    inverse = lax.rsqrt(jnp.mean(value_rows * value_rows, axis=-1, keepdims=True) + eps)
    normed = value_rows * inverse
    return (normed, inverse, normed * gain)


def rms_backward(grad, normed, inverse, gain):
    scaled = grad * gain
    return inverse * (scaled - normed * jnp.mean(scaled * normed, axis=-1, keepdims=True))


def rotate(value_rows, cosine, sine):
    half = value_rows.shape[-1] // 2
    first, second = (value_rows[..., :half], value_rows[..., half:])
    return jnp.concatenate(
        [first * cosine - second * sine, second * cosine + first * sine], axis=-1
    )


def rotate_back(grad, cosine, sine):
    half = grad.shape[-1] // 2
    first, second = (grad[..., :half], grad[..., half:])
    return jnp.concatenate(
        [first * cosine + second * sine, second * cosine - first * sine], axis=-1
    )


def allowed_pairs(key_ok, qpos, seq_len):
    kpos = jnp.arange(seq_len, dtype=jnp.int32)
    return (kpos[None, :] // BLOCK <= qpos[:, None] // BLOCK) & (key_ok[None, :] > 0)


def masked_scores(query_rows, key_rows, key_ok, qpos, scale):
    raw = (
        jnp.einsum("qkgd,jkd->kgqj", query_rows, key_rows, preferred_element_type=jnp.float32)
        * scale
    )
    allowed = allowed_pairs(key_ok, qpos, key_rows.shape[0])
    return jnp.where(allowed, raw, jnp.float32(-1e30))


def dot_left(left, right):
    return lax.dot_general(
        left, right, (((0,), (0,)), ((), ())), preferred_element_type=jnp.float32
    )


def dot_right(left, right):
    return lax.dot_general(
        left, right, (((1,), (1,)), ((), ())), preferred_element_type=jnp.float32
    )


def shards(
    inputs,
    valid,
    out_grad,
    teacher,
    norm_attn,
    w_query,
    key_matrix,
    value_matrix,
    w_out,
    norm_mlp,
    w_gate,
    w_up,
    w_down,
):
    seqs, seg, width = inputs.shape
    ctx_size = lax.axis_size("context")
    index = lax.axis_index("context")
    scale = HEAD_SIZE ** (-0.5)
    half = HEAD_SIZE // 2
    gathered = (
        lax.all_gather(norm_attn, "context", axis=0, tiled=True),
        lax.all_gather(w_query, "context", axis=0, tiled=True),
        lax.all_gather(key_matrix, "context", axis=0, tiled=True),
        lax.all_gather(value_matrix, "context", axis=0, tiled=True),
        lax.all_gather(w_out, "context", axis=1, tiled=True),
        lax.all_gather(norm_mlp, "context", axis=0, tiled=True),
        lax.all_gather(w_gate, "context", axis=0, tiled=True),
        lax.all_gather(w_up, "context", axis=0, tiled=True),
        lax.all_gather(w_down, "context", axis=1, tiled=True),
    )
    gain_first, wq, wk, wv, wo, gain_second, wg, wu, wd = gathered
    gain1 = gain_first.astype(jnp.float32)
    gain2 = gain_second.astype(jnp.float32)
    heads_q = wq.shape[1] // HEAD_SIZE
    heads_kv = wk.shape[1] // HEAD_SIZE
    head_group = heads_q // heads_kv
    row_count = seqs * seg
    positions = index * seg + jnp.arange(seg, dtype=jnp.int32)
    freqs = jnp.exp(-math.log(theta) * jnp.arange(half, dtype=jnp.float32) / half)
    angles = positions.astype(jnp.float32)[:, None] * freqs[None, :]
    cosine = jnp.cos(angles)[:, None, :]
    sine = jnp.sin(angles)[:, None, :]
    x = inputs.astype(jnp.float32)
    normed1, inverse1, pre1 = rms_forward(x, gain1)
    h1 = pre1.astype(jnp.bfloat16).reshape(row_count, width)
    query_before_rotary = jnp.dot(h1, wq, preferred_element_type=jnp.float32).reshape(
        seqs, seg, heads_q, HEAD_SIZE
    )
    key_before_rotary = jnp.dot(h1, wk, preferred_element_type=jnp.float32).reshape(
        seqs, seg, heads_kv, HEAD_SIZE
    )
    value_own = (
        jnp.dot(h1, wv, preferred_element_type=jnp.float32)
        .astype(jnp.bfloat16)
        .reshape(seqs, seg, heads_kv * HEAD_SIZE)
    )
    query_rows = (
        rotate(query_before_rotary, cosine, sine)
        .astype(jnp.bfloat16)
        .reshape(seqs, seg, heads_kv, head_group, HEAD_SIZE)
    )
    key_own = (
        rotate(key_before_rotary, cosine, sine)
        .astype(jnp.bfloat16)
        .reshape(seqs, seg, heads_kv * HEAD_SIZE)
    )
    keys_all, values_all, valid_all = (
        lax.all_gather(key_own, "context", axis=1, tiled=True),
        lax.all_gather(value_own, "context", axis=1, tiled=True),
        lax.all_gather(valid.astype(jnp.bfloat16), "context", axis=1, tiled=True),
    )
    seq_len = keys_all.shape[1]

    def attend(carry, items):
        qseq, kseq, vseq, okseq = items
        key_rows = kseq.reshape(seq_len, heads_kv, HEAD_SIZE)
        value_rows = vseq.reshape(seq_len, heads_kv, HEAD_SIZE)
        scores = masked_scores(qseq, key_rows, okseq, positions, scale)
        top = jnp.max(scores, axis=-1, keepdims=True)
        expo = jnp.exp(scores - top)
        total = jnp.sum(expo, axis=-1, keepdims=True)
        probr = (expo / total).astype(jnp.bfloat16)
        ctx = jnp.einsum("kgqj,jkd->qkgd", probr, value_rows, preferred_element_type=jnp.float32)
        lse = (top + jnp.log(total))[..., 0]
        return (carry, (ctx.astype(jnp.bfloat16).reshape(seg, heads_q * HEAD_SIZE), lse))

    carry, (context, lse_all) = lax.scan(
        attend, jnp.float32(0.0), (query_rows, keys_all, values_all, valid_all)
    )
    ctx_flat = context.reshape(row_count, heads_q * HEAD_SIZE)
    attn = lax.psum(
        jnp.dot(ctx_flat, wo, preferred_element_type=jnp.float32).astype(jnp.bfloat16), "tensor"
    ).astype(jnp.float32)
    resid = x + attn.reshape(seqs, seg, width)
    normed2, inverse2, pre2 = rms_forward(resid, gain2)
    h2 = pre2.astype(jnp.bfloat16).reshape(row_count, width)
    gate = jnp.dot(h2, wg, preferred_element_type=jnp.float32)
    up = jnp.dot(h2, wu, preferred_element_type=jnp.float32)
    sigma = jax.nn.sigmoid(gate)
    silu = gate * sigma
    act = (silu * up).astype(jnp.bfloat16)
    mixed = lax.psum(
        jnp.dot(act, wd, preferred_element_type=jnp.float32).astype(jnp.bfloat16), "tensor"
    ).astype(jnp.float32)
    out = resid + mixed.reshape(seqs, seg, width)
    output = out.astype(jnp.bfloat16)
    validf = valid.astype(jnp.float32)[..., None]
    diff = out - teacher.astype(jnp.float32)
    count, squares = lax.psum(
        (jnp.sum(valid.astype(jnp.float32)), jnp.sum(validf * diff * diff)), "context"
    )
    loss = squares / (count * width)
    dout = validf * (
        out_grad.astype(jnp.float32) + jnp.float32(seqs * seg * ctx_size) / count * diff
    )
    dm = dout.astype(jnp.bfloat16).reshape(row_count, width)
    grad_down = dot_left(act, dm)
    dact = dot_right(dm, wd)
    dgate = (dact * up * sigma * (1.0 + gate * (1.0 - sigma))).astype(jnp.bfloat16)
    dup = (dact * silu).astype(jnp.bfloat16)
    grad_gate = dot_left(h2, dgate)
    grad_up = dot_left(h2, dup)
    dh2 = (
        lax.psum((dot_right(dgate, wg) + dot_right(dup, wu)).astype(jnp.bfloat16), "tensor")
        .astype(jnp.float32)
        .reshape(seqs, seg, width)
    )
    grad_gain2 = jnp.sum(dh2 * normed2, axis=(0, 1))
    dresid = dout + rms_backward(dh2, normed2, inverse2, gain2)
    dattn = dresid.astype(jnp.bfloat16).reshape(row_count, width)
    grad_out = dot_left(ctx_flat, dattn)
    dctx = (
        dot_right(dattn, wo)
        .astype(jnp.bfloat16)
        .reshape(seqs, seg, heads_kv, head_group, HEAD_SIZE)
    )

    def attend_back(carry, items):
        qseq, kseq, vseq, okseq, lseq, dseq = items
        allowed = allowed_pairs(okseq, positions, seq_len)

        def head_back(parts):
            qhead, khead, vhead, dhead, lhead = parts
            raw = (
                jnp.einsum("qgd,jd->gqj", qhead, khead, preferred_element_type=jnp.float32) * scale
            )
            scores = jnp.where(allowed[None], raw, jnp.float32(-1e30))
            prob = jnp.exp(scores - lhead[..., None])
            probr = prob.astype(jnp.bfloat16)
            dprob = jnp.einsum("qgd,jd->gqj", dhead, vhead, preferred_element_type=jnp.float32)
            delta = jnp.sum(prob * dprob, axis=-1, keepdims=True)
            dscore = (prob * (dprob - delta)).astype(jnp.bfloat16)
            dq = (
                jnp.einsum("gqj,jd->qgd", dscore, khead, preferred_element_type=jnp.float32) * scale
            )
            dk = (
                jnp.einsum("gqj,qgd->jd", dscore, qhead, preferred_element_type=jnp.float32) * scale
            )
            dv = jnp.einsum("gqj,qgd->jd", probr, dhead, preferred_element_type=jnp.float32)
            return (dq, dk, dv)

        heads_in = (
            jnp.moveaxis(qseq, 1, 0),
            jnp.moveaxis(kseq.reshape(seq_len, heads_kv, HEAD_SIZE), 1, 0),
            jnp.moveaxis(vseq.reshape(seq_len, heads_kv, HEAD_SIZE), 1, 0),
            jnp.moveaxis(dseq, 1, 0),
            lseq,
        )
        dq_heads, dk_heads, dv_heads = lax.map(head_back, heads_in)
        dq = jnp.moveaxis(dq_heads, 0, 1)
        dk = jnp.moveaxis(dk_heads, 0, 1).reshape(seq_len, heads_kv * HEAD_SIZE)
        dv = jnp.moveaxis(dv_heads, 0, 1).reshape(seq_len, heads_kv * HEAD_SIZE)
        dk_own, dv_own = (
            lax.psum_scatter(dk, "context", scatter_dimension=0, tiled=True),
            lax.psum_scatter(dv, "context", scatter_dimension=0, tiled=True),
        )
        return (carry, (dq, dk_own, dv_own))

    carry, (dq_all, dk_all, dv_all) = lax.scan(
        attend_back, jnp.float32(0.0), (query_rows, keys_all, values_all, valid_all, lse_all, dctx)
    )
    dqpre = (
        rotate_back(dq_all.reshape(seqs, seg, heads_q, HEAD_SIZE), cosine, sine)
        .astype(jnp.bfloat16)
        .reshape(row_count, heads_q * HEAD_SIZE)
    )
    dkpre = (
        rotate_back(dk_all.reshape(seqs, seg, heads_kv, HEAD_SIZE), cosine, sine)
        .astype(jnp.bfloat16)
        .reshape(row_count, heads_kv * HEAD_SIZE)
    )
    dvr = dv_all.astype(jnp.bfloat16).reshape(row_count, heads_kv * HEAD_SIZE)
    grad_query = dot_left(h1, dqpre)
    grad_key = dot_left(h1, dkpre)
    grad_value = dot_left(h1, dvr)
    dh1 = (
        lax.psum(
            (dot_right(dqpre, wq) + dot_right(dkpre, wk) + dot_right(dvr, wv)).astype(jnp.bfloat16),
            "tensor",
        )
        .astype(jnp.float32)
        .reshape(seqs, seg, width)
    )
    grad_gain1 = jnp.sum(dh1 * normed1, axis=(0, 1))
    input_grad = dresid + rms_backward(dh1, normed1, inverse1, gain1)
    summed = (
        lax.psum_scatter(grad_gain1, "context", scatter_dimension=0, tiled=True),
        lax.psum_scatter(grad_query, "context", scatter_dimension=0, tiled=True),
        lax.psum_scatter(grad_key, "context", scatter_dimension=0, tiled=True),
        lax.psum_scatter(grad_value, "context", scatter_dimension=0, tiled=True),
        lax.psum_scatter(grad_out, "context", scatter_dimension=1, tiled=True),
        lax.psum_scatter(grad_gain2, "context", scatter_dimension=0, tiled=True),
        lax.psum_scatter(grad_gate, "context", scatter_dimension=0, tiled=True),
        lax.psum_scatter(grad_up, "context", scatter_dimension=0, tiled=True),
        lax.psum_scatter(grad_down, "context", scatter_dimension=1, tiled=True),
    )
    (
        grad_gain1,
        grad_query,
        grad_key,
        grad_value,
        grad_out,
        grad_gain2,
        grad_gate,
        grad_up,
        grad_down,
    ) = summed
    return (
        output,
        loss,
        input_grad,
        grad_gain1,
        grad_gain2,
        grad_query,
        grad_key,
        grad_value,
        grad_out,
        grad_gate,
        grad_up,
        grad_down,
    )


def solution(mesh):
    in_specs = (
        P(None, "context", None),
        P(None, "context"),
        P(None, "context", None),
        P(None, "context", None),
        P("context"),
        P("context", "tensor"),
        P("context", "tensor"),
        P("context", "tensor"),
        P("tensor", "context"),
        P("context"),
        P("context", "tensor"),
        P("context", "tensor"),
        P("tensor", "context"),
    )
    out_specs = (
        P(None, "context", None),
        P(),
        P(None, "context", None),
        P("context"),
        P("context"),
        P("context", "tensor"),
        P("context", "tensor"),
        P("context", "tensor"),
        P("tensor", "context"),
        P("context", "tensor"),
        P("context", "tensor"),
        P("tensor", "context"),
    )
    fits = dict(mesh.shape) == {"tensor": 2, "context": 16}
    return jax.shard_map(
        layer if fits else shards, mesh=mesh, in_specs=in_specs, out_specs=out_specs, check_vma=False
    )
```

```python
import functools
import functools
import math

import jax
import jax.numpy as jnp
from jax import lax
from jax.experimental import pallas as pl
from jax.experimental.pallas import tpu as pltpu
from jax.sharding import PartitionSpec as P

HEAD_SIZE = 80
BLOCK = 256
LANES = 128

eps = 1e-05
theta = 10000.0
BF = jnp.bfloat16
F32 = jnp.float32
MIB = 1024 * 1024
SLOW = ()


def whole(shape, dtype):
    return jax.ShapeDtypeStruct(tuple(shape), dtype)


def kernel_call(body, outs, ins, scalars=0, far=(), flops=0, scratch=(), limit=16, name=None):
    single = not isinstance(outs, (list, tuple))
    spec = lambda i: (
        pl.BlockSpec(memory_space=pltpu.SMEM)
        if i < scalars
        else pl.BlockSpec(memory_space=pl.ANY)
        if i in far
        else pl.BlockSpec(memory_space=pltpu.VMEM)
    )
    out_spec = pl.BlockSpec(memory_space=pltpu.VMEM)
    nbytes = sum(math.prod(a.shape) * a.dtype.itemsize for a in ins)
    nbytes += sum(math.prod(o.shape) * o.dtype.itemsize for o in ([outs] if single else outs))
    return pl.pallas_call(
        body,
        out_shape=outs,
        in_specs=[spec(i) for i in range(len(ins))],
        out_specs=out_spec if single else [out_spec] * len(outs),
        scratch_shapes=list(scratch),
        compiler_params=pltpu.CompilerParams(vmem_limit_bytes=limit * MIB),
        cost_estimate=pl.CostEstimate(flops=flops if name in SLOW else 0, bytes_accessed=0, transcendentals=0),
        name=name,
    )(*ins)


def dot_nn(a, b):
    return lax.dot_general(a, b, (((1,), (0,)), ((), ())), preferred_element_type=F32)


def dot_nt(a, b):
    return lax.dot_general(a, b, (((1,), (1,)), ((), ())), preferred_element_type=F32)


def dot_tn(a, b):
    return lax.dot_general(a, b, (((0,), (0,)), ((), ())), preferred_element_type=F32)


def move_c(a):
    return lax.ppermute(a, "context", [(k, k ^ 1) for k in range(16)])


def move_x(a):
    return lax.ppermute(a, "context", [(k, k ^ 2) for k in range(16)])


def move_z(a, step):
    return lax.ppermute(a, "context", [(k, (k + 4 * step) % 16) for k in range(16)])


def move_y(a):
    return lax.ppermute(a, "tensor", [(0, 1), (1, 0)])


def share_out(a):
    return lax.all_to_all(a, "context", split_axis=0, concat_axis=0, tiled=True)


def after(value, *others):
    return lax.optimization_barrier((value, *others))[0]


def stack(pieces):
    def body(*refs):
        for m in range(4):
            refs[4][m] = refs[m][...]

    return kernel_call(body, whole((4, *pieces[0].shape), BF), tuple(pieces), limit=8, name="stack")


def gather_rows(own, *late, early=(), mid=()):
    near = [own] + [move_z(own, m) for m in (1, 2, 3)]
    far = [move_x(own)]
    far += [move_x(after(near[1], far[0], *early)), None, move_x(after(near[3], far[0], *early))]
    far[2] = move_x(after(near[2], far[1], far[3], *mid))
    near_all, far_all = stack(near), stack(far)
    last = after(far_all, *late) if late else far_all
    return (near_all, move_c(near_all), far_all, move_c(last)), near, far


def scatter_rows(part, *late):
    far1, far0, near1, near0 = part
    shape = far1.shape[1:]

    def add_far(a_ref, b_ref, *outs):
        for m in range(4):
            outs[m][...] = (a_ref[m].astype(F32) + b_ref[m].astype(F32)).astype(BF)

    def add_near(m, a_ref, b_ref, c_ref, out_ref):
        out_ref[...] = (a_ref[m].astype(F32) + b_ref[m].astype(F32) + c_ref[...].astype(F32)).astype(BF)

    far = kernel_call(add_far, [whole(shape, BF)] * 4, (far0, move_c(far1)), limit=16, name="add_far")
    near1 = move_c(near1)
    come = {m: move_x(far[m]) for m in (2, 1, 3, 0)}
    if late:
        come[2] = after(come[2], *late)
    terms = [near0, near1, come[0]]
    for m in (2, 1, 3):
        body = functools.partial(add_near, m)
        s = kernel_call(body, whole(shape, BF), (near0, near1, come[m]), limit=8, name="add_near")
        terms.append(move_z(s, 4 - m))
    return terms, far, come


def part_shapes(seg, width):
    return [
        whole((4, seg, width), BF),
        whole((4, seg, width), BF),
        whole((4, seg, width), BF),
        whole((4, seg, width), BF),
    ]


def write_part(outs, group, value):
    far1, far0, near1, near0 = outs
    seg = far1.shape[1]
    to = (near0, near1, far0, far1)[group]
    for m in range(4):
        to[m] = value[m * seg : (m + 1) * seg].astype(BF)


def total(refs):
    out = refs[0][0].astype(F32) + refs[1][0].astype(F32)
    for r in refs[2:]:
        out = out + r[...].astype(F32)
    return out


FIRST = 384
SECOND = 640
EXTRA = 4


def pack_first(wq, wk, wv, wot, extra, wdt):
    rows, d = wq.shape[0], HEAD_SIZE
    hidden = wdt.shape[1] // 16
    some = FIRST - 4 * d - EXTRA

    def body(q_ref, k_ref, v_ref, o_ref, e_ref, d_ref, out_ref):
        for k in range(16):
            block = jnp.concatenate(
                [
                    q_ref[:, k * d : (k + 1) * d],
                    k_ref[:, k // 4 * d : (k // 4 + 1) * d],
                    v_ref[:, k // 4 * d : (k // 4 + 1) * d],
                    o_ref[:, k * d : (k + 1) * d],
                    e_ref[...],
                    d_ref[:, k * hidden : k * hidden + some],
                ],
                axis=1,
            )
            out_ref[k] = block

    return kernel_call(
        body, whole((16, rows, FIRST), BF), (wq, wk, wv, wot, extra, wdt), limit=16, name="pack_first"
    )


def pack_second(wg, wu, wdt):
    rows = wg.shape[0]
    hidden = wg.shape[1] // 16
    some = FIRST - 4 * HEAD_SIZE - EXTRA
    spare = SECOND - 3 * hidden + some

    def body(g_ref, u_ref, d_ref, out_ref):
        for k in range(16):
            block = jnp.concatenate(
                [
                    d_ref[:, k * hidden + some : (k + 1) * hidden],
                    g_ref[:, k * hidden : (k + 1) * hidden],
                    u_ref[:, k * hidden : (k + 1) * hidden],
                    jnp.zeros((rows, spare), BF),
                ],
                axis=1,
            )
            out_ref[k] = block

    return kernel_call(body, whole((16, rows, SECOND), BF), (wg, wu, wdt), limit=16, name="pack_second")


def share_blocks(a):
    return share_out(a.reshape(-1, a.shape[2])).reshape(a.shape)


def of_other(a):
    return lax.all_gather(a, "tensor", axis=0, tiled=False)


def over_sequences(parts):
    return lax.psum_scatter(parts, "tensor", scatter_dimension=0, tiled=False)


def unpack_second(second, hidden):
    rows = second.shape[1]
    left = 3 * hidden - SECOND

    def body(s_ref, g_ref, u_ref, d_ref):
        for k in range(16):
            b = s_ref[k]
            c = b[:, : 2 * hidden].astype(F32)
            g_ref[:, k * hidden : (k + 1) * hidden] = c[:, :hidden]
            u_ref[:, k * hidden : (k + 1) * hidden] = c[:, hidden : 2 * hidden]
            d_ref[:, k * hidden : (k + 1) * hidden] = jnp.concatenate(
                [b[:, 2 * hidden :], jnp.zeros((rows, left), BF)], axis=1
            )

    wide = (rows, 16 * hidden)
    return kernel_call(
        body, [whole(wide, F32), whole(wide, F32), whole(wide, BF)], (second,), limit=16, name="unpack_second"
    )


def unpack_first(first, down, hidden):
    rows, d = first.shape[1], HEAD_SIZE
    cut = SECOND - 2 * hidden
    rest = 4 * d + hidden - cut

    def body(f_ref, down_ref, q_ref, k_ref, v_ref, o_ref, d_ref, tail_ref):
        tail = jnp.zeros((rows, 3), F32)
        d_ref[...] = down_ref[...].astype(F32)
        for k in range(16):
            b = f_ref[k].astype(F32)
            q_ref[:, k * d : (k + 1) * d] = b[:, :d]
            o_ref[:, k * d : (k + 1) * d] = b[:, 3 * d : 4 * d]
            if k % 4 == 0:
                keys = jnp.zeros((rows, 2 * d), F32)
            keys = keys + b[:, d : 3 * d]
            if k % 4 == 3:
                k_ref[:, k // 4 * d : (k // 4 + 1) * d] = keys[:, :d]
                v_ref[:, k // 4 * d : (k // 4 + 1) * d] = keys[:, d:]
            tail = tail + b[:, rest : rest + 3]
            d_ref[:, k * hidden + cut : (k + 1) * hidden] = b[:, 4 * d : rest]
        tail_ref[...] = tail

    outs = [whole((rows, w), F32) for w in (16 * d, 4 * d, 4 * d, 16 * d, 16 * hidden, 3)]
    return kernel_call(body, outs, (first, down), limit=16, name="unpack_first")


def order_attention(mine_ref, other_ref, w_ref, out_ref, row_ref, info_ref):
    size, d = mine_ref.shape[1], HEAD_SIZE
    info_ref[...] = jnp.zeros_like(info_ref)
    for k in range(16):
        rs = slice(k * size, (k + 1) * size)
        parts = [mine_ref[k], other_ref[k]]
        w_ref[rs, :] = jnp.concatenate([p[:, : 3 * d] for p in parts], axis=1)
        out_ref[rs, :] = jnp.concatenate([p[:, 3 * d : 4 * d] for p in parts], axis=1)
        info_ref[rs, :EXTRA] = parts[0][:, 4 * d : 4 * d + EXTRA].astype(F32)
    for b in range(16 * size // LANES):
        rs = slice(b * LANES, (b + 1) * LANES)
        row_ref[:, rs] = info_ref[rs, :].T[0:8, :]


def order_feed(fm_ref, fo_ref, m_ref, o_ref, gu_ref, d_ref, hidden):
    size = m_ref.shape[1]
    at = 4 * HEAD_SIZE + EXTRA
    rest = hidden - (FIRST - at)
    for k in range(16):
        rs = slice(k * size, (k + 1) * size)
        fm, fo, m, o = fm_ref[k], fo_ref[k], m_ref[k], o_ref[k]
        gu_ref[rs, :] = jnp.concatenate(
            [
                m[:, rest : rest + hidden],
                o[:, rest : rest + hidden],
                m[:, rest + hidden : rest + 2 * hidden],
                o[:, rest + hidden : rest + 2 * hidden],
            ],
            axis=1,
        )
        d_ref[rs, :] = jnp.concatenate([fm[:, at:], m[:, :rest], fo[:, at:], o[:, :rest]], axis=1)


def turn(a, cosine, sine):
    half = HEAD_SIZE // 2
    lane = lax.broadcasted_iota(jnp.int32, a.shape, 1)
    swapped = jnp.where(lane < half, pltpu.roll(a, LANES - half, 1), pltpu.roll(a, half, 1))
    return a * cosine + swapped * sine


def head_of(value, at):
    part = value[:, at * HEAD_SIZE : (at + 1) * HEAD_SIZE]
    return jnp.concatenate([part, jnp.zeros((value.shape[0], LANES - HEAD_SIZE), value.dtype)], axis=1)


def attention(place, pieces, mine, both, kpos, cosine, sine):
    seg, width = pieces[0].shape[1:]
    rows = 16 * seg
    blocks = rows // BLOCK
    scale = HEAD_SIZE ** (-0.5)

    def body(place_ref, *refs):
        x_refs = refs[:4]
        mine_ref, both_ref, kpos_ref, cos_ref, sin_ref = refs[4:9]
        h_ref, q_ref, k_ref, v_ref, ctx_ref, lse_ref, w_ref, wo_ref, row_ref, *part = refs[9:22]
        other_ref, info_ref, sem = refs[22:]
        other = pltpu.make_async_copy(both_ref.at[1 - place_ref[3]], other_ref, sem)
        other.start()
        other.wait()
        order_attention(mine_ref, other_ref, w_ref, wo_ref, row_ref, info_ref)
        z = place_ref[0]
        gain = row_ref[0:1, :]
        counts = jnp.where(place_ref[3] == 0, row_ref[2:3, :], row_ref[3:4, :])
        length = jnp.sum(counts, axis=1, keepdims=True) / F32(width // 16)
        for g in range(4):

            @pl.loop(0, 4)
            def _(m):
                squares = jnp.zeros((seg, LANES), F32)
                for b in range(width // LANES):
                    tile = x_refs[g][m, :, b * LANES : (b + 1) * LANES].astype(F32)
                    squares = squares + tile * tile
                inv = lax.rsqrt(jnp.sum(squares, axis=1, keepdims=True) / F32(width) + eps)
                to = pl.ds(pl.multiple_of((g * 4 + m) * seg, seg), seg)
                for b in range(width // LANES):
                    at = slice(b * LANES, (b + 1) * LANES)
                    tile = x_refs[g][m, :, at].astype(F32)
                    h_ref[to, at] = (tile * inv * gain[:, at]).astype(BF)

        for g in range(4):
            qkv = dot_nn(h_ref[g * 4 * seg : (g + 1) * 4 * seg, :], w_ref[...])
            for m in range(4):
                to = pl.multiple_of(lax.rem(z - m + 4, 4) * BLOCK + g * seg, seg)
                to = pl.ds(to, seg)
                piece = qkv[m * seg : (m + 1) * seg]
                cosine, sine = cos_ref[to, :], sin_ref[to, :]
                for h in range(2):
                    q_ref[h, to, :] = turn(head_of(piece, 3 * h), cosine, sine).astype(BF)
                    k_ref[h, to, :] = turn(head_of(piece, 3 * h + 1), cosine, sine).astype(BF)
                    v_ref[h, to, :] = head_of(piece, 3 * h + 2).astype(BF)
        for i in range(blocks):
            m = lax.rem(z - i + 4, 4)
            n = (i + 1) * BLOCK
            ok = kpos_ref[:, :n].astype(F32) < length
            for h in range(2):
                s = dot_nt(q_ref[h, i * BLOCK : n, :], k_ref[h, :n, :]) * scale
                s = jnp.where(ok, s, F32(-1e30))
                top = jnp.max(s, axis=1, keepdims=True)
                e = jnp.exp(s - top)
                tot = jnp.sum(e, axis=1, keepdims=True)
                ctx = dot_nn((e * (1.0 / tot)).astype(BF), v_ref[h, :n, :]).astype(BF)
                for g in range(4):
                    to = pl.ds(pl.multiple_of((g * 4 + m) * seg, seg), seg)
                    ctx_ref[to, h * HEAD_SIZE : (h + 1) * HEAD_SIZE] = ctx[g * seg : (g + 1) * seg, :HEAD_SIZE]
                lse_ref[h, i * BLOCK : n, :] = top + jnp.log(tot)
        for g in (3, 2, 1, 0):
            write_part(part, g, dot_nt(ctx_ref[g * 4 * seg : (g + 1) * 4 * seg, :], wo_ref[...]))

    outs = [
        whole((rows, width), BF),
        whole((2, rows, LANES), BF),
        whole((2, rows, LANES), BF),
        whole((2, rows, LANES), BF),
        whole((rows, 2 * HEAD_SIZE), BF),
        whole((2, rows, 1), F32),
        whole((width, 6 * HEAD_SIZE), BF),
        whole((width, 2 * HEAD_SIZE), BF),
        whole((8, width), F32),
    ] + part_shapes(seg, width)
    flops = 2 * rows * width * 6 * LANES + 2 * rows * rows * LANES * 2 * 2
    out = kernel_call(
        body,
        outs,
        (place, *pieces, mine, both, kpos, cosine, sine),
        scalars=1,
        far=(6,),
        scratch=[pltpu.VMEM(mine.shape, BF), pltpu.VMEM((width, LANES), F32), pltpu.SemaphoreType.DMA],
        limit=24,
        flops=flops,
        name="attention",
    )
    return out[:9], out[9:]


def attention_back(place, pieces, weights, w_o, length, kpos, cosine, sine, q, k, v, lse):
    seg, width = pieces[0].shape[1:]
    rows = 16 * seg
    blocks = rows // BLOCK
    scale = HEAD_SIZE ** (-0.5)

    def body(place_ref, *refs):
        d_refs = [refs[i // 4].at[i % 4] for i in range(16)]
        w_ref, wo_ref, len_ref, kpos_ref, cos_ref, sin_ref, q_ref, k_ref, v_ref, lse_ref = refs[4:14]
        da_ref, dqkv_ref, *part = refs[14:20]
        dctx_ref, dk_ref, dv_ref = refs[20:]
        z = place_ref[0]
        length = len_ref[0:1, 0:1]
        for i in range(16):
            da_ref[i * seg : (i + 1) * seg, :] = d_refs[i][...]
        for g in range(4):
            dctx = dot_nn(da_ref[g * 4 * seg : (g + 1) * 4 * seg, :], wo_ref[...])
            for m in range(4):
                to = pl.multiple_of(lax.rem(z - m + 4, 4) * BLOCK + g * seg, seg)
                for h in range(2):
                    dctx_ref[h, pl.ds(to, seg), :] = head_of(dctx[m * seg : (m + 1) * seg], h).astype(BF)
        dk_ref[...] = jnp.zeros_like(dk_ref)
        dv_ref[...] = jnp.zeros_like(dv_ref)

        def put(i, at, value):
            m = lax.rem(z - i + 4, 4)
            for g in range(4):
                to = pl.ds(pl.multiple_of((g * 4 + m) * seg, seg), seg)
                dqkv_ref[to, at * HEAD_SIZE : (at + 1) * HEAD_SIZE] = value[g * seg : (g + 1) * seg, :HEAD_SIZE]

        for i in range(blocks):
            n = (i + 1) * BLOCK
            ok = kpos_ref[:, :n].astype(F32) < length
            cosine, sine = cos_ref[i * BLOCK : n, :], sin_ref[i * BLOCK : n, :]
            for h in range(2):
                qi = q_ref[h, i * BLOCK : n, :]
                di = dctx_ref[h, i * BLOCK : n, :]
                s = dot_nt(qi, k_ref[h, :n, :]) * scale
                p = jnp.where(ok, jnp.exp(s - lse_ref[h, i * BLOCK : n, :]), F32(0.0))
                dp = dot_nt(di, v_ref[h, :n, :])
                delta = jnp.sum(p * dp, axis=1, keepdims=True)
                ds = (p * (dp - delta)).astype(BF)
                dq = dot_nn(ds, k_ref[h, :n, :]) * scale
                put(i, 3 * h, turn(dq, cosine, -sine).astype(BF))
                dk_ref[h, :n, :] += dot_tn(ds, qi)
                dv_ref[h, :n, :] += dot_tn(p.astype(BF), di)
        for i in range(blocks):
            rs = slice(i * BLOCK, (i + 1) * BLOCK)
            for h in range(2):
                dk = turn(dk_ref[h, rs, :] * scale, cos_ref[rs, :], -sin_ref[rs, :])
                put(i, 3 * h + 1, dk.astype(BF))
                put(i, 3 * h + 2, dv_ref[h, rs, :].astype(BF))
        for g in (3, 2, 1, 0):
            write_part(part, g, dot_nt(dqkv_ref[g * 4 * seg : (g + 1) * 4 * seg, :], w_ref[...]))

    outs = [whole((rows, width), BF), whole((rows, 6 * HEAD_SIZE), BF)] + part_shapes(seg, width)
    flops = 2 * rows * width * 6 * LANES + 2 * rows * rows * LANES * 2 * 5
    out = kernel_call(
        body,
        outs,
        (place, *pieces, weights, w_o, length, kpos, cosine, sine, q, k, v, lse),
        scalars=1,
        flops=flops,
        scratch=[
            pltpu.VMEM((2, rows, LANES), BF),
            pltpu.VMEM((2, rows, LANES), F32),
            pltpu.VMEM((2, rows, LANES), F32),
        ],
        name="attention_back",
    )
    return out[0], out[1], out[2:]


def write_blocks(out_ref, index, chunk, value):
    rows = out_ref.shape[2]
    for k in range(4):
        out_ref[index, chunk * 4 + k] = value[k * rows : (k + 1) * rows].astype(BF)


def attention_grads(place, h1, dqkv, da, ctx, weights, rest, tail2, squares):
    rows, width = h1.shape
    d, cut = HEAD_SIZE, rest.shape[1] // 2
    spare = FIRST - 4 * d - cut - 3

    def body(place_ref, h_ref, dqkv_ref, da_ref, ctx_ref, w_ref, rest_ref, tail_ref, sq_ref, out_ref):
        y = place_ref[3]
        quarter = width // 4
        for b in range(4):
            at = slice(b * quarter, (b + 1) * quarter)
            g = dot_tn(h_ref[:, at], dqkv_ref[...])
            tail1 = jnp.sum(g * w_ref[at, :].astype(F32), axis=1, keepdims=True)
            o = dot_tn(da_ref[:, at], ctx_ref[...])
            sq = jnp.broadcast_to(sq_ref[0:1, 0:1], (quarter, 1))
            last = [tail1, tail_ref[at, :], sq, jnp.zeros((quarter, spare), F32)]
            for h, index in enumerate((y, 1 - y)):
                parts = [g[:, 3 * d * h : 3 * d * (h + 1)], o[:, d * h : d * (h + 1)]]
                parts += [rest_ref[at, cut * h : cut * (h + 1)].astype(F32)]
                write_blocks(out_ref, index, b, jnp.concatenate(parts + last, axis=1))

    return kernel_call(
        body,
        whole((2, 16, width // 16, FIRST), BF),
        (place, h1, dqkv, da, ctx, weights, rest, tail2, squares),
        scalars=1,
        flops=2 * rows * width * 8 * d,
        name="attention_grads",
    )


def feed(place, pieces, first_mine, first_both, mine, other, hidden):
    seg, width = pieces[0].shape[1:]
    rows = 16 * seg
    columns = 2 * hidden

    def body(place_ref, *refs):
        h_refs = [refs[i // 4].at[i % 4] for i in range(16)]
        fm_ref, fboth_ref, m_ref, o_ref, h_ref, gate_ref, act_ref, wg_ref, wd_ref, *part = refs[4:17]
        fo_ref, sem = refs[17:]
        first = pltpu.make_async_copy(fboth_ref.at[1 - place_ref[3]], fo_ref, sem)
        first.start()
        for i in range(16):
            h_ref[i * seg : (i + 1) * seg, :] = h_refs[i][...]
        first.wait()
        order_feed(fm_ref, fo_ref, m_ref, o_ref, wg_ref, wd_ref, hidden)
        for g in range(4):
            rs = slice(g * 4 * seg, (g + 1) * 4 * seg)
            gu = dot_nn(h_ref[rs, :], wg_ref[...])
            gate_ref[rs, :] = gu
            gate, up = gu[:, :columns], gu[:, columns:]
            act_ref[rs, :] = (gate * jax.nn.sigmoid(gate) * up).astype(BF)
        for g in (3, 2, 1, 0):
            rs = slice(g * 4 * seg, (g + 1) * 4 * seg)
            write_part(part, g, dot_nt(act_ref[rs, :], wd_ref[...]))

    outs = [whole((rows, width), BF), whole((rows, 2 * columns), F32), whole((rows, columns), BF)]
    outs += [whole((width, 2 * columns), BF), whole((width, columns), BF)]
    out = kernel_call(
        body,
        outs + part_shapes(seg, width),
        (place, *pieces, first_mine, first_both, mine, other),
        scalars=1,
        far=(6,),
        scratch=[pltpu.VMEM(first_mine.shape, BF), pltpu.SemaphoreType.DMA],
        limit=26,
        name="feed",
    )
    return out[:5], out[5:]


def feed_back(pieces, w_gu, w_d, gate_up):
    seg, width = pieces[0].shape[1:]
    rows = 16 * seg
    hidden = w_d.shape[1]

    def body(*refs):
        d_refs = [refs[i // 4].at[i % 4] for i in range(16)]
        wg_ref, wd_ref, gate_ref, dm_ref, dgu_ref, *part = refs[4:]
        for i in range(16):
            dm_ref[i * seg : (i + 1) * seg, :] = d_refs[i][...]
        for g in (3, 2, 1, 0):
            rs = slice(g * 4 * seg, (g + 1) * 4 * seg)
            dact = dot_nn(dm_ref[rs, :], wd_ref[...])
            gate, up = gate_ref[rs, :hidden], gate_ref[rs, hidden:]
            sigma = jax.nn.sigmoid(gate)
            dgate = dact * up * sigma * (1.0 + gate * (1.0 - sigma))
            dgu_ref[rs, :] = jnp.concatenate([dgate, dact * (gate * sigma)], axis=1).astype(BF)
        for g in (3, 2, 1, 0):
            rs = slice(g * 4 * seg, (g + 1) * 4 * seg)
            write_part(part, g, dot_nt(dgu_ref[rs, :], wg_ref[...]))

    outs = [whole((rows, width), BF), whole((rows, 2 * hidden), BF)]
    out = kernel_call(
        body,
        outs + part_shapes(seg, width),
        (*pieces, w_gu, w_d, gate_up),
        flops=2 * rows * width * hidden * 3,
        limit=16,
        name="feed_back",
    )
    return out[0], out[1], out[2:]


def down_grads(dm, act):
    rows, width = dm.shape
    hidden = act.shape[1]

    def body(dm_ref, act_ref, out_ref):
        quarter = width // 4
        for b in range(4):
            at = slice(b * quarter, (b + 1) * quarter)
            out_ref[at, :] = dot_tn(dm_ref[:, at], act_ref[...]).astype(BF)

    return kernel_call(
        body, whole((width, hidden), BF), (dm, act), flops=2 * rows * width * hidden, limit=16, name="down_grads"
    )


def feed_grads(place, down, h2, dgu, w_gu):
    rows, width = h2.shape
    hidden = down.shape[1] // 2
    cut = SECOND - 2 * hidden
    left = hidden - cut

    def body(place_ref, down_ref, h_ref, dgu_ref, w_ref, out_ref, rest_ref, tail_ref):
        y = place_ref[3]
        quarter = width // 4
        for b in range(4):
            at = slice(b * quarter, (b + 1) * quarter)
            g = dot_tn(h_ref[:, at], dgu_ref[...])
            tail_ref[at, :] = jnp.sum(g * w_ref[at, :].astype(F32), axis=1, keepdims=True)
            down = down_ref[at, :].astype(F32)
            rest_ref[at, :] = jnp.concatenate([down[:, cut:hidden], down[:, hidden + cut :]], axis=1).astype(BF)
            for h, index in enumerate((y, 1 - y)):
                parts = [
                    g[:, hidden * h : hidden * (h + 1)],
                    g[:, hidden * (2 + h) : hidden * (3 + h)],
                    down[:, hidden * h : hidden * h + cut],
                ]
                write_blocks(out_ref, index, b, jnp.concatenate(parts, axis=1))

    outs = [whole((2, 16, width // 16, SECOND), BF)] + [whole((width, 2 * left), BF), whole((width, 1), F32)]
    return kernel_call(
        body,
        outs,
        (place, down, h2, dgu, w_gu),
        scalars=1,
        flops=2 * rows * width * hidden * 4,
        limit=16,
        name="feed_grads",
    )


def norm_back(grad, rows, inverse, gain):
    normed = rows * inverse
    scaled = grad * gain
    return inverse * (scaled - normed * jnp.mean(scaled * normed, axis=-1, keepdims=True))


def rms_of(rows):
    return lax.rsqrt(jnp.mean(rows * rows, axis=-1, keepdims=True) + eps)


def rows_after_attention(terms, own, info):
    def body(*refs):
        *term_refs, own_ref, info_ref, resid_ref, h_ref = refs
        resid = own_ref[...].astype(F32) + total(term_refs)
        resid_ref[...] = resid
        h_ref[...] = (resid * rms_of(resid) * info_ref[1:2, :]).astype(BF)

    return kernel_call(
        body, [whole(own.shape, F32), whole(own.shape, BF)], (*terms, own, info), limit=16, name="after_attention"
    )


def rows_after_feed(terms, resid, valid, teacher, out_grad, factor):
    def body(*refs):
        *term_refs, resid_ref, ok_ref, teacher_ref, grad_ref, factor_ref = refs[:-4]
        out_ref, dout_ref, dm_ref, squares_ref = refs[-4:]
        out = resid_ref[...] + total(term_refs)
        out_ref[...] = out.astype(BF)
        ok = ok_ref[...]
        diff = out - teacher_ref[...].astype(F32)
        part = jnp.sum(ok * diff * diff, axis=0, keepdims=True)
        squares_ref[...] = jnp.broadcast_to(jnp.sum(part, axis=1, keepdims=True), squares_ref.shape)
        dout = ok * (grad_ref[...].astype(F32) + factor_ref[0:1, 0:1] * diff)
        dout_ref[...] = dout
        dm_ref[...] = dout.astype(BF)

    shape = resid.shape
    return kernel_call(
        body,
        [whole(shape, BF), whole(shape, F32), whole(shape, BF), whole((8, LANES), F32)],
        (*terms, resid, valid, teacher, out_grad, factor),
        limit=16,
        name="after_feed",
    )


def rows_after_feed_back(terms, resid, dout, info):
    def body(*refs):
        *term_refs, resid_ref, dout_ref, info_ref, dresid_ref, da_ref = refs
        resid = resid_ref[...]
        dresid = dout_ref[...] + norm_back(total(term_refs), resid, rms_of(resid), info_ref[1:2, :])
        dresid_ref[...] = dresid
        da_ref[...] = dresid.astype(BF)

    return kernel_call(
        body,
        [whole(resid.shape, F32), whole(resid.shape, BF)],
        (*terms, resid, dout, info),
        flops=10**11,
        limit=16,
        name="after_feed_back",
    )


def rows_at_end(terms, own, dresid, info):
    def body(*refs):
        *term_refs, own_ref, dresid_ref, info_ref, dx_ref = refs
        rows = own_ref[...].astype(F32)
        dx = dresid_ref[...] + norm_back(total(term_refs), rows, rms_of(rows), info_ref[0:1, :])
        dx_ref[...] = dx.astype(BF)

    return kernel_call(body, whole(own.shape, BF), (*terms, own, dresid, info), limit=16, name="at_end")


def layer(
    inputs,
    valid,
    out_grad,
    teacher,
    norm_attn,
    w_query,
    key_matrix,
    value_matrix,
    w_out,
    norm_mlp,
    w_gate,
    w_up,
    w_down,
):
    seqs, seg, width = inputs.shape
    y = lax.axis_index("tensor")
    k = lax.axis_index("context")
    z, x, c = k // 4, (k // 2) % 2, k % 2
    place = jnp.stack([z, x, c, y]).astype(jnp.int32)
    seq_len = 16 * seg
    first = y == 0

    def mine(a):
        return lax.dynamic_index_in_dim(a, y, 0, keepdims=False)

    own = mine(inputs)
    counts = jnp.sum(valid.astype(F32), axis=1).astype(BF)
    ones = jnp.ones_like(norm_attn)
    extra = jnp.stack([norm_attn, norm_mlp, ones * counts[0], ones * counts[1]], axis=1)
    hidden = w_gate.shape[1] // 16
    bit = jnp.arange(2, dtype=jnp.int32)
    pos = (
        jnp.arange(4, dtype=jnp.int32)[:, None, None, None] * (4 * seg)
        + (bit ^ x)[None, :, None, None] * (2 * seg)
        + (bit ^ c)[None, None, :, None] * seg
        + jnp.arange(seg, dtype=jnp.int32)[None, None, None, :]
    ).reshape(seq_len)
    half = HEAD_SIZE // 2
    freqs = jnp.exp(-math.log(theta) * jnp.arange(half, dtype=F32) / half)
    angles = pos.astype(F32)[:, None] * freqs[None, :]
    cos_half, sin_half = jnp.cos(angles), jnp.sin(angles)
    pad = jnp.zeros((seq_len, LANES - HEAD_SIZE), F32)
    cosine = jnp.concatenate([cos_half, cos_half, pad], axis=1)
    sine = jnp.concatenate([-sin_half, sin_half, pad], axis=1)
    kpos = pos[None, :]

    firsts = pack_first(w_query, key_matrix, value_matrix, w_out.T, extra, w_down.T)
    seconds = pack_second(after(w_gate, cosine, sine), w_up, w_down.T)
    first_in = share_blocks(firsts)
    first_both = of_other(first_in)
    pieces, near, far = gather_rows(after(own, first_in), first_both)
    second_in = share_blocks(after(seconds, *near, *far))
    (h1, q, keys, values, ctx, lse, w_qkv, w_o, info), part = attention(
        place, pieces, first_in, first_both, kpos, cosine, sine
    )
    lengths = jnp.sum(info[2:4], axis=1) / F32(width // 16)
    count = lengths[0] + lengths[1]
    length = jnp.full((8, LANES), jnp.where(first, lengths[0], lengths[1]), F32)
    factor = jnp.full((8, LANES), F32(seqs * seq_len) / count, F32)
    terms, far, come = scatter_rows(part)
    second_other = move_y(after(second_in, come[2]))
    resid, h2_own = rows_after_attention(terms, own, info)
    pieces, _, _ = gather_rows(h2_own, mid=(second_other,))
    (h2, gate_up, act, w_gu, w_d), part = feed(
        place, pieces, first_in, first_both, second_in, second_other, hidden
    )
    okf = mine(valid).astype(F32)[:, None]
    terms, _, _ = scatter_rows(part)
    out_own, dout, dm_own, squares = rows_after_feed(
        terms, resid, okf, mine(teacher), mine(out_grad), factor
    )
    pieces, _, _ = gather_rows(dm_own)
    dm, dgu, part = feed_back(pieces, w_gu, w_d, gate_up)
    terms, far, _ = scatter_rows(part)
    down = down_grads(after(dm, part[0]), act)
    shares, rest, tail2 = feed_grads(place, down, h2, after(dgu, *far), w_gu)
    summed = over_sequences(shares)
    dresid, da_own = rows_after_feed_back(terms, resid, dout, info)
    pieces, near, far = gather_rows(da_own)
    seconds = share_blocks(after(summed, *near, *far))
    da, dqkv, part = attention_back(
        place, pieces, w_qkv, w_o, length, kpos, cosine, sine, q, keys, values, lse
    )
    terms, far, x_come = scatter_rows(part)
    shares = attention_grads(place, h1, after(dqkv, *far), da, ctx, w_qkv, rest, tail2, squares)
    summed = over_sequences(after(shares, seconds, x_come[2]))
    dx = rows_at_end(terms, own, dresid, info)
    firsts = share_blocks(after(summed, seconds, dx))
    grad_gate, grad_up, down = unpack_second(after(seconds, dx), hidden)
    both_out = move_y(out_own)
    both_dx = move_y(dx)
    output = jnp.stack([jnp.where(first, out_own, both_out), jnp.where(first, both_out, out_own)])
    input_grad = jnp.stack([jnp.where(first, dx, both_dx), jnp.where(first, both_dx, dx)]).astype(F32)
    grad_query, grad_key, grad_value, grad_out, grad_down, tails = unpack_first(firsts, down, hidden)
    return (
        output,
        tails[0, 2] / (count * width),
        input_grad,
        tails[:, 0] / norm_attn.astype(F32),
        tails[:, 1] / norm_mlp.astype(F32),
        grad_query,
        grad_key,
        grad_value,
        grad_out.T,
        grad_gate,
        grad_up,
        grad_down.T,
    )


def rms_forward(value_rows, gain):
    inverse = lax.rsqrt(jnp.mean(value_rows * value_rows, axis=-1, keepdims=True) + eps)
    normed = value_rows * inverse
    return (normed, inverse, normed * gain)


def rms_backward(grad, normed, inverse, gain):
    scaled = grad * gain
    return inverse * (scaled - normed * jnp.mean(scaled * normed, axis=-1, keepdims=True))


def rotate(value_rows, cosine, sine):
    half = value_rows.shape[-1] // 2
    first, second = (value_rows[..., :half], value_rows[..., half:])
    return jnp.concatenate(
        [first * cosine - second * sine, second * cosine + first * sine], axis=-1
    )


def rotate_back(grad, cosine, sine):
    half = grad.shape[-1] // 2
    first, second = (grad[..., :half], grad[..., half:])
    return jnp.concatenate(
        [first * cosine + second * sine, second * cosine - first * sine], axis=-1
    )


def allowed_pairs(key_ok, qpos, seq_len):
    kpos = jnp.arange(seq_len, dtype=jnp.int32)
    return (kpos[None, :] // BLOCK <= qpos[:, None] // BLOCK) & (key_ok[None, :] > 0)


def masked_scores(query_rows, key_rows, key_ok, qpos, scale):
    raw = (
        jnp.einsum("qkgd,jkd->kgqj", query_rows, key_rows, preferred_element_type=jnp.float32)
        * scale
    )
    allowed = allowed_pairs(key_ok, qpos, key_rows.shape[0])
    return jnp.where(allowed, raw, jnp.float32(-1e30))


def dot_left(left, right):
    return lax.dot_general(
        left, right, (((0,), (0,)), ((), ())), preferred_element_type=jnp.float32
    )


def dot_right(left, right):
    return lax.dot_general(
        left, right, (((1,), (1,)), ((), ())), preferred_element_type=jnp.float32
    )


def shards(
    inputs,
    valid,
    out_grad,
    teacher,
    norm_attn,
    w_query,
    key_matrix,
    value_matrix,
    w_out,
    norm_mlp,
    w_gate,
    w_up,
    w_down,
):
    seqs, seg, width = inputs.shape
    ctx_size = lax.axis_size("context")
    index = lax.axis_index("context")
    scale = HEAD_SIZE ** (-0.5)
    half = HEAD_SIZE // 2
    gathered = (
        lax.all_gather(norm_attn, "context", axis=0, tiled=True),
        lax.all_gather(w_query, "context", axis=0, tiled=True),
        lax.all_gather(key_matrix, "context", axis=0, tiled=True),
        lax.all_gather(value_matrix, "context", axis=0, tiled=True),
        lax.all_gather(w_out, "context", axis=1, tiled=True),
        lax.all_gather(norm_mlp, "context", axis=0, tiled=True),
        lax.all_gather(w_gate, "context", axis=0, tiled=True),
        lax.all_gather(w_up, "context", axis=0, tiled=True),
        lax.all_gather(w_down, "context", axis=1, tiled=True),
    )
    gain_first, wq, wk, wv, wo, gain_second, wg, wu, wd = gathered
    gain1 = gain_first.astype(jnp.float32)
    gain2 = gain_second.astype(jnp.float32)
    heads_q = wq.shape[1] // HEAD_SIZE
    heads_kv = wk.shape[1] // HEAD_SIZE
    head_group = heads_q // heads_kv
    row_count = seqs * seg
    positions = index * seg + jnp.arange(seg, dtype=jnp.int32)
    freqs = jnp.exp(-math.log(theta) * jnp.arange(half, dtype=jnp.float32) / half)
    angles = positions.astype(jnp.float32)[:, None] * freqs[None, :]
    cosine = jnp.cos(angles)[:, None, :]
    sine = jnp.sin(angles)[:, None, :]
    x = inputs.astype(jnp.float32)
    normed1, inverse1, pre1 = rms_forward(x, gain1)
    h1 = pre1.astype(jnp.bfloat16).reshape(row_count, width)
    query_before_rotary = jnp.dot(h1, wq, preferred_element_type=jnp.float32).reshape(
        seqs, seg, heads_q, HEAD_SIZE
    )
    key_before_rotary = jnp.dot(h1, wk, preferred_element_type=jnp.float32).reshape(
        seqs, seg, heads_kv, HEAD_SIZE
    )
    value_own = (
        jnp.dot(h1, wv, preferred_element_type=jnp.float32)
        .astype(jnp.bfloat16)
        .reshape(seqs, seg, heads_kv * HEAD_SIZE)
    )
    query_rows = (
        rotate(query_before_rotary, cosine, sine)
        .astype(jnp.bfloat16)
        .reshape(seqs, seg, heads_kv, head_group, HEAD_SIZE)
    )
    key_own = (
        rotate(key_before_rotary, cosine, sine)
        .astype(jnp.bfloat16)
        .reshape(seqs, seg, heads_kv * HEAD_SIZE)
    )
    keys_all, values_all, valid_all = (
        lax.all_gather(key_own, "context", axis=1, tiled=True),
        lax.all_gather(value_own, "context", axis=1, tiled=True),
        lax.all_gather(valid.astype(jnp.bfloat16), "context", axis=1, tiled=True),
    )
    seq_len = keys_all.shape[1]

    def attend(carry, items):
        qseq, kseq, vseq, okseq = items
        key_rows = kseq.reshape(seq_len, heads_kv, HEAD_SIZE)
        value_rows = vseq.reshape(seq_len, heads_kv, HEAD_SIZE)
        scores = masked_scores(qseq, key_rows, okseq, positions, scale)
        top = jnp.max(scores, axis=-1, keepdims=True)
        expo = jnp.exp(scores - top)
        total = jnp.sum(expo, axis=-1, keepdims=True)
        probr = (expo / total).astype(jnp.bfloat16)
        ctx = jnp.einsum("kgqj,jkd->qkgd", probr, value_rows, preferred_element_type=jnp.float32)
        lse = (top + jnp.log(total))[..., 0]
        return (carry, (ctx.astype(jnp.bfloat16).reshape(seg, heads_q * HEAD_SIZE), lse))

    carry, (context, lse_all) = lax.scan(
        attend, jnp.float32(0.0), (query_rows, keys_all, values_all, valid_all)
    )
    ctx_flat = context.reshape(row_count, heads_q * HEAD_SIZE)
    attn = lax.psum(
        jnp.dot(ctx_flat, wo, preferred_element_type=jnp.float32).astype(jnp.bfloat16), "tensor"
    ).astype(jnp.float32)
    resid = x + attn.reshape(seqs, seg, width)
    normed2, inverse2, pre2 = rms_forward(resid, gain2)
    h2 = pre2.astype(jnp.bfloat16).reshape(row_count, width)
    gate = jnp.dot(h2, wg, preferred_element_type=jnp.float32)
    up = jnp.dot(h2, wu, preferred_element_type=jnp.float32)
    sigma = jax.nn.sigmoid(gate)
    silu = gate * sigma
    act = (silu * up).astype(jnp.bfloat16)
    mixed = lax.psum(
        jnp.dot(act, wd, preferred_element_type=jnp.float32).astype(jnp.bfloat16), "tensor"
    ).astype(jnp.float32)
    out = resid + mixed.reshape(seqs, seg, width)
    output = out.astype(jnp.bfloat16)
    validf = valid.astype(jnp.float32)[..., None]
    diff = out - teacher.astype(jnp.float32)
    count, squares = lax.psum(
        (jnp.sum(valid.astype(jnp.float32)), jnp.sum(validf * diff * diff)), "context"
    )
    loss = squares / (count * width)
    dout = validf * (
        out_grad.astype(jnp.float32) + jnp.float32(seqs * seg * ctx_size) / count * diff
    )
    dm = dout.astype(jnp.bfloat16).reshape(row_count, width)
    grad_down = dot_left(act, dm)
    dact = dot_right(dm, wd)
    dgate = (dact * up * sigma * (1.0 + gate * (1.0 - sigma))).astype(jnp.bfloat16)
    dup = (dact * silu).astype(jnp.bfloat16)
    grad_gate = dot_left(h2, dgate)
    grad_up = dot_left(h2, dup)
    dh2 = (
        lax.psum((dot_right(dgate, wg) + dot_right(dup, wu)).astype(jnp.bfloat16), "tensor")
        .astype(jnp.float32)
        .reshape(seqs, seg, width)
    )
    grad_gain2 = jnp.sum(dh2 * normed2, axis=(0, 1))
    dresid = dout + rms_backward(dh2, normed2, inverse2, gain2)
    dattn = dresid.astype(jnp.bfloat16).reshape(row_count, width)
    grad_out = dot_left(ctx_flat, dattn)
    dctx = (
        dot_right(dattn, wo)
        .astype(jnp.bfloat16)
        .reshape(seqs, seg, heads_kv, head_group, HEAD_SIZE)
    )

    def attend_back(carry, items):
        qseq, kseq, vseq, okseq, lseq, dseq = items
        allowed = allowed_pairs(okseq, positions, seq_len)

        def head_back(parts):
            qhead, khead, vhead, dhead, lhead = parts
            raw = (
                jnp.einsum("qgd,jd->gqj", qhead, khead, preferred_element_type=jnp.float32) * scale
            )
            scores = jnp.where(allowed[None], raw, jnp.float32(-1e30))
            prob = jnp.exp(scores - lhead[..., None])
            probr = prob.astype(jnp.bfloat16)
            dprob = jnp.einsum("qgd,jd->gqj", dhead, vhead, preferred_element_type=jnp.float32)
            delta = jnp.sum(prob * dprob, axis=-1, keepdims=True)
            dscore = (prob * (dprob - delta)).astype(jnp.bfloat16)
            dq = (
                jnp.einsum("gqj,jd->qgd", dscore, khead, preferred_element_type=jnp.float32) * scale
            )
            dk = (
                jnp.einsum("gqj,qgd->jd", dscore, qhead, preferred_element_type=jnp.float32) * scale
            )
            dv = jnp.einsum("gqj,qgd->jd", probr, dhead, preferred_element_type=jnp.float32)
            return (dq, dk, dv)

        heads_in = (
            jnp.moveaxis(qseq, 1, 0),
            jnp.moveaxis(kseq.reshape(seq_len, heads_kv, HEAD_SIZE), 1, 0),
            jnp.moveaxis(vseq.reshape(seq_len, heads_kv, HEAD_SIZE), 1, 0),
            jnp.moveaxis(dseq, 1, 0),
            lseq,
        )
        dq_heads, dk_heads, dv_heads = lax.map(head_back, heads_in)
        dq = jnp.moveaxis(dq_heads, 0, 1)
        dk = jnp.moveaxis(dk_heads, 0, 1).reshape(seq_len, heads_kv * HEAD_SIZE)
        dv = jnp.moveaxis(dv_heads, 0, 1).reshape(seq_len, heads_kv * HEAD_SIZE)
        dk_own, dv_own = (
            lax.psum_scatter(dk, "context", scatter_dimension=0, tiled=True),
            lax.psum_scatter(dv, "context", scatter_dimension=0, tiled=True),
        )
        return (carry, (dq, dk_own, dv_own))

    carry, (dq_all, dk_all, dv_all) = lax.scan(
        attend_back, jnp.float32(0.0), (query_rows, keys_all, values_all, valid_all, lse_all, dctx)
    )
    dqpre = (
        rotate_back(dq_all.reshape(seqs, seg, heads_q, HEAD_SIZE), cosine, sine)
        .astype(jnp.bfloat16)
        .reshape(row_count, heads_q * HEAD_SIZE)
    )
    dkpre = (
        rotate_back(dk_all.reshape(seqs, seg, heads_kv, HEAD_SIZE), cosine, sine)
        .astype(jnp.bfloat16)
        .reshape(row_count, heads_kv * HEAD_SIZE)
    )
    dvr = dv_all.astype(jnp.bfloat16).reshape(row_count, heads_kv * HEAD_SIZE)
    grad_query = dot_left(h1, dqpre)
    grad_key = dot_left(h1, dkpre)
    grad_value = dot_left(h1, dvr)
    dh1 = (
        lax.psum(
            (dot_right(dqpre, wq) + dot_right(dkpre, wk) + dot_right(dvr, wv)).astype(jnp.bfloat16),
            "tensor",
        )
        .astype(jnp.float32)
        .reshape(seqs, seg, width)
    )
    grad_gain1 = jnp.sum(dh1 * normed1, axis=(0, 1))
    input_grad = dresid + rms_backward(dh1, normed1, inverse1, gain1)
    summed = (
        lax.psum_scatter(grad_gain1, "context", scatter_dimension=0, tiled=True),
        lax.psum_scatter(grad_query, "context", scatter_dimension=0, tiled=True),
        lax.psum_scatter(grad_key, "context", scatter_dimension=0, tiled=True),
        lax.psum_scatter(grad_value, "context", scatter_dimension=0, tiled=True),
        lax.psum_scatter(grad_out, "context", scatter_dimension=1, tiled=True),
        lax.psum_scatter(grad_gain2, "context", scatter_dimension=0, tiled=True),
        lax.psum_scatter(grad_gate, "context", scatter_dimension=0, tiled=True),
        lax.psum_scatter(grad_up, "context", scatter_dimension=0, tiled=True),
        lax.psum_scatter(grad_down, "context", scatter_dimension=1, tiled=True),
    )
    (
        grad_gain1,
        grad_query,
        grad_key,
        grad_value,
        grad_out,
        grad_gain2,
        grad_gate,
        grad_up,
        grad_down,
    ) = summed
    return (
        output,
        loss,
        input_grad,
        grad_gain1,
        grad_gain2,
        grad_query,
        grad_key,
        grad_value,
        grad_out,
        grad_gate,
        grad_up,
        grad_down,
    )


def solution(mesh):
    in_specs = (
        P(None, "context", None),
        P(None, "context"),
        P(None, "context", None),
        P(None, "context", None),
        P("context"),
        P("context", "tensor"),
        P("context", "tensor"),
        P("context", "tensor"),
        P("tensor", "context"),
        P("context"),
        P("context", "tensor"),
        P("context", "tensor"),
        P("tensor", "context"),
    )
    out_specs = (
        P(None, "context", None),
        P(),
        P(None, "context", None),
        P("context"),
        P("context"),
        P("context", "tensor"),
        P("context", "tensor"),
        P("context", "tensor"),
        P("tensor", "context"),
        P("context", "tensor"),
        P("context", "tensor"),
        P("tensor", "context"),
    )
    fits = dict(mesh.shape) == {"tensor": 2, "context": 16}
    return jax.shard_map(
        layer if fits else shards, mesh=mesh, in_specs=in_specs, out_specs=out_specs, check_vma=False
    )
```
